512 devices in a mesh: seq: 64 (over z, x_hi, core), row: 8 (over y, x_lo).
Axes of the slice: x: 4 (x_hi: 2, x_lo: 2; x = x_hi * 2 + x_lo), y: 4, z: 16, core: 2. Of those that a mesh axis runs over, the one named last changes fastest.
Arguments:
- patch_queries: bfloat16 [8192, 2048], P('seq', 'row'), may hold values from -15 to 15
- patch_keys: bfloat16 [8192, 2048], P('seq', 'row'), may hold values from -15 to 15
- patch_values: bfloat16 [8192, 2048], P('seq', 'row'), may hold values from -6 to 6
- patch_tasks: int32 [8192], P('seq'), may hold values from 0 to 7
- residual: bfloat16 [8192, 2048], P('seq', 'row'), may hold values from -6 to 6
- output_weight: bfloat16 [2048, 2048], P('row'), may hold values from -0.5 to 0.5
- global_down: bfloat16 [2048, 16], P('row'), may hold values from -0.5 to 0.5
- global_up: bfloat16 [16, 2048], P(None, 'row'), may hold values from -1.5 to 1.5
- global_scales: float32 [8, 16], replicated, may hold values from 0.25 to 4
- local_weight: bfloat16 [2048, 512], P('row'), may hold values from -0.125 to 0.125
- byte_ids: int32 [65536], P('seq'), may hold values from 0 to 255
- byte_table: bfloat16 [256, 512], replicated, may hold values from -6 to 6
- position_table: bfloat16 [8, 512], replicated, may hold values from -6 to 6
- norm_gain: float32 [512], replicated, may hold values from 0.5 to 1.5
- hidden_in: bfloat16 [2048, 512], P('row', 'seq'), may hold values from -0.25 to 0.25
- hidden_out: bfloat16 [2048, 512], P('row', 'seq'), may hold values from -0.125 to 0.125
- local_down: bfloat16 [512, 16], replicated, may hold values from -0.25 to 0.25
- local_up: bfloat16 [16, 2048], P(None, 'row'), may hold values from -1.5 to 1.5
- local_scales: float32 [8, 16], replicated, may hold values from 0.25 to 4
- cotangent: bfloat16 [65536, 512], P(('seq', 'row')), may hold values from -6 to 6
Outputs:
- grad_global_down: float32 [2048, 16], P('row')
- grad_global_up: float32 [16, 2048], P(None, 'row')
- grad_global_scales: float32 [8, 16], replicated
- grad_local_down: float32 [512, 16], replicated
- grad_local_up: float32 [16, 2048], P(None, 'row')
- grad_local_scales: float32 [8, 16], replicated
The draws below stay inside these ranges and needn't reach their ends.
All inputs are finite; a program needn't handle non-finite values.
Results may differ from the reference program's by a relative error of at most 0.028.
Values may be sent and summed in bfloat16 or wider, within the bound.
No kernel may reach another device: no remote copies, remote signals or barrier semaphores. Data moves between devices by JAX's collectives and lax.ppermute only.
A program may use at most 64 MiB of HBM per device.

```python
import math
import jax
import jax.numpy as jnp
import numpy as np
from jax import lax

D = 2048
HEADS = 16
HEAD = 128
L = 512
FF_L = 2048
VOCAB = 256
PATCH = 8
RANK = 16
TASKS = 8
PATCHES = 8192
BYTES = 65536
N_ROW = 8


def draw_patch_queries(key, part):
    values = 2.5 * jnp.clip(jax.random.normal(jax.random.fold_in(key, 11), (PATCHES, HEADS * HEAD), jnp.float32), -6.0, 6.0)
    return values.astype(jnp.bfloat16)


def draw_patch_keys(key, part):
    values = jnp.clip(jax.random.normal(jax.random.fold_in(key, 13), (PATCHES, HEADS * HEAD), jnp.float32), -6.0, 6.0)
    return values.astype(jnp.bfloat16)


def plant(array, rng, least, high):
    longest = array.shape.index(max(array.shape))
    spots = []
    for shift in (0, 1):
        where = [jax.random.randint(jax.random.fold_in(rng, axis), (), 0, length) for axis, length in enumerate(array.shape)]
        where[longest] = (where[longest] + shift) % array.shape[longest]
        spots.append(tuple(where))
    return array.at[spots[0]].set(least).at[spots[1]].set(high)


def block_scale(own_key, shape, pieces, smallest, largest):
    loudness = 1.0
    for axis_at, blocks in pieces:
        draws = jax.random.uniform(jax.random.fold_in(jax.random.fold_in(own_key, 6), axis_at), (blocks,), jnp.float32, smallest / len(pieces), largest / len(pieces))
        loudness = loudness * jnp.repeat(jnp.exp(draws), shape[axis_at] // blocks).reshape((-1,) + (1,) * (len(shape) - 1 - axis_at))
    return loudness


def rank_table(count, skew):
    portions = [(1 << 20) // math.isqrt(rank ** skew) + 1 for rank in range(1, count + 1)]
    scale = 1 + sum(portions) // (1 << 30)
    return np.cumsum(np.array([max(1, weight // scale) for weight in portions]))


def skewed_ids(stream_key, dims, count, lean):
    table = rank_table(count, lean)
    lot = jax.random.randint(jax.random.fold_in(stream_key, 1), dims, 0, int(table[count - 1]))
    grade = jnp.searchsorted(jnp.asarray(table, jnp.int32), lot, side="right")
    return jax.random.permutation(jax.random.fold_in(stream_key, 2), count)[grade].astype(jnp.int32)


def centred(own_key, shape, spread, bound, pieces=(), held_as=jnp.bfloat16):
    loudness = block_scale(own_key, shape, pieces, -0.22, 0.18) if pieces else 1.0
    result = jax.random.normal(own_key, shape, jnp.float32) * spread * loudness
    return jnp.minimum(jnp.maximum(result, -bound), bound).astype(held_as)


def setup_inputs(seed: int = 0) -> dict:
    seeds = jax.random.split(jax.random.key(seed), 21)
    patch_queries = draw_patch_queries(jax.random.fold_in(seeds[20], 71), 0)
    patch_keys = draw_patch_keys(jax.random.fold_in(seeds[20], 71), 0)
    patch_values = centred(seeds[2], (PATCHES, HEADS * HEAD), 1.0, 6.0, ((0, 64), (1, 8)))
    patch_tasks = plant(jax.random.randint(seeds[3], (PATCHES,), 0, TASKS), jax.random.fold_in(seeds[3], 1), 0, TASKS - 1).astype(jnp.int32)
    residual = centred(seeds[4], (PATCHES, D), 1.0, 6.0, ((0, 64), (1, 8)))
    output_weight = centred(seeds[5], (HEADS * HEAD, D), HEAD ** -0.5, 0.5, ((0, 8),))
    global_down = centred(seeds[6], (HEADS * HEAD, RANK), HEAD ** -0.5, 0.5, ((0, 8),))
    global_up = centred(seeds[7], (RANK, D), RANK ** -0.5, 1.5, ((1, 8),))
    global_scales = jnp.clip(jnp.exp(jax.random.uniform(seeds[8], (TASKS, RANK), jnp.float32, math.log(0.25), math.log(4.0))), 0.25, 4.0)
    local_weight = centred(seeds[9], (D, L), D ** -0.5, 0.125, ((0, 8),))
    byte_ids = plant(skewed_ids(seeds[10], (BYTES,), VOCAB, 2), jax.random.fold_in(seeds[10], 3), 0, VOCAB - 1).astype(jnp.int32)
    byte_table = centred(seeds[11], (VOCAB, L), 1.0, 6.0)
    position_table = centred(seeds[12], (PATCH, L), 1.0, 6.0)
    norm_gain = jnp.clip(1.0 + 0.1 * jax.random.normal(seeds[13], (L,), jnp.float32), 0.5, 1.5)
    hidden_in = centred(seeds[14], (FF_L, L), L ** -0.5, 0.25, ((0, 8), (1, 64)))
    hidden_out = centred(seeds[15], (FF_L, L), FF_L ** -0.5, 0.125, ((0, 8), (1, 64)))
    local_down = centred(seeds[16], (L, RANK), L ** -0.5, 0.25)
    local_up = centred(seeds[17], (RANK, FF_L), RANK ** -0.5, 1.5, ((1, 8),))
    local_scales = jnp.clip(jnp.exp(jax.random.uniform(seeds[18], (TASKS, RANK), jnp.float32, math.log(0.25), math.log(4.0))), 0.25, 4.0)
    cotangent = centred(seeds[19], (BYTES, L), 1.0, 6.0, ((0, 512),))
    return {"patch_queries": patch_queries, "patch_keys": patch_keys, "patch_values": patch_values, "patch_tasks": patch_tasks, "residual": residual, "output_weight": output_weight, "global_down": global_down, "global_up": global_up, "global_scales": global_scales, "local_weight": local_weight, "byte_ids": byte_ids, "byte_table": byte_table, "position_table": position_table, "norm_gain": norm_gain, "hidden_in": hidden_in, "hidden_out": hidden_out, "local_down": local_down, "local_up": local_up, "local_scales": local_scales, "cotangent": cotangent}


def rounded(value):
    return lax.optimization_barrier(value.astype(jnp.bfloat16)).astype(jnp.float32)

def contract(left, right, left_dim, right_dim):
    return lax.dot_general(left, right, (((left_dim,), (right_dim,)), ((), ())), preferred_element_type=jnp.float32)

def select_rows(table, tasks):
    picks = (tasks[:, None] == jnp.arange(table.shape[0], dtype=jnp.int32)[None, :]).astype(jnp.float32)
    return jnp.dot(picks, table, precision=lax.Precision.HIGHEST)

def task_totals(tasks, values):
    picks = (tasks[:, None] == jnp.arange(TASKS, dtype=jnp.int32)[None, :]).astype(jnp.float32)
    return lax.dot_general(picks, values, (((0,), (0,)), ((), ())), precision=lax.Precision.HIGHEST)

def gelu_slope(upper):
    cumulative = 0.5 * (1.0 + lax.erf(upper * 0.7071067811865476))
    density = jnp.exp(-0.5 * upper * upper) * 0.3989422804014327
    return cumulative + upper * density

def local_inputs(identities, projected, tasks, byte_table, position_table, norm_gain, local_down, local_scales):
    count = identities.shape[0]
    picks = (identities[:, None] == jnp.arange(VOCAB, dtype=jnp.int32)[None, :]).astype(jnp.bfloat16)
    embedded = jnp.dot(picks, byte_table, preferred_element_type=jnp.float32)
    patches = count // PATCH
    inputs = embedded.reshape(patches, PATCH, -1) + position_table.astype(jnp.float32)[None] + projected.astype(jnp.float32)[:, None, :]
    inputs = inputs.reshape(count, -1)
    inverse = lax.rsqrt(lax.optimization_barrier(jnp.mean(inputs * inputs, axis=1, keepdims=True)) + 1e-06)
    normed = (inputs * inverse * norm_gain).astype(jnp.bfloat16)
    lowered = jnp.dot(normed, local_down, preferred_element_type=jnp.float32)
    byte_tasks = jnp.repeat(tasks, PATCH)
    scales = select_rows(local_scales, byte_tasks)
    shrunk = (lowered * scales).astype(jnp.bfloat16)
    return (inputs, inverse, normed, lowered, scales, shrunk, byte_tasks)

def backward_norm(back_total, inputs, inverse, norm_gain, cotangent):
    gained = back_total * norm_gain
    average = lax.optimization_barrier(jnp.mean(gained * inputs, axis=1, keepdims=True))
    return cotangent.astype(jnp.float32) + inverse * (gained - inputs * inverse * inverse * average)

def causal_attention(patch_queries, patch_keys, patch_values):
    total = patch_queries.shape[0]
    width = patch_queries.shape[1]
    heads = width // HEAD
    block = math.gcd(total, 512)
    key_heads = patch_keys.reshape(total, heads, HEAD).astype(jnp.float32)
    value_heads = patch_values.reshape(total, heads, HEAD).astype(jnp.float32)
    places = jnp.arange(total, dtype=jnp.int32)
    scale = 1.0 / math.sqrt(HEAD)

    def one_block(index):
        first = index * block
        query_heads = lax.dynamic_slice_in_dim(patch_queries, first, block, 0).reshape(block, heads, HEAD).astype(jnp.float32)
        scores = jnp.einsum('qhd,khd->hqk', query_heads, key_heads) * scale
        allowed = places[None, :] <= (first + jnp.arange(block, dtype=jnp.int32))[:, None]
        scores = jnp.where(allowed[None], scores, -1e+30)
        top = lax.optimization_barrier(jnp.max(scores, axis=2, keepdims=True))
        weights = jnp.where(allowed[None], jnp.exp(scores - top), 0.0)
        mass = lax.optimization_barrier(jnp.sum(weights, axis=2))
        mixed = jnp.einsum('hqk,khd->qhd', rounded(weights), value_heads)
        mixed = mixed / jnp.transpose(mass)[:, :, None]
        return mixed.reshape(block, width).astype(jnp.bfloat16)
    blocks = lax.map(one_block, jnp.arange(total // block, dtype=jnp.int32))
    return blocks.reshape(total, width)

def reference(patch_queries, patch_keys, patch_values, patch_tasks, residual, output_weight, global_down, global_up, global_scales, local_weight, byte_ids, byte_table, position_table, norm_gain, hidden_in, hidden_out, local_down, local_up, local_scales, cotangent):
    attended = causal_attention(patch_queries, patch_keys, patch_values)
    reduced = jnp.dot(attended, global_down, preferred_element_type=jnp.float32)
    task_scales = select_rows(global_scales, patch_tasks)
    scaled = (reduced * task_scales).astype(jnp.bfloat16)
    mixed = residual.astype(jnp.float32) + jnp.dot(scaled, global_up, preferred_element_type=jnp.float32)
    group = HEADS * HEAD // N_ROW
    for index in range(N_ROW):
        part = jnp.dot(attended[:, index * group:(index + 1) * group], output_weight[index * group:(index + 1) * group], preferred_element_type=jnp.float32)
        mixed = mixed + rounded(part)
    mixed_b = mixed.astype(jnp.bfloat16)
    projected = jnp.dot(mixed_b, local_weight, preferred_element_type=jnp.float32).astype(jnp.bfloat16)
    inputs, inverse, normed, lowered, scales, shrunk, byte_tasks = local_inputs(byte_ids, projected, patch_tasks, byte_table, position_table, norm_gain, local_down, local_scales)
    hidden = FF_L // N_ROW
    back_norm = jnp.zeros(inputs.shape, jnp.float32)
    back_rank = jnp.zeros(lowered.shape, jnp.float32)
    pieces_up = []
    for index in range(N_ROW):
        rows_in = hidden_in[index * hidden:(index + 1) * hidden]
        rows_out = hidden_out[index * hidden:(index + 1) * hidden]
        columns_up = local_up[:, index * hidden:(index + 1) * hidden]
        upper = contract(normed, rows_in, 1, 1) + jnp.dot(shrunk, columns_up, preferred_element_type=jnp.float32)
        through = contract(cotangent, rows_out, 1, 1)
        grown = (through * gelu_slope(upper)).astype(jnp.bfloat16)
        pieces_up.append(contract(shrunk, grown, 0, 0))
        back_norm = back_norm + rounded(jnp.dot(grown, rows_in, preferred_element_type=jnp.float32))
        back_rank = back_rank + rounded(contract(grown, columns_up, 1, 1))
    grad_local_up = jnp.concatenate(pieces_up, axis=1)
    grad_local_scales = task_totals(byte_tasks, back_rank * lowered)
    moved = (back_rank * scales).astype(jnp.bfloat16)
    grad_local_down = contract(normed, moved, 0, 0)
    back_total = back_norm + contract(moved, local_down, 1, 1)
    back_inputs = backward_norm(back_total, inputs, inverse, norm_gain, cotangent)
    patch_grad = back_inputs.reshape(-1, PATCH, back_inputs.shape[1]).sum(axis=1).astype(jnp.bfloat16)
    back_mixed = contract(patch_grad, local_weight, 1, 1).astype(jnp.bfloat16)
    grad_global_up = contract(scaled, back_mixed, 0, 0)
    back_scaled = contract(back_mixed, global_up, 1, 1)
    grad_global_scales = task_totals(patch_tasks, back_scaled * reduced)
    back_reduced = (back_scaled * task_scales).astype(jnp.bfloat16)
    grad_global_down = contract(attended, back_reduced, 0, 0)
    return (grad_global_down, grad_global_up, grad_global_scales, grad_local_down, grad_local_up, grad_local_scales)
```

```python
import math

import jax
import jax.numpy as jnp
from jax import lax
from jax.sharding import Mesh
from jax.sharding import PartitionSpec as P

HEAD = 128
VOCAB = 256
PATCH = 8
TASKS = 8
RANK = 16
ROW = ("row_0", "row_1")
SEQ = ("seq_0", "seq_1", "seq_2")
Z, FAR, CORE = SEQ
SEQ_ROW = SEQ + ROW
SWAP = [(0, 1), (1, 0)]
BF = jnp.bfloat16
F32 = jnp.float32


def exchange(pieces, axis):
    return lax.all_to_all(pieces, axis, split_axis=0, concat_axis=0, tiled=True)


def to_everyone(array, axis):
    size = lax.axis_size(axis)
    return exchange(jnp.broadcast_to(array[None], (size, *array.shape)), axis)


def contract(left, right, left_dim, right_dim):
    return lax.dot_general(
        left, right, (((left_dim,), (right_dim,)), ((), ())), preferred_element_type=F32
    )


def select_rows(table, tasks):
    picks = (tasks[:, None] == jnp.arange(table.shape[0], dtype=jnp.int32)[None, :]).astype(F32)
    return jnp.dot(picks, table, precision=lax.Precision.HIGHEST)


def task_totals(tasks, values):
    picks = (tasks[:, None] == jnp.arange(TASKS, dtype=jnp.int32)[None, :]).astype(F32)
    return lax.dot_general(picks, values, (((0,), (0,)), ((), ())), precision=lax.Precision.HIGHEST)


def gelu_slope(upper):
    cumulative = 0.5 * (1.0 + lax.erf(upper * 0.7071067811865476))
    density = jnp.exp(-0.5 * upper * upper) * 0.3989422804014327
    return cumulative + upper * density


def in_pair_order(mine, other, place, axis):
    first = jnp.where(place == 0, mine, other)
    second = jnp.where(place == 0, other, mine)
    return jnp.concatenate([first, second], axis=axis)


def attend(state, queries, query_places, keys, values, key_places):
    top, mass, out = state
    scores = contract(queries, keys, 1, 1) * (1.0 / math.sqrt(HEAD))
    allowed = key_places[None, :] <= query_places[:, None]
    scores = jnp.where(allowed, scores, -1e30)
    new_top = jnp.maximum(top, jnp.max(scores, axis=1, keepdims=True))
    weights = jnp.where(allowed, jnp.exp(scores - new_top), 0.0)
    shrink = jnp.exp(top - new_top)
    mass = mass * shrink + jnp.sum(weights, axis=1, keepdims=True)
    out = out * shrink + jnp.dot(weights.astype(BF), values, preferred_element_type=F32)
    return (new_top, mass, out)


def body(
    patch_queries,
    patch_keys,
    patch_values,
    patch_tasks,
    residual,
    output_weight,
    global_down,
    global_up,
    global_scales,
    local_weight,
    byte_ids,
    byte_table,
    position_table,
    norm_gain,
    hidden_in,
    hidden_out,
    local_down,
    local_up,
    local_scales,
    cotangent,
):
    rows, width = patch_queries.shape
    ring = lax.axis_size(Z)
    row_count = lax.axis_size(ROW)
    z = lax.axis_index(Z)
    far = lax.axis_index(FAR)
    core = lax.axis_index(CORE)
    row_index = lax.axis_index(ROW)
    columns = local_weight.shape[1]
    units = hidden_in.shape[0]
    share = hidden_in.shape[1]

    def head(array, which):
        return lax.dynamic_slice_in_dim(array, which * HEAD, HEAD, 1)

    trio = (patch_queries, patch_keys, patch_values)
    mine = jnp.concatenate([head(a, core) for a in trio], axis=1)
    other = jnp.concatenate([head(a, 1 - core) for a in trio], axis=1)
    both = jnp.concatenate([mine, lax.ppermute(other, CORE, SWAP)], axis=0)
    queries = both[:, :HEAD]
    hidden = jnp.concatenate([hidden_in.T, hidden_out.T], axis=0)
    halves = [hidden[:, k * HEAD : (k + 1) * HEAD] for k in range(units // HEAD)]
    arrived = lax.ppermute(jnp.concatenate([queries, *halves], axis=0), FAR, SWAP)
    chip_rows = 2 * rows
    tall = 2 * share
    far_hidden = jnp.concatenate(
        [
            arrived[chip_rows + k * tall : chip_rows + (k + 1) * tall]
            for k in range(units // HEAD)
        ],
        axis=1,
    )
    queries = jnp.concatenate([queries, arrived[:chip_rows]], axis=0)
    packet = jnp.concatenate([both[:, HEAD:], hidden, far_hidden], axis=0)

    def places(z_index, far_index):
        start = (z_index * 4 + far_index * 2) * rows
        count = jnp.arange(rows, dtype=jnp.int32)
        return jnp.concatenate([start + core * rows + count, start + (1 - core) * rows + count])

    query_places = jnp.concatenate([places(z, far), places(z, 1 - far)])
    total = 2 * chip_rows
    state = (
        jnp.full((total, 1), -1e30, F32),
        jnp.zeros((total, 1), F32),
        jnp.zeros((total, HEAD), F32),
    )
    up = [(i, (i + 1) % ring) for i in range(ring)]
    down = [(i, (i - 1) % ring) for i in range(ring)]

    def visit(state, packets, indices):
        keys = jnp.concatenate([p[:chip_rows, :HEAD] for p in packets])
        values = jnp.concatenate([p[:chip_rows, HEAD:] for p in packets])
        key_places = jnp.concatenate([places(i, far) for i in indices])
        return attend(state, queries, query_places, keys, values, key_places)

    riders = [None] * ring
    riders[0] = packet[chip_rows:]
    rising = falling = packet
    now, at = [packet], [z]
    for step in range(1, ring // 2 + 1):
        rising = lax.ppermute(rising, Z, up)
        riders[-step % ring] = rising[chip_rows:]
        later, then = [rising], [(z - step) % ring]
        if step < ring // 2:
            falling = lax.ppermute(falling, Z, down)
            riders[step] = falling[chip_rows:]
            later.append(falling)
            then.append((z + step) % ring)
        state = visit(state, now, at)
        now, at = later, then
    state = visit(state, now, at)

    top, mass, out = state
    level = jnp.where(mass > 0, top + jnp.log(jnp.where(mass > 0, mass, 1.0)), -1e30)
    out = out / jnp.where(mass > 0, mass, 1.0)
    sent = level[chip_rows:]
    high = sent.astype(BF)
    middle = (sent - high.astype(F32)).astype(BF)
    low = (sent - high.astype(F32) - middle.astype(F32)).astype(BF)
    wide = [jnp.broadcast_to(a, (chip_rows, n)) for a, n in ((high, 32), (middle, 32), (low, 64))]
    met = lax.ppermute(jnp.concatenate([out[chip_rows:].astype(BF), *wide], axis=1), FAR, SWAP)
    met = met.astype(F32)
    far_level = met[:, 128:129] + met[:, 160:161] + met[:, 192:193]
    own_level = level[:chip_rows]
    peak = jnp.maximum(own_level, far_level)
    own_part = jnp.exp(own_level - peak)
    far_part = jnp.exp(far_level - peak)
    merged = (own_part * out[:chip_rows] + far_part * met[:, :HEAD]) / (own_part + far_part)
    merged = merged.astype(BF)
    partner = lax.ppermute(merged[rows:], CORE, SWAP)
    attended = in_pair_order(merged[:rows], partner, core, 1)

    riders = jnp.stack(riders)
    riders = jnp.roll(riders, z, axis=0)
    riders = riders.reshape(ring, 2, tall, units)
    riders = in_pair_order(riders[:, 0:1], riders[:, 1:2], far, 1)
    rest = lax.ppermute(riders, CORE, SWAP)
    riders = in_pair_order(riders[:, :, None], rest[:, :, None], core, 2)
    riders = riders.reshape(ring, 2, 2, 2, share, units)
    rows_in = riders[:, :, :, 0].reshape(columns, units)
    rows_out = riders[:, :, :, 1].reshape(columns, units)
    lanes = 128
    stacked = jnp.concatenate(
        [rows_in, local_up, jnp.zeros((lanes - RANK, units), BF)], axis=0
    )

    up_rows = jnp.concatenate([global_up[:, :128], global_up[:, 128:]], axis=0)
    up_rows = jnp.concatenate([up_rows[8 * k : 8 * k + 8] for k in range(4)], axis=1)
    weights = jnp.concatenate([local_weight, up_rows], axis=0)
    weights = lax.all_gather(weights, ROW, axis=0, tiled=False)
    local_whole = weights[:, :width].reshape(-1, columns)
    up_rows = weights[:, width:]
    up_rows = jnp.concatenate([up_rows[:, :, 128 * k : 128 * k + 128] for k in range(4)], axis=1)
    up_whole = jnp.concatenate([up_rows[:, :RANK], up_rows[:, RANK:]], axis=2)
    cotangent_all = lax.all_gather(cotangent, ROW, axis=0, tiled=True)
    through = contract(cotangent_all, rows_out, 1, 0)

    task_scales = select_rows(global_scales, patch_tasks)
    part = contract(output_weight, attended, 0, 1).astype(BF).reshape(row_count, width, rows)
    low_part = contract(global_down, attended, 0, 1).astype(BF)
    low_part = jnp.broadcast_to(low_part[None], (row_count, RANK, rows))
    arrived = exchange(jnp.concatenate([part, low_part], axis=1), ROW)
    arrived = arrived.astype(F32).sum(axis=0)
    reduced = jnp.transpose(arrived[width:])
    scaled = (reduced * task_scales).astype(BF)
    mixed = arrived[:width] + jnp.transpose(residual.astype(F32)) + contract(global_up, scaled, 0, 1)
    mixed_b = mixed.astype(BF)
    own_patches = rows // row_count
    own_bytes = own_patches * PATCH
    own_tasks = lax.dynamic_slice_in_dim(patch_tasks, row_index * own_patches, own_patches)
    own_ids = lax.dynamic_slice_in_dim(byte_ids, row_index * own_bytes, own_bytes)
    projected = contract(mixed_b, local_weight, 0, 0).astype(BF)
    projected = exchange(projected.reshape(row_count, own_patches, columns), ROW)
    projected = projected.astype(F32).sum(axis=0).astype(BF)

    picks = (own_ids[:, None] == jnp.arange(VOCAB, dtype=jnp.int32)[None, :]).astype(BF)
    embedded = jnp.dot(picks, byte_table, preferred_element_type=F32)
    embedded = embedded.reshape(own_patches, PATCH, -1) + position_table.astype(F32)[None]
    inputs = (embedded + projected.astype(F32)[:, None, :]).reshape(own_bytes, columns)
    inverse = lax.rsqrt(jnp.mean(inputs * inputs, axis=1, keepdims=True) + 1e-06)
    normed = (inputs * inverse * norm_gain).astype(BF)
    lowered = jnp.dot(normed, local_down, preferred_element_type=F32)
    byte_tasks = jnp.repeat(own_tasks, PATCH)
    scales = select_rows(local_scales, byte_tasks)
    shrunk = (lowered * scales).astype(BF)
    joined = jnp.concatenate(
        [normed, shrunk, jnp.zeros((own_bytes, lanes - RANK), BF)], axis=1
    )
    joined = to_everyone(joined, ROW).reshape(row_count * own_bytes, columns + lanes)
    upper = contract(joined, stacked, 1, 0)
    grown = (through * gelu_slope(upper)).astype(BF)
    grad_local_up = contract(joined[:, columns:], grown, 0, 0)[:RANK]
    back = contract(grown, stacked, 1, 1).astype(BF)
    back = exchange(back.reshape(row_count, own_bytes, columns + lanes), ROW)
    back = back.astype(F32).sum(axis=0)
    back_norm = back[:, :columns]
    back_rank = back[:, columns : columns + RANK]
    grad_local_scales = task_totals(byte_tasks, back_rank * lowered)
    moved = (back_rank * scales).astype(BF)
    grad_local_down = contract(moved, normed, 0, 0)
    back_total = back_norm + contract(moved, local_down, 1, 1)
    gained = back_total * norm_gain
    average = jnp.mean(gained * inputs, axis=1, keepdims=True)
    back_inputs = cotangent.astype(F32) + inverse * (
        gained - inputs * inverse * inverse * average
    )
    patch_grad = back_inputs.reshape(own_patches, PATCH, -1).sum(axis=1).astype(BF)

    spare = jnp.zeros((TASKS, columns - RANK), F32)
    local_rows = jnp.concatenate([grad_local_scales, spare], axis=1)
    local_rows = jnp.concatenate([grad_local_down, local_rows, jnp.zeros_like(local_rows)])
    row_pack = jnp.concatenate([patch_grad, local_rows.astype(BF)], axis=0)
    row_pack = to_everyone(row_pack, ROW)
    patch_grads = row_pack[:, :own_patches].reshape(rows, columns)
    local_sums = row_pack[:, own_patches:].astype(F32).sum(axis=0)
    back_mixed = contract(patch_grads, local_weight, 1, 1).astype(BF)
    back_whole = contract(patch_grads, local_whole, 1, 1).astype(BF)
    up_flat = jnp.transpose(up_whole, (1, 0, 2)).reshape(RANK, -1)
    back_scaled = contract(back_whole, up_flat, 1, 1)
    grad_global_up = contract(scaled, back_mixed, 0, 0)
    grad_global_scales = task_totals(patch_tasks, back_scaled * reduced)
    back_reduced = (back_scaled * task_scales).astype(BF)
    grad_global_down = contract(back_reduced, attended, 0, 0)

    small = jnp.concatenate([grad_global_scales, jnp.zeros((TASKS, width - RANK), F32)], axis=1)
    small_local = local_sums[RANK : RANK + TASKS, :width]
    packed = jnp.concatenate(
        [
            grad_global_down,
            grad_global_up,
            grad_local_up,
            local_sums[:RANK, :width],
            local_sums[:RANK, width:],
            small,
            small_local,
        ]
    ).astype(BF)
    shape = packed.shape
    pieces = packed.reshape(lax.axis_size(SEQ), -1)
    pieces = exchange(pieces, SEQ).astype(F32).sum(axis=0).astype(BF)
    packed = to_everyone(pieces, SEQ).reshape(shape).astype(F32)
    return (
        jnp.transpose(packed[:16]),
        packed[16:32],
        packed[80:88, :RANK],
        jnp.transpose(jnp.concatenate([packed[48:64], packed[64:80]], axis=1)),
        packed[32:48],
        packed[88:96, :RANK],
    )


def solution(mesh):
    torus = Mesh(mesh.devices.reshape(16, 2, 2, 4, 2), SEQ_ROW)
    placed = (
        P(SEQ, ROW),
        P(SEQ, ROW),
        P(SEQ, ROW),
        P(SEQ),
        P(SEQ, ROW),
        P(ROW, None),
        P(ROW, None),
        P(None, ROW),
        P(),
        P(ROW, None),
        P(SEQ),
        P(),
        P(),
        P(),
        P(ROW, SEQ),
        P(ROW, SEQ),
        P(),
        P(None, ROW),
        P(),
        P(SEQ_ROW, None),
    )
    return jax.shard_map(
        body,
        mesh=torus,
        in_specs=placed,
        out_specs=(P(ROW, None), P(None, ROW), P(), P(), P(None, ROW), P()),
        check_vma=False,
    )
```

```python
import math

import jax
import jax.numpy as jnp
from jax import lax
from jax.sharding import Mesh
from jax.sharding import PartitionSpec as P

HEAD = 128
VOCAB = 256
PATCH = 8
TASKS = 8
RANK = 16
ROW = ("row_0", "row_1")
SEQ = ("seq_0", "near", "seq_1", "seq_2")
Z, NEAR, FAR, CORE = SEQ
QUAD = (NEAR, FAR)
LINE, SIDE = ROW
SEQ_ROW = SEQ + ROW
SWAP = [(0, 1), (1, 0)]
BF = jnp.bfloat16
F32 = jnp.float32


def exchange(pieces, axis):
    return lax.all_to_all(pieces, axis, split_axis=0, concat_axis=0, tiled=True)


def to_everyone(array, axis):
    size = lax.axis_size(axis)
    return exchange(jnp.broadcast_to(array[None], (size, *array.shape)), axis)


def contract(left, right, left_dim, right_dim):
    return lax.dot_general(
        left, right, (((left_dim,), (right_dim,)), ((), ())), preferred_element_type=F32
    )


def select_rows(table, tasks):
    picks = (tasks[:, None] == jnp.arange(table.shape[0], dtype=jnp.int32)[None, :]).astype(F32)
    return jnp.dot(picks, table, precision=lax.Precision.HIGHEST)


def task_totals(tasks, values):
    picks = (tasks[:, None] == jnp.arange(TASKS, dtype=jnp.int32)[None, :]).astype(F32)
    return lax.dot_general(picks, values, (((0,), (0,)), ((), ())), precision=lax.Precision.HIGHEST)


def gelu_slope(upper):
    cumulative = 0.5 * (1.0 + lax.erf(upper * 0.7071067811865476))
    density = jnp.exp(-0.5 * upper * upper) * 0.3989422804014327
    return cumulative + upper * density


def in_pair_order(mine, other, place, axis):
    first = jnp.where(place == 0, mine, other)
    second = jnp.where(place == 0, other, mine)
    return jnp.concatenate([first, second], axis=axis)


def total(array):
    return lax.optimization_barrier(array.astype(F32).sum(axis=0))


def fold(array):
    array = jnp.concatenate([array[:, :128], array[:, 128:]], axis=0)
    return jnp.concatenate([array[8 * k : 8 * k + 8] for k in range(4)], axis=1)


def unfold(array):
    array = jnp.concatenate([array[:, :, 128 * k : 128 * k + 128] for k in range(4)], axis=1)
    return jnp.concatenate([array[:, :RANK], array[:, RANK:]], axis=2)


def attend(state, queries, query_places, keys, values, key_places):
    top, mass, out = state
    scores = contract(queries, keys, 1, 1) * (1.0 / math.sqrt(HEAD))
    allowed = key_places[None, :] <= query_places[:, None]
    scores = jnp.where(allowed, scores, -1e30)
    new_top = jnp.maximum(top, jnp.max(scores, axis=1, keepdims=True))
    weights = jnp.where(allowed, jnp.exp(scores - new_top), 0.0)
    shrink = jnp.exp(top - new_top)
    mass = mass * shrink + jnp.sum(weights, axis=1, keepdims=True)
    out = out * shrink + jnp.dot(weights.astype(BF), values, preferred_element_type=F32)
    return (new_top, mass, out)


def body(
    patch_queries,
    patch_keys,
    patch_values,
    patch_tasks,
    residual,
    output_weight,
    global_down,
    global_up,
    global_scales,
    local_weight,
    byte_ids,
    byte_table,
    position_table,
    norm_gain,
    hidden_in,
    hidden_out,
    local_down,
    local_up,
    local_scales,
    cotangent,
):
    rows, width = patch_queries.shape
    ring = lax.axis_size(Z)
    row_count = lax.axis_size(ROW)
    z = lax.axis_index(Z)
    near = lax.axis_index(NEAR)
    far = lax.axis_index(FAR)
    side = lax.axis_index(SIDE)
    core = lax.axis_index(CORE)
    row_index = lax.axis_index(ROW)
    columns = local_weight.shape[1]
    units = hidden_in.shape[0]
    share = hidden_in.shape[1]

    weights = jnp.concatenate([local_weight, fold(global_up), fold(local_up)], axis=0)
    weights = lax.all_gather(weights, ROW, axis=0, tiled=False)
    local_whole = weights[:, :width].reshape(-1, columns)
    up_whole = unfold(weights[:, width : width + 8])
    up_whole = jnp.transpose(up_whole, (1, 0, 2)).reshape(RANK, -1)
    line = lax.axis_size(LINE)
    local_ups = unfold(weights[:, width + 8 :]).reshape(line, 2, RANK, units)
    local_ups = lax.dynamic_index_in_dim(local_ups, side, 1, keepdims=False)
    local_ups = jnp.concatenate([local_ups[k] for k in range(line)], axis=1)
    cotangents = jnp.concatenate([cotangent, lax.ppermute(cotangent, SIDE, SWAP)], axis=0)

    def head(array, which):
        return lax.dynamic_slice_in_dim(array, which * HEAD, HEAD, 1)

    trio = (patch_queries, patch_keys, patch_values)
    mine = jnp.concatenate([head(a, core) for a in trio], axis=1)
    other = jnp.concatenate([head(a, 1 - core) for a in trio], axis=1)
    both = jnp.concatenate([mine, lax.ppermute(other, CORE, SWAP)], axis=0)
    hidden = jnp.concatenate([hidden_in.T, hidden_out.T], axis=0)
    halves = [hidden[:, k * HEAD : (k + 1) * HEAD] for k in range(units // HEAD)]
    chip_rows = 2 * rows
    tall = 2 * share
    quad = to_everyone(jnp.concatenate([both[:, :HEAD], *halves], axis=0), QUAD)
    sides = lax.axis_size(QUAD)
    queries = quad[:, :chip_rows].reshape(sides * chip_rows, HEAD)
    quad_hidden = jnp.concatenate(
        [
            quad[:, chip_rows + k * tall : chip_rows + (k + 1) * tall].reshape(sides * tall, HEAD)
            for k in range(units // HEAD)
        ],
        axis=1,
    )
    packet = jnp.concatenate([both[:, HEAD:], quad_hidden], axis=0)

    def places(z_index, near_index, far_index):
        start = (z_index * 8 + near_index * 4 + far_index * 2) * rows
        count = jnp.arange(rows, dtype=jnp.int32)
        return jnp.concatenate([start + core * rows + count, start + (1 - core) * rows + count])

    query_places = jnp.concatenate([places(z, k // 2, k % 2) for k in range(sides)])
    count = sides * chip_rows
    state = (
        jnp.full((count, 1), -1e30, F32),
        jnp.zeros((count, 1), F32),
        jnp.zeros((count, HEAD), F32),
    )
    up = [(i, (i + 1) % ring) for i in range(ring)]
    down = [(i, (i - 1) % ring) for i in range(ring)]

    def visit(state, packets, indices):
        keys = jnp.concatenate([p[:chip_rows, :HEAD] for p in packets])
        values = jnp.concatenate([p[:chip_rows, HEAD:] for p in packets])
        key_places = jnp.concatenate([places(i, near, far) for i in indices])
        return attend(state, queries, query_places, keys, values, key_places)

    riders = [None] * ring
    riders[0] = packet[chip_rows:]
    rising = falling = packet
    now, at = [packet], [z]
    for step in range(1, ring // 2 + 1):
        rising = lax.ppermute(rising, Z, up)
        riders[-step % ring] = rising[chip_rows:]
        later, then = [rising], [(z - step) % ring]
        if step < ring // 2:
            falling = lax.ppermute(falling, Z, down)
            riders[step] = falling[chip_rows:]
            later.append(falling)
            then.append((z + step) % ring)
        state = visit(state, now, at)
        now, at = later, then
    state = visit(state, now, at)
    state, local_whole, up_whole, local_ups, cotangents = lax.optimization_barrier(
        (state, local_whole, up_whole, local_ups, cotangents)
    )

    riders = jnp.roll(jnp.stack(riders), z, axis=0).reshape(ring * sides * tall, units)
    riders = lax.all_gather(riders, LINE, axis=0, tiled=False)

    top, mass, out = state
    level = jnp.where(mass > 0, top + jnp.log(jnp.where(mass > 0, mass, 1.0)), -1e30)
    out = out / jnp.where(mass > 0, mass, 1.0)
    high = level.astype(BF)
    middle = (level - high.astype(F32)).astype(BF)
    low = (level - high.astype(F32) - middle.astype(F32)).astype(BF)
    wide = [jnp.broadcast_to(a, (count, n)) for a, n in ((high, 32), (middle, 32), (low, 64))]
    met = jnp.concatenate([out.astype(BF), *wide], axis=1)
    met = exchange(met.reshape(sides, chip_rows, 2 * HEAD), QUAD).astype(F32)
    levels = met[:, :, 128:129] + met[:, :, 160:161] + met[:, :, 192:193]
    parts = jnp.exp(levels - jnp.max(levels, axis=0, keepdims=True))
    merged = (parts * met[:, :, :HEAD]).sum(axis=0) / parts.sum(axis=0)
    merged = merged.astype(BF)
    partner = lax.ppermute(merged[rows:], CORE, SWAP)
    attended = in_pair_order(merged[:rows], partner, core, 1)

    task_scales = select_rows(global_scales, patch_tasks)
    part = contract(output_weight, attended, 0, 1).astype(BF).reshape(row_count, width, rows)
    low_part = contract(global_down, attended, 0, 1).astype(BF)
    low_part = jnp.broadcast_to(low_part[None], (row_count, RANK, rows))
    arrived = exchange(jnp.concatenate([part, low_part], axis=1), ROW)
    arrived, riders = lax.optimization_barrier((arrived, riders))
    arrived = arrived.astype(F32).sum(axis=0)

    rest = lax.ppermute(riders, CORE, SWAP)
    split = (line, ring * sides, 2, 1, share, units)
    riders = in_pair_order(riders.reshape(split), rest.reshape(split), core, 3)
    riders = jnp.moveaxis(riders, 2, 0).reshape(2, line, columns, units)
    rows_in, rows_out = (
        jnp.concatenate([riders[way, k] for k in range(line)], axis=1) for way in range(2)
    )
    lanes = 128
    stacked = jnp.concatenate(
        [rows_in, local_ups, jnp.zeros((lanes - RANK, line * units), BF)], axis=0
    )

    reduced = jnp.transpose(arrived[width:])
    scaled = (reduced * task_scales).astype(BF)
    mixed = arrived[:width] + jnp.transpose(residual.astype(F32)) + contract(global_up, scaled, 0, 1)
    mixed_b = mixed.astype(BF)
    own_patches = rows // row_count
    own_bytes = own_patches * PATCH
    own_tasks = lax.dynamic_slice_in_dim(patch_tasks, row_index * own_patches, own_patches)
    own_ids = lax.dynamic_slice_in_dim(byte_ids, row_index * own_bytes, own_bytes)
    projected = contract(mixed_b, local_weight, 0, 0).astype(BF)
    projected = exchange(projected.reshape(row_count, own_patches, columns), ROW)
    projected = total(projected).astype(BF)

    picks = (own_ids[:, None] == jnp.arange(VOCAB, dtype=jnp.int32)[None, :]).astype(BF)
    embedded = jnp.dot(picks, byte_table, preferred_element_type=F32)
    embedded = embedded.reshape(own_patches, PATCH, -1) + position_table.astype(F32)[None]
    inputs = (embedded + projected.astype(F32)[:, None, :]).reshape(own_bytes, columns)
    inverse = lax.rsqrt(jnp.mean(inputs * inputs, axis=1, keepdims=True) + 1e-06)
    normed = (inputs * inverse * norm_gain).astype(BF)
    lowered = jnp.dot(normed, local_down, preferred_element_type=F32)
    byte_tasks = jnp.repeat(own_tasks, PATCH)
    scales = select_rows(local_scales, byte_tasks)
    shrunk = (lowered * scales).astype(BF)
    joined = jnp.concatenate(
        [normed, shrunk, jnp.zeros((own_bytes, lanes - RANK), BF)], axis=1
    )
    joined = jnp.concatenate([joined, lax.ppermute(joined, SIDE, SWAP)], axis=0)
    through = contract(cotangents, rows_out, 1, 0)
    upper = contract(joined, stacked, 1, 0)
    grown = (through * gelu_slope(upper)).astype(BF)
    back = contract(grown, stacked, 1, 1)
    back = back[:own_bytes] + lax.ppermute(back[own_bytes:].astype(BF), SIDE, SWAP).astype(F32)
    ups = contract(joined[:, columns:], grown, 0, 0)[:RANK].astype(BF)
    back_norm = back[:, :columns]
    back_rank = back[:, columns : columns + RANK]
    grad_local_scales = task_totals(byte_tasks, back_rank * lowered)
    moved = (back_rank * scales).astype(BF)
    grad_local_down = contract(moved, normed, 0, 0)
    back_total = back_norm + contract(moved, local_down, 1, 1)
    gained = back_total * norm_gain
    average = jnp.mean(gained * inputs, axis=1, keepdims=True)
    back_inputs = cotangent.astype(F32) + inverse * (
        gained - inputs * inverse * inverse * average
    )
    patch_grad = back_inputs.reshape(own_patches, PATCH, -1).sum(axis=1)
    patch_grad = lax.optimization_barrier(patch_grad).astype(BF)

    spare = jnp.zeros((TASKS, columns - RANK), F32)
    local_rows = jnp.concatenate([grad_local_scales, spare], axis=1)
    local_rows = jnp.concatenate([grad_local_down, local_rows, jnp.zeros_like(local_rows)])
    row_pack = jnp.concatenate([patch_grad, local_rows.astype(BF)], axis=0)
    row_pack = jnp.broadcast_to(row_pack[None], (row_count, *row_pack.shape))
    ups = jnp.stack([ups[:, units * k : units * (k + 1)] for k in range(line)])
    ups = jnp.stack([jnp.where(side == k, ups, jnp.zeros_like(ups)) for k in range(2)], axis=1)
    ups = jnp.pad(ups.reshape(row_count, RANK, units), [(0, 0), (0, 0), (0, columns - units)])
    row_pack = exchange(jnp.concatenate([row_pack, ups], axis=1), ROW)
    patch_grads = row_pack[:, :own_patches].reshape(rows, columns)
    local_sums = total(row_pack[:, own_patches:])
    back_mixed = contract(patch_grads, local_weight, 1, 1).astype(BF)
    back_whole = contract(patch_grads, local_whole, 1, 1).astype(BF)
    back_scaled = contract(back_whole, up_whole, 1, 1)
    grad_global_up = contract(scaled, back_mixed, 0, 0)
    grad_global_scales = task_totals(patch_tasks, back_scaled * reduced)
    back_reduced = (back_scaled * task_scales).astype(BF)
    grad_global_down = contract(back_reduced, attended, 0, 0)

    small = jnp.concatenate([grad_global_scales, jnp.zeros((TASKS, width - RANK), F32)], axis=1)
    small_local = local_sums[RANK : RANK + TASKS, :width]
    packed = jnp.concatenate(
        [
            grad_global_down,
            grad_global_up,
            local_sums[2 * RANK :, :units],
            local_sums[:RANK, :width],
            local_sums[:RANK, width:],
            small,
            small_local,
        ]
    ).astype(BF)
    shape = packed.shape
    pieces = packed.reshape(lax.axis_size(SEQ), -1)
    pieces = exchange(pieces, SEQ).astype(F32).sum(axis=0)
    packed = to_everyone(pieces, SEQ).reshape(shape)
    return (
        jnp.transpose(packed[:16]),
        packed[16:32],
        packed[80:88, :RANK],
        jnp.transpose(jnp.concatenate([packed[48:64], packed[64:80]], axis=1)),
        packed[32:48],
        packed[88:96, :RANK],
    )


def solution(mesh):
    torus = Mesh(mesh.devices.reshape(8, 2, 2, 2, 4, 2), SEQ_ROW)
    placed = (
        P(SEQ, ROW),
        P(SEQ, ROW),
        P(SEQ, ROW),
        P(SEQ),
        P(SEQ, ROW),
        P(ROW, None),
        P(ROW, None),
        P(None, ROW),
        P(),
        P(ROW, None),
        P(SEQ),
        P(),
        P(),
        P(),
        P(ROW, SEQ),
        P(ROW, SEQ),
        P(),
        P(None, ROW),
        P(),
        P(SEQ_ROW, None),
    )
    return jax.shard_map(
        body,
        mesh=torus,
        in_specs=placed,
        out_specs=(P(ROW, None), P(None, ROW), P(), P(), P(None, ROW), P()),
        check_vma=False,
    )
```

```python
import math

import jax
import jax.numpy as jnp
from jax import lax
from jax.sharding import Mesh
from jax.sharding import PartitionSpec as P

HEAD = 128
VOCAB = 256
PATCH = 8
TASKS = 8
RANK = 16
ROW = ("row_0", "row_1")
SEQ = ("seq_0", "near", "seq_1", "seq_2")
Z, NEAR, FAR, CORE = SEQ
QUAD = (NEAR, FAR)
EIGHT = (NEAR, FAR, CORE)
LINE, SIDE = ROW
SEQ_ROW = SEQ + ROW
SWAP = [(0, 1), (1, 0)]
BF = jnp.bfloat16
F32 = jnp.float32


def exchange(pieces, axis):
    return lax.all_to_all(pieces, axis, split_axis=0, concat_axis=0, tiled=True)


def to_everyone(array, axis):
    size = lax.axis_size(axis)
    return exchange(jnp.broadcast_to(array[None], (size, *array.shape)), axis)


def contract(left, right, left_dim, right_dim):
    return lax.dot_general(
        left, right, (((left_dim,), (right_dim,)), ((), ())), preferred_element_type=F32
    )


def select_rows(table, tasks):
    picks = (tasks[:, None] == jnp.arange(table.shape[0], dtype=jnp.int32)[None, :]).astype(F32)
    return jnp.dot(picks, table, precision=lax.Precision.HIGHEST)


def task_totals(tasks, values):
    picks = (tasks[:, None] == jnp.arange(TASKS, dtype=jnp.int32)[None, :]).astype(F32)
    return lax.dot_general(picks, values, (((0,), (0,)), ((), ())), precision=lax.Precision.HIGHEST)


def gelu_slope(upper):
    cumulative = 0.5 * (1.0 + lax.erf(upper * 0.7071067811865476))
    density = jnp.exp(-0.5 * upper * upper) * 0.3989422804014327
    return cumulative + upper * density


def in_pair_order(mine, other, place, axis):
    first = jnp.where(place == 0, mine, other)
    second = jnp.where(place == 0, other, mine)
    return jnp.concatenate([first, second], axis=axis)


def total(array):
    return lax.optimization_barrier(array.astype(F32).sum(axis=0))


def fold(array):
    array = jnp.concatenate([array[:, :128], array[:, 128:]], axis=0)
    return jnp.concatenate([array[8 * k : 8 * k + 8] for k in range(4)], axis=1)


def unfold(array):
    array = jnp.concatenate([array[:, :, 128 * k : 128 * k + 128] for k in range(4)], axis=1)
    return jnp.concatenate([array[:, :RANK], array[:, RANK:]], axis=2)


def attend(state, queries, query_places, keys, values, key_places):
    top, mass, out = state
    scores = contract(queries, keys, 1, 1) * (1.0 / math.sqrt(HEAD))
    allowed = key_places[None, :] <= query_places[:, None]
    scores = jnp.where(allowed, scores, -1e30)
    new_top = jnp.maximum(top, jnp.max(scores, axis=1, keepdims=True))
    weights = jnp.where(allowed, jnp.exp(scores - new_top), 0.0)
    shrink = jnp.exp(top - new_top)
    mass = mass * shrink + jnp.sum(weights, axis=1, keepdims=True)
    out = out * shrink + jnp.dot(weights.astype(BF), values, preferred_element_type=F32)
    return (new_top, mass, out)


def body(
    patch_queries,
    patch_keys,
    patch_values,
    patch_tasks,
    residual,
    output_weight,
    global_down,
    global_up,
    global_scales,
    local_weight,
    byte_ids,
    byte_table,
    position_table,
    norm_gain,
    hidden_in,
    hidden_out,
    local_down,
    local_up,
    local_scales,
    cotangent,
):
    rows, width = patch_queries.shape
    ring = lax.axis_size(Z)
    row_count = lax.axis_size(ROW)
    z = lax.axis_index(Z)
    near = lax.axis_index(NEAR)
    far = lax.axis_index(FAR)
    side = lax.axis_index(SIDE)
    core = lax.axis_index(CORE)
    row_index = lax.axis_index(ROW)
    columns = local_weight.shape[1]
    units = hidden_in.shape[0]
    share = hidden_in.shape[1]

    hidden = jnp.concatenate([hidden_in.T, hidden_out.T], axis=0)
    hidden = in_pair_order(hidden, lax.ppermute(hidden, FAR, SWAP), far, 0)
    weights = jnp.concatenate([local_weight, fold(global_up), fold(local_up)], axis=0)
    weights = lax.all_gather(weights, ROW, axis=0, tiled=False)
    cotangents = jnp.concatenate([cotangent, lax.ppermute(cotangent, SIDE, SWAP)], axis=0)

    def head(array, which):
        return lax.dynamic_slice_in_dim(array, which * HEAD, HEAD, 1)

    trio = (patch_queries, patch_keys, patch_values)
    mine = jnp.concatenate([head(a, core) for a in trio], axis=1)
    other = jnp.concatenate([head(a, 1 - core) for a in trio], axis=1)
    both = jnp.concatenate([mine, lax.ppermute(other, CORE, SWAP)], axis=0)
    chip_rows = 2 * rows
    packet = both[:, HEAD:]
    quad = to_everyone(both[:, :HEAD], QUAD)
    sides = lax.axis_size(QUAD)
    queries = quad.reshape(sides * chip_rows, HEAD)

    def places(z_index, near_index, far_index):
        start = (z_index * 8 + near_index * 4 + far_index * 2) * rows
        count = jnp.arange(rows, dtype=jnp.int32)
        return jnp.concatenate([start + core * rows + count, start + (1 - core) * rows + count])

    query_places = jnp.concatenate([places(z, k // 2, k % 2) for k in range(sides)])
    count = sides * chip_rows
    state = (
        jnp.full((count, 1), -1e30, F32),
        jnp.zeros((count, 1), F32),
        jnp.zeros((count, HEAD), F32),
    )
    up = [(i, (i + 1) % ring) for i in range(ring)]
    down = [(i, (i - 1) % ring) for i in range(ring)]

    def visit(state, packets, indices):
        keys = jnp.concatenate([p[:, :HEAD] for p in packets])
        values = jnp.concatenate([p[:, HEAD:] for p in packets])
        key_places = jnp.concatenate([places(i, near, far) for i in indices])
        return attend(state, queries, query_places, keys, values, key_places)

    rising = falling = packet
    held, at = [[packet]], [[z]]
    for step in range(1, ring // 2 + 1):
        rising = lax.ppermute(rising, Z, up)
        held.append([rising])
        at.append([(z - step) % ring])
        if step < ring // 2:
            falling = lax.ppermute(falling, Z, down)
            held[-1].append(falling)
            at[-1].append((z + step) % ring)
        if step == 1:
            rising, falling, hidden, queries = lax.optimization_barrier(
                (rising, falling, hidden, queries)
            )
            hidden = to_everyone(hidden, (Z, NEAR)).reshape(-1, units)
        elif step == 2:
            rising, falling, hidden = lax.optimization_barrier((rising, falling, hidden))
        if step >= 2:
            state = visit(state, held[step - 2], at[step - 2])
    state = visit(state, held[-2], at[-2])
    state = visit(state, held[-1], at[-1])
    state, weights, hidden = lax.optimization_barrier((state, weights, hidden))
    riders = lax.all_gather(hidden, LINE, axis=0, tiled=False)

    local_whole = weights[:, :width].reshape(-1, columns)
    up_whole = unfold(weights[:, width : width + 8])
    up_whole = jnp.transpose(up_whole, (1, 0, 2)).reshape(RANK, -1)
    line = lax.axis_size(LINE)
    local_ups = unfold(weights[:, width + 8 :]).reshape(line, 2, RANK, units)
    local_ups = lax.dynamic_index_in_dim(local_ups, side, 1, keepdims=False)
    local_ups = jnp.concatenate([local_ups[k] for k in range(line)], axis=1)

    top, mass, out = state
    level = jnp.where(mass > 0, top + jnp.log(jnp.where(mass > 0, mass, 1.0)), -1e30)
    out = out / jnp.where(mass > 0, mass, 1.0)
    high = lax.reduce_precision(level, 8, 7)
    middle = lax.reduce_precision(level - high, 8, 7)
    low = level - high - middle
    wide = [
        jnp.broadcast_to(a.astype(BF), (count, n))
        for a, n in ((high, 32), (middle, 32), (low, 64))
    ]
    met = jnp.concatenate([out.astype(BF), *wide], axis=1)
    met = exchange(met.reshape(sides, chip_rows, 2 * HEAD), QUAD).astype(F32)
    levels = met[:, :, 128:129] + met[:, :, 160:161] + met[:, :, 192:193]
    parts = jnp.exp(levels - jnp.max(levels, axis=0, keepdims=True))
    merged = (parts * met[:, :, :HEAD]).sum(axis=0) / parts.sum(axis=0)
    merged = merged.astype(BF)
    partner = lax.ppermute(merged[rows:], CORE, SWAP)
    attended = in_pair_order(merged[:rows], partner, core, 1)

    task_scales = select_rows(global_scales, patch_tasks)
    part = contract(output_weight, attended, 0, 1).astype(BF).reshape(row_count, width, rows)
    low_part = contract(global_down, attended, 0, 1).astype(BF)
    low_part = jnp.broadcast_to(low_part[None], (row_count, RANK, rows))
    arrived = exchange(jnp.concatenate([part, low_part], axis=1), ROW)
    arrived, riders = lax.optimization_barrier((arrived, riders))
    arrived = arrived.astype(F32).sum(axis=0)

    reduced = jnp.transpose(arrived[width:])
    scaled = (reduced * task_scales).astype(BF)
    mixed = arrived[:width] + jnp.transpose(residual.astype(F32)) + contract(global_up, scaled, 0, 1)
    mixed_b = mixed.astype(BF)
    own_patches = rows // row_count
    own_bytes = own_patches * PATCH
    own_tasks = lax.dynamic_slice_in_dim(patch_tasks, row_index * own_patches, own_patches)
    own_ids = lax.dynamic_slice_in_dim(byte_ids, row_index * own_bytes, own_bytes)
    projected = contract(mixed_b, local_weight, 0, 0).astype(BF)
    projected = exchange(projected.reshape(row_count, own_patches, columns), ROW)
    projected = total(projected).astype(BF)

    rest = lax.ppermute(riders, CORE, SWAP)
    split = (line, columns // (2 * share), 2, 1, share, units)
    riders = in_pair_order(riders.reshape(split), rest.reshape(split), core, 3)
    riders = jnp.moveaxis(riders, 2, 0).reshape(2, line, columns, units)
    rows_in, rows_out = (
        jnp.concatenate([riders[way, k] for k in range(line)], axis=1) for way in range(2)
    )
    lanes = 128
    stacked = jnp.concatenate(
        [rows_in, local_ups, jnp.zeros((lanes - RANK, line * units), BF)], axis=0
    )

    picks = (own_ids[:, None] == jnp.arange(VOCAB, dtype=jnp.int32)[None, :]).astype(BF)
    embedded = jnp.dot(picks, byte_table, preferred_element_type=F32)
    embedded = embedded.reshape(own_patches, PATCH, -1) + position_table.astype(F32)[None]
    inputs = (embedded + projected.astype(F32)[:, None, :]).reshape(own_bytes, columns)
    inverse = lax.rsqrt(jnp.mean(inputs * inputs, axis=1, keepdims=True) + 1e-06)
    normed = (inputs * inverse * norm_gain).astype(BF)
    lowered = jnp.dot(normed, local_down, preferred_element_type=F32)
    byte_tasks = jnp.repeat(own_tasks, PATCH)
    scales = select_rows(local_scales, byte_tasks)
    shrunk = (lowered * scales).astype(BF)
    joined = jnp.concatenate(
        [normed, shrunk, jnp.zeros((own_bytes, lanes - RANK), BF)], axis=1
    )
    joined = jnp.concatenate([joined, lax.ppermute(joined, SIDE, SWAP)], axis=0)
    through = contract(cotangents, rows_out, 1, 0)
    upper = contract(joined, stacked, 1, 0)
    grown = (through * gelu_slope(upper)).astype(BF)
    back = contract(grown, stacked, 1, 1)
    back = back[:own_bytes] + lax.ppermute(back[own_bytes:].astype(BF), SIDE, SWAP).astype(F32)
    ups = contract(joined[:, columns:], grown, 0, 0)[:RANK].astype(BF)
    back_norm = back[:, :columns]
    back_rank = back[:, columns : columns + RANK]
    grad_local_scales = task_totals(byte_tasks, back_rank * lowered)
    moved = (back_rank * scales).astype(BF)
    grad_local_down = contract(moved, normed, 0, 0)
    back_total = back_norm + contract(moved, local_down, 1, 1)
    gained = back_total * norm_gain
    average = jnp.mean(gained * inputs, axis=1, keepdims=True)
    back_inputs = cotangent.astype(F32) + inverse * (
        gained - inputs * inverse * inverse * average
    )
    patch_grad = back_inputs.reshape(own_patches, PATCH, -1).sum(axis=1)
    patch_grad = lax.optimization_barrier(patch_grad).astype(BF)

    spare = jnp.zeros((TASKS, columns - RANK), F32)
    local_rows = jnp.concatenate([grad_local_scales, spare], axis=1)
    local_rows = jnp.concatenate([grad_local_down, local_rows, jnp.zeros_like(local_rows)])
    row_pack = jnp.concatenate([patch_grad, local_rows.astype(BF)], axis=0)
    row_pack = jnp.broadcast_to(row_pack[None], (row_count, *row_pack.shape))
    ups = jnp.stack([ups[:, units * k : units * (k + 1)] for k in range(line)])
    ups = jnp.stack([jnp.where(side == k, ups, jnp.zeros_like(ups)) for k in range(2)], axis=1)
    ups = jnp.pad(ups.reshape(row_count, RANK, units), [(0, 0), (0, 0), (0, columns - units)])
    row_pack = exchange(jnp.concatenate([row_pack, ups], axis=1), ROW)
    patch_grads = row_pack[:, :own_patches].reshape(rows, columns)
    local_sums = total(row_pack[:, own_patches:])
    back_mixed = contract(patch_grads, local_weight, 1, 1).astype(BF)
    back_whole = contract(patch_grads, local_whole, 1, 1).astype(BF)
    back_scaled = contract(back_whole, up_whole, 1, 1)
    grad_global_up = contract(scaled, back_mixed, 0, 0)
    grad_global_scales = task_totals(patch_tasks, back_scaled * reduced)
    back_reduced = (back_scaled * task_scales).astype(BF)
    grad_global_down = contract(back_reduced, attended, 0, 0)

    small = jnp.concatenate([grad_global_scales, jnp.zeros((TASKS, width - RANK), F32)], axis=1)
    small_local = local_sums[RANK : RANK + TASKS, :width]
    packed = jnp.concatenate(
        [
            grad_global_down,
            grad_global_up,
            local_sums[2 * RANK :, :units],
            local_sums[:RANK, :width],
            local_sums[:RANK, width:],
            small,
            small_local,
        ]
    ).astype(BF)
    shape = packed.shape
    pieces = packed.reshape(lax.axis_size(EIGHT), -1, shape[1])
    pieces = exchange(pieces, EIGHT).astype(F32).sum(axis=0)
    pieces = to_everyone(pieces, Z).sum(axis=0)
    packed = to_everyone(pieces, EIGHT).reshape(shape)
    return (
        jnp.transpose(packed[:16]),
        packed[16:32],
        packed[80:88, :RANK],
        jnp.transpose(jnp.concatenate([packed[48:64], packed[64:80]], axis=1)),
        packed[32:48],
        packed[88:96, :RANK],
    )


def solution(mesh):
    torus = Mesh(mesh.devices.reshape(8, 2, 2, 2, 4, 2), SEQ_ROW)
    placed = (
        P(SEQ, ROW),
        P(SEQ, ROW),
        P(SEQ, ROW),
        P(SEQ),
        P(SEQ, ROW),
        P(ROW, None),
        P(ROW, None),
        P(None, ROW),
        P(),
        P(ROW, None),
        P(SEQ),
        P(),
        P(),
        P(),
        P(ROW, SEQ),
        P(ROW, SEQ),
        P(),
        P(None, ROW),
        P(),
        P(SEQ_ROW, None),
    )
    return jax.shard_map(
        body,
        mesh=torus,
        in_specs=placed,
        out_specs=(P(ROW, None), P(None, ROW), P(), P(), P(None, ROW), P()),
        check_vma=False,
    )
```

```python
import math

import jax
import jax.numpy as jnp
from jax import lax
from jax.sharding import Mesh
from jax.sharding import PartitionSpec as P

HEAD = 128
VOCAB = 256
PATCH = 8
TASKS = 8
RANK = 16
ROW = ("row_0", "row_1")
SEQ = ("seq_0", "near", "seq_1", "seq_2")
Z, NEAR, FAR, CORE = SEQ
QUAD = (NEAR, FAR)
EIGHT = (NEAR, FAR, CORE)
LINE, SIDE = ROW
SEQ_ROW = SEQ + ROW
SWAP = [(0, 1), (1, 0)]
BF = jnp.bfloat16
F32 = jnp.float32


def exchange(pieces, axis):
    return lax.all_to_all(pieces, axis, split_axis=0, concat_axis=0, tiled=True)


def to_everyone(array, axis):
    size = lax.axis_size(axis)
    return exchange(jnp.broadcast_to(array[None], (size, *array.shape)), axis)


def contract(left, right, left_dim, right_dim):
    return lax.dot_general(
        left, right, (((left_dim,), (right_dim,)), ((), ())), preferred_element_type=F32
    )


def select_rows(table, tasks):
    picks = (tasks[:, None] == jnp.arange(table.shape[0], dtype=jnp.int32)[None, :]).astype(F32)
    return jnp.dot(picks, table, precision=lax.Precision.HIGHEST)


def task_totals(tasks, values):
    picks = (tasks[:, None] == jnp.arange(TASKS, dtype=jnp.int32)[None, :]).astype(F32)
    return lax.dot_general(picks, values, (((0,), (0,)), ((), ())), precision=lax.Precision.HIGHEST)


def gelu_slope(upper):
    cumulative = 0.5 * (1.0 + lax.erf(upper * 0.7071067811865476))
    density = jnp.exp(-0.5 * upper * upper) * 0.3989422804014327
    return cumulative + upper * density


def in_pair_order(mine, other, place, axis):
    first = jnp.where(place == 0, mine, other)
    second = jnp.where(place == 0, other, mine)
    return jnp.concatenate([first, second], axis=axis)


def total(array):
    return lax.optimization_barrier(array.astype(F32).sum(axis=0))


def fold(array):
    array = jnp.concatenate([array[:, :128], array[:, 128:]], axis=0)
    return jnp.concatenate([array[8 * k : 8 * k + 8] for k in range(4)], axis=1)


def unfold(array):
    array = jnp.concatenate([array[:, :, 128 * k : 128 * k + 128] for k in range(4)], axis=1)
    return jnp.concatenate([array[:, :RANK], array[:, RANK:]], axis=2)


def attend(state, queries, query_places, keys, values, key_places):
    top, mass, out = state
    scores = contract(queries, keys, 1, 1) * (1.0 / math.sqrt(HEAD))
    allowed = key_places[None, :] <= query_places[:, None]
    scores = jnp.where(allowed, scores, -1e30)
    new_top = jnp.maximum(top, jnp.max(scores, axis=1, keepdims=True))
    weights = jnp.where(allowed, jnp.exp(scores - new_top), 0.0)
    shrink = jnp.exp(top - new_top)
    mass = mass * shrink + jnp.sum(weights, axis=1, keepdims=True)
    out = out * shrink + jnp.dot(weights.astype(BF), values, preferred_element_type=F32)
    return (new_top, mass, out)


def body(
    patch_queries,
    patch_keys,
    patch_values,
    patch_tasks,
    residual,
    output_weight,
    global_down,
    global_up,
    global_scales,
    local_weight,
    byte_ids,
    byte_table,
    position_table,
    norm_gain,
    hidden_in,
    hidden_out,
    local_down,
    local_up,
    local_scales,
    cotangent,
):
    rows, width = patch_queries.shape
    ring = lax.axis_size(Z)
    row_count = lax.axis_size(ROW)
    z = lax.axis_index(Z)
    near = lax.axis_index(NEAR)
    far = lax.axis_index(FAR)
    side = lax.axis_index(SIDE)
    core = lax.axis_index(CORE)
    row_index = lax.axis_index(ROW)
    columns = local_weight.shape[1]
    units = hidden_in.shape[0]
    share = hidden_in.shape[1]

    hidden = jnp.concatenate([hidden_in.T, hidden_out.T], axis=0)
    weights = jnp.concatenate([local_weight, fold(global_up), fold(local_up)], axis=0)
    weights = lax.all_gather(weights, ROW, axis=0, tiled=False)
    cotangents = jnp.concatenate([cotangent, lax.ppermute(cotangent, SIDE, SWAP)], axis=0)

    def head(array, which):
        return lax.dynamic_slice_in_dim(array, which * HEAD, HEAD, 1)

    trio = (patch_queries, patch_keys, patch_values)
    mine = jnp.concatenate([head(a, core) for a in trio], axis=1)
    other = jnp.concatenate([head(a, 1 - core) for a in trio], axis=1)
    both = jnp.concatenate([mine, lax.ppermute(other, CORE, SWAP)], axis=0)
    chip_rows = 2 * rows
    packet = both[:, HEAD:]
    quad = to_everyone(both[:, :HEAD], QUAD)
    sides = lax.axis_size(QUAD)
    queries = quad.reshape(sides * chip_rows, HEAD)

    def places(z_index, near_index, far_index):
        start = (z_index * 8 + near_index * 4 + far_index * 2) * rows
        count = jnp.arange(rows, dtype=jnp.int32)
        return jnp.concatenate([start + core * rows + count, start + (1 - core) * rows + count])

    query_places = jnp.concatenate([places(z, k // 2, k % 2) for k in range(sides)])
    count = sides * chip_rows
    state = (
        jnp.full((count, 1), -1e30, F32),
        jnp.zeros((count, 1), F32),
        jnp.zeros((count, HEAD), F32),
    )
    up = [(i, (i + 1) % ring) for i in range(ring)]
    down = [(i, (i - 1) % ring) for i in range(ring)]

    def visit(state, packets, indices):
        keys = jnp.concatenate([p[:, :HEAD] for p in packets])
        values = jnp.concatenate([p[:, HEAD:] for p in packets])
        key_places = jnp.concatenate([places(i, near, far) for i in indices])
        return attend(state, queries, query_places, keys, values, key_places)

    rising = falling = packet
    held, at = [[packet]], [[z]]
    for step in range(1, ring // 2 + 1):
        rising = lax.ppermute(rising, Z, up)
        held.append([rising])
        at.append([(z - step) % ring])
        if step < ring // 2:
            falling = lax.ppermute(falling, Z, down)
            held[-1].append(falling)
            at[-1].append((z + step) % ring)
        if step == 1:
            rising, falling, hidden, queries = lax.optimization_barrier(
                (rising, falling, hidden, queries)
            )
            hidden = to_everyone(hidden, (FAR, LINE, CORE)).reshape(-1, units)
        elif step == 2:
            rising, falling, hidden = lax.optimization_barrier((rising, falling, hidden))
        if step >= 2:
            state = visit(state, held[step - 2], at[step - 2])
    state = visit(state, held[-2], at[-2])
    now, weights, hidden = lax.optimization_barrier((held[-1], weights, hidden))
    state = visit(state, now, at[-1])
    riders = lax.all_gather(hidden, (Z, NEAR), axis=0, tiled=True)

    local_whole = weights[:, :width].reshape(-1, columns)
    up_whole = unfold(weights[:, width : width + 8])
    up_whole = jnp.transpose(up_whole, (1, 0, 2)).reshape(RANK, -1)
    line = lax.axis_size(LINE)
    local_ups = unfold(weights[:, width + 8 :]).reshape(line, 2, RANK, units)
    local_ups = lax.dynamic_index_in_dim(local_ups, side, 1, keepdims=False)
    local_ups = jnp.concatenate([local_ups[k] for k in range(line)], axis=1)

    top, mass, out = state
    level = jnp.where(mass > 0, top + jnp.log(jnp.where(mass > 0, mass, 1.0)), -1e30)
    out = out / jnp.where(mass > 0, mass, 1.0)
    high = lax.reduce_precision(level, 8, 7)
    middle = lax.reduce_precision(level - high, 8, 7)
    low = level - high - middle
    wide = [
        jnp.broadcast_to(a.astype(BF), (count, n))
        for a, n in ((high, 32), (middle, 32), (low, 64))
    ]
    met = jnp.concatenate([out.astype(BF), *wide], axis=1)
    met = exchange(met.reshape(sides, chip_rows, 2 * HEAD), QUAD).astype(F32)
    levels = met[:, :, 128:129] + met[:, :, 160:161] + met[:, :, 192:193]
    parts = jnp.exp(levels - jnp.max(levels, axis=0, keepdims=True))
    merged = (parts * met[:, :, :HEAD]).sum(axis=0) / parts.sum(axis=0)
    merged = merged.astype(BF)
    partner = lax.ppermute(merged[rows:], CORE, SWAP)
    attended = in_pair_order(merged[:rows], partner, core, 1)

    task_scales = select_rows(global_scales, patch_tasks)
    part = contract(output_weight, attended, 0, 1).astype(BF).reshape(row_count, width, rows)
    low_part = contract(global_down, attended, 0, 1).astype(BF)
    low_part = jnp.broadcast_to(low_part[None], (row_count, RANK, rows))
    arrived = exchange(jnp.concatenate([part, low_part], axis=1), ROW)
    arrived = arrived.astype(F32).sum(axis=0)

    reduced = jnp.transpose(arrived[width:])
    scaled = (reduced * task_scales).astype(BF)
    mixed = arrived[:width] + jnp.transpose(residual.astype(F32)) + contract(global_up, scaled, 0, 1)
    mixed_b = mixed.astype(BF)
    own_patches = rows // row_count
    own_bytes = own_patches * PATCH
    own_tasks = lax.dynamic_slice_in_dim(patch_tasks, row_index * own_patches, own_patches)
    own_ids = lax.dynamic_slice_in_dim(byte_ids, row_index * own_bytes, own_bytes)
    projected = contract(mixed_b, local_weight, 0, 0).astype(BF)
    projected = exchange(projected.reshape(row_count, own_patches, columns), ROW)
    projected = total(projected).astype(BF)

    riders = riders.reshape(columns // (2 * share), line, 2, 2, share, units)
    riders = jnp.transpose(riders, (3, 1, 0, 2, 4, 5)).reshape(2, line, columns, units)
    rows_in, rows_out = (
        jnp.concatenate([riders[way, k] for k in range(line)], axis=1) for way in range(2)
    )
    lanes = 128
    stacked = jnp.concatenate(
        [rows_in, local_ups, jnp.zeros((lanes - RANK, line * units), BF)], axis=0
    )

    picks = (own_ids[:, None] == jnp.arange(VOCAB, dtype=jnp.int32)[None, :]).astype(BF)
    embedded = jnp.dot(picks, byte_table, preferred_element_type=F32)
    embedded = embedded.reshape(own_patches, PATCH, -1) + position_table.astype(F32)[None]
    inputs = (embedded + projected.astype(F32)[:, None, :]).reshape(own_bytes, columns)
    inverse = lax.rsqrt(jnp.mean(inputs * inputs, axis=1, keepdims=True) + 1e-06)
    normed = (inputs * inverse * norm_gain).astype(BF)
    lowered = jnp.dot(normed, local_down, preferred_element_type=F32)
    byte_tasks = jnp.repeat(own_tasks, PATCH)
    scales = select_rows(local_scales, byte_tasks)
    shrunk = (lowered * scales).astype(BF)
    joined = jnp.concatenate(
        [normed, shrunk, jnp.zeros((own_bytes, lanes - RANK), BF)], axis=1
    )
    joined = jnp.concatenate([joined, lax.ppermute(joined, SIDE, SWAP)], axis=0)
    through = contract(cotangents, rows_out, 1, 0)
    upper = contract(joined, stacked, 1, 0)
    grown = (through * gelu_slope(upper)).astype(BF)
    back = contract(grown, stacked, 1, 1)
    back = back[:own_bytes] + lax.ppermute(back[own_bytes:].astype(BF), SIDE, SWAP).astype(F32)
    ups = contract(joined[:, columns:], grown, 0, 0)[:RANK].astype(BF)
    back_norm = back[:, :columns]
    back_rank = back[:, columns : columns + RANK]
    grad_local_scales = task_totals(byte_tasks, back_rank * lowered)
    moved = (back_rank * scales).astype(BF)
    grad_local_down = contract(moved, normed, 0, 0)
    back_total = back_norm + contract(moved, local_down, 1, 1)
    gained = back_total * norm_gain
    average = jnp.mean(gained * inputs, axis=1, keepdims=True)
    back_inputs = cotangent.astype(F32) + inverse * (
        gained - inputs * inverse * inverse * average
    )
    patch_grad = back_inputs.reshape(own_patches, PATCH, -1).sum(axis=1)
    patch_grad = lax.optimization_barrier(patch_grad).astype(BF)

    spare = jnp.zeros((TASKS, columns - RANK), F32)
    local_rows = jnp.concatenate([grad_local_scales, spare], axis=1)
    local_rows = jnp.concatenate([grad_local_down, local_rows, jnp.zeros_like(local_rows)])
    row_pack = jnp.concatenate([patch_grad, local_rows.astype(BF)], axis=0)
    row_pack = jnp.broadcast_to(row_pack[None], (row_count, *row_pack.shape))
    ups = jnp.stack([ups[:, units * k : units * (k + 1)] for k in range(line)])
    ups = jnp.stack([jnp.where(side == k, ups, jnp.zeros_like(ups)) for k in range(2)], axis=1)
    ups = jnp.pad(ups.reshape(row_count, RANK, units), [(0, 0), (0, 0), (0, columns - units)])
    row_pack = exchange(jnp.concatenate([row_pack, ups], axis=1), ROW)
    patch_grads = row_pack[:, :own_patches].reshape(rows, columns)
    local_sums = total(row_pack[:, own_patches:])
    back_mixed = contract(patch_grads, local_weight, 1, 1).astype(BF)
    back_whole = contract(patch_grads, local_whole, 1, 1).astype(BF)
    back_scaled = contract(back_whole, up_whole, 1, 1)
    grad_global_up = contract(scaled, back_mixed, 0, 0)
    grad_global_scales = task_totals(patch_tasks, back_scaled * reduced)
    back_reduced = (back_scaled * task_scales).astype(BF)
    grad_global_down = contract(back_reduced, attended, 0, 0)

    small = jnp.concatenate([grad_global_scales, jnp.zeros((TASKS, width - RANK), F32)], axis=1)
    small_local = local_sums[RANK : RANK + TASKS, :width]
    packed = jnp.concatenate(
        [
            grad_global_down,
            grad_global_up,
            local_sums[2 * RANK :, :units],
            local_sums[:RANK, :width],
            local_sums[:RANK, width:],
            small,
            small_local,
        ]
    ).astype(BF)
    shape = packed.shape
    pieces = packed.reshape(lax.axis_size(EIGHT), -1, shape[1])
    pieces = total(exchange(pieces, EIGHT)).astype(BF)
    pieces = total(to_everyone(pieces, Z)).astype(BF)
    packed = to_everyone(pieces, EIGHT).reshape(shape).astype(F32)
    return (
        jnp.transpose(packed[:16]),
        packed[16:32],
        packed[80:88, :RANK],
        jnp.transpose(jnp.concatenate([packed[48:64], packed[64:80]], axis=1)),
        packed[32:48],
        packed[88:96, :RANK],
    )


def solution(mesh):
    torus = Mesh(mesh.devices.reshape(8, 2, 2, 2, 4, 2), SEQ_ROW)
    placed = (
        P(SEQ, ROW),
        P(SEQ, ROW),
        P(SEQ, ROW),
        P(SEQ),
        P(SEQ, ROW),
        P(ROW, None),
        P(ROW, None),
        P(None, ROW),
        P(),
        P(ROW, None),
        P(SEQ),
        P(),
        P(),
        P(),
        P(ROW, SEQ),
        P(ROW, SEQ),
        P(),
        P(None, ROW),
        P(),
        P(SEQ_ROW, None),
    )
    return jax.shard_map(
        body,
        mesh=torus,
        in_specs=placed,
        out_specs=(P(ROW, None), P(None, ROW), P(), P(), P(None, ROW), P()),
        check_vma=False,
    )
```

```python
import functools
import math

import jax
import jax.numpy as jnp
from jax import lax
from jax.experimental import pallas as pl
from jax.experimental.pallas import tpu as pltpu
from jax.sharding import Mesh
from jax.sharding import PartitionSpec as P

HEAD = 128
VOCAB = 256
PATCH = 8
TASKS = 8
RANK = 16
ROW = ("row_0", "row_1")
SEQ = ("seq_0", "near", "seq_1", "seq_2")
Z, NEAR, FAR, CORE = SEQ
QUAD = (NEAR, FAR)
EIGHT = (NEAR, FAR, CORE)
LINE, SIDE = ROW
SEQ_ROW = SEQ + ROW
SWAP = [(0, 1), (1, 0)]
BF = jnp.bfloat16
F32 = jnp.float32


def exchange(pieces, axis):
    return lax.all_to_all(pieces, axis, split_axis=0, concat_axis=0, tiled=True)


def to_everyone(array, axis):
    size = lax.axis_size(axis)
    return exchange(jnp.broadcast_to(array[None], (size, *array.shape)), axis)


def contract(left, right, left_dim, right_dim):
    return lax.dot_general(
        left, right, (((left_dim,), (right_dim,)), ((), ())), preferred_element_type=F32
    )


def select_rows(table, tasks):
    picks = (tasks[:, None] == jnp.arange(table.shape[0], dtype=jnp.int32)[None, :]).astype(F32)
    return jnp.dot(picks, table, precision=lax.Precision.HIGHEST)


def task_totals(tasks, values):
    picks = (tasks[:, None] == jnp.arange(TASKS, dtype=jnp.int32)[None, :]).astype(F32)
    return lax.dot_general(picks, values, (((0,), (0,)), ((), ())), precision=lax.Precision.HIGHEST)


def gelu_slope(upper):
    cumulative = 0.5 * (1.0 + lax.erf(upper * 0.7071067811865476))
    density = jnp.exp(-0.5 * upper * upper) * 0.3989422804014327
    return cumulative + upper * density


def in_pair_order(mine, other, place, axis):
    first = jnp.where(place == 0, mine, other)
    second = jnp.where(place == 0, other, mine)
    return jnp.concatenate([first, second], axis=axis)


def total(array):
    return lax.optimization_barrier(array.astype(F32).sum(axis=0))


def fold(array):
    array = jnp.concatenate([array[:, :128], array[:, 128:]], axis=0)
    return jnp.concatenate([array[8 * k : 8 * k + 8] for k in range(4)], axis=1)


def unfold(array):
    array = jnp.concatenate([array[:, :, 128 * k : 128 * k + 128] for k in range(4)], axis=1)
    return jnp.concatenate([array[:, :RANK], array[:, RANK:]], axis=2)


def attend_kernel(spots, queries, *refs, count, start, finish):
    packets, refs = refs[:count], refs[count:]
    rows = queries.shape[0]
    half = rows // 2
    if start:
        top = jnp.full((rows, 1), -1e20, F32)
        mass = jnp.zeros((rows, HEAD), F32)
        out = jnp.zeros((rows, HEAD), F32)
    else:
        top, mass, out = refs[0][:, :1], refs[1][...], refs[2][...]
        refs = refs[3:]
    core = spots[0]

    def inside(shape, dim):
        at = lax.broadcasted_iota(jnp.int32, shape, dim)
        return jnp.where(at < half, at + core * half, at - core * half)

    query_places = (spots[1] + pl.program_id(0)) * rows + inside((rows, 1), 0)
    own = queries[...]
    for index in range(count):
        keys = packets[index][:, :HEAD]
        values = packets[index][:, HEAD:]
        key_places = spots[2 + index] * rows + inside((1, rows), 1)
        scores = contract(own, keys, 1, 1) * (1.0 / math.sqrt(HEAD))
        scores = jnp.where(key_places <= query_places, scores, -1e30)
        new_top = jnp.maximum(top, jnp.max(scores, axis=1, keepdims=True))
        weights = jnp.exp(scores - new_top)
        shrink = jnp.exp(top - new_top)
        mass = mass * shrink + (weights[:, :HEAD] + weights[:, HEAD:])
        out = out * shrink + jnp.dot(weights.astype(BF), values, preferred_element_type=F32)
        top = new_top
    if not finish:
        refs[0][...] = jnp.broadcast_to(top, (rows, HEAD))
        refs[1][...] = mass
        refs[2][...] = out
        return
    mass = jnp.sum(mass, axis=1, keepdims=True)
    safe = jnp.where(mass > 0, mass, 1.0)
    level = jnp.where(mass > 0, top + jnp.log(safe), -1e30)
    level = jnp.broadcast_to(level, (rows, HEAD))
    high = level.astype(BF).astype(F32)
    middle = (level - high).astype(BF).astype(F32)
    low = level - high - middle
    lane = lax.broadcasted_iota(jnp.int32, (rows, HEAD), 1)
    level = jnp.where(lane < 32, high, jnp.where(lane < 64, middle, low))
    refs[0][:, :HEAD] = (out / safe).astype(BF)
    refs[0][:, HEAD:] = level.astype(BF)


def attend(spots, queries, packets, state, finish):
    total_rows = queries.shape[0]
    rows = packets[0].shape[0]
    block = pl.BlockSpec((rows, HEAD), lambda k: (k, 0))
    whole = pl.BlockSpec(packets[0].shape, lambda k: (0, 0))
    start = state is None
    state = () if start else state
    if finish:
        shapes = jax.ShapeDtypeStruct((total_rows, 2 * HEAD), BF)
        outs = pl.BlockSpec((rows, 2 * HEAD), lambda k: (k, 0))
    else:
        shapes = (jax.ShapeDtypeStruct((total_rows, HEAD), F32),) * 3
        outs = (block,) * 3
    return pl.pallas_call(
        functools.partial(attend_kernel, count=len(packets), start=start, finish=finish),
        grid=(total_rows // rows,),
        in_specs=[pl.BlockSpec(memory_space=pltpu.SMEM), block]
        + [whole] * len(packets)
        + [block] * len(state),
        out_specs=outs,
        out_shape=shapes,
        name="attend",
    )(spots, queries, *packets, *state)


def body(
    patch_queries,
    patch_keys,
    patch_values,
    patch_tasks,
    residual,
    output_weight,
    global_down,
    global_up,
    global_scales,
    local_weight,
    byte_ids,
    byte_table,
    position_table,
    norm_gain,
    hidden_in,
    hidden_out,
    local_down,
    local_up,
    local_scales,
    cotangent,
):
    rows, width = patch_queries.shape
    ring = lax.axis_size(Z)
    row_count = lax.axis_size(ROW)
    z = lax.axis_index(Z)
    near = lax.axis_index(NEAR)
    far = lax.axis_index(FAR)
    side = lax.axis_index(SIDE)
    line = lax.axis_size(LINE)
    core = lax.axis_index(CORE)
    row_index = lax.axis_index(ROW)
    columns = local_weight.shape[1]
    units = hidden_in.shape[0]
    share = hidden_in.shape[1]

    hidden = jnp.concatenate([hidden_in.T, hidden_out.T], axis=0)
    weights = jnp.concatenate([local_weight, fold(global_up), fold(local_up)], axis=0)
    weights = lax.all_gather(weights, ROW, axis=0, tiled=False)
    cotangents = jnp.concatenate([cotangent, lax.ppermute(cotangent, SIDE, SWAP)], axis=0)

    def head(array, which):
        return lax.dynamic_slice_in_dim(array, which * HEAD, HEAD, 1)

    trio = (patch_queries, patch_keys, patch_values)
    mine = jnp.concatenate([head(a, core) for a in trio], axis=1)
    other = jnp.concatenate([head(a, 1 - core) for a in trio], axis=1)
    both = jnp.concatenate([mine, lax.ppermute(other, CORE, SWAP)], axis=0)
    chip_rows = 2 * rows
    packet = both[:, HEAD:]
    quad = to_everyone(both[:, :HEAD], QUAD)
    sides = lax.axis_size(QUAD)
    queries = quad.reshape(sides * chip_rows, HEAD)

    up = [(i, (i + 1) % ring) for i in range(ring)]
    down = [(i, (i - 1) % ring) for i in range(ring)]

    rising = falling = packet
    held, at = [packet], [z]
    for step in range(1, ring // 2 + 1):
        rising = lax.ppermute(rising, Z, up)
        held.append(rising)
        at.append((z - step) % ring)
        if step < ring // 2:
            falling = lax.ppermute(falling, Z, down)
            held.append(falling)
            at.append((z + step) % ring)
        if step == 1:
            rising, falling, hidden, queries = lax.optimization_barrier(
                (rising, falling, hidden, queries)
            )
            hidden = to_everyone(hidden, (FAR, LINE, CORE))
            hidden = hidden.reshape(2, line, 2, 2, share, units)
            hidden = jnp.transpose(hidden, (1, 3, 0, 2, 4, 5)).reshape(-1, units)
        elif step == 2:
            rising, falling, hidden = lax.optimization_barrier((rising, falling, hidden))
    spots = jnp.stack([z * sides] + [k * sides + near * 2 + far for k in at]).astype(jnp.int32)
    spots = jnp.concatenate([core.astype(jnp.int32)[None], spots])
    state = attend(spots, queries, held[:-1], None, False)
    last, weights, hidden = lax.optimization_barrier((held[-1], weights, hidden))
    met = attend(jnp.concatenate([spots[:2], spots[-1:]]), queries, [last], state, True)
    riders = lax.all_gather(hidden, (Z, NEAR), axis=0, tiled=True)

    local_whole = weights[:, :width].reshape(-1, columns)
    up_whole = unfold(weights[:, width : width + 8])
    up_whole = jnp.transpose(up_whole, (1, 0, 2)).reshape(RANK, -1)
    local_ups = unfold(weights[:, width + 8 :]).reshape(line, 2, RANK, units)
    local_ups = lax.dynamic_index_in_dim(local_ups, side, 1, keepdims=False)
    local_ups = jnp.concatenate([local_ups[k] for k in range(line)], axis=1)

    met = exchange(met.reshape(sides, chip_rows, 2 * HEAD), QUAD).astype(F32)
    levels = met[:, :, 128:129] + met[:, :, 160:161] + met[:, :, 192:193]
    parts = jnp.exp(levels - jnp.max(levels, axis=0, keepdims=True))
    merged = (parts * met[:, :, :HEAD]).sum(axis=0) / parts.sum(axis=0)
    merged = merged.astype(BF)
    partner = lax.ppermute(merged[rows:], CORE, SWAP)
    attended = in_pair_order(merged[:rows], partner, core, 1)

    task_scales = select_rows(global_scales, patch_tasks)
    part = contract(output_weight, attended, 0, 1).astype(BF).reshape(row_count, width, rows)
    low_part = contract(global_down, attended, 0, 1).astype(BF)
    low_part = jnp.broadcast_to(low_part[None], (row_count, RANK, rows))
    arrived = exchange(jnp.concatenate([part, low_part], axis=1), ROW)
    arrived = arrived.astype(F32).sum(axis=0)

    reduced = jnp.transpose(arrived[width:])
    scaled = (reduced * task_scales).astype(BF)
    mixed = arrived[:width] + jnp.transpose(residual.astype(F32)) + contract(global_up, scaled, 0, 1)
    mixed_b = mixed.astype(BF)
    own_patches = rows // row_count
    own_bytes = own_patches * PATCH
    own_tasks = lax.dynamic_slice_in_dim(patch_tasks, row_index * own_patches, own_patches)
    own_ids = lax.dynamic_slice_in_dim(byte_ids, row_index * own_bytes, own_bytes)
    projected = contract(mixed_b, local_weight, 0, 0).astype(BF)
    projected = exchange(projected.reshape(row_count, own_patches, columns), ROW)
    projected = total(projected).astype(BF)

    riders = riders.reshape(-1, line, 2, 4 * share, units)
    riders = jnp.transpose(riders, (2, 1, 0, 3, 4)).reshape(2, line, columns, units)
    rows_in, rows_out = (
        jnp.concatenate([riders[way, k] for k in range(line)], axis=1) for way in range(2)
    )
    lanes = 128
    stacked = jnp.concatenate(
        [rows_in, local_ups, jnp.zeros((lanes - RANK, line * units), BF)], axis=0
    )

    picks = (own_ids[:, None] == jnp.arange(VOCAB, dtype=jnp.int32)[None, :]).astype(BF)
    embedded = jnp.dot(picks, byte_table, preferred_element_type=F32)
    embedded = embedded.reshape(own_patches, PATCH, -1) + position_table.astype(F32)[None]
    inputs = (embedded + projected.astype(F32)[:, None, :]).reshape(own_bytes, columns)
    inverse = lax.rsqrt(jnp.mean(inputs * inputs, axis=1, keepdims=True) + 1e-06)
    normed = (inputs * inverse * norm_gain).astype(BF)
    lowered = jnp.dot(normed, local_down, preferred_element_type=F32)
    byte_tasks = jnp.repeat(own_tasks, PATCH)
    scales = select_rows(local_scales, byte_tasks)
    shrunk = (lowered * scales).astype(BF)
    joined = jnp.concatenate(
        [normed, shrunk, jnp.zeros((own_bytes, lanes - RANK), BF)], axis=1
    )
    joined = jnp.concatenate([joined, lax.ppermute(joined, SIDE, SWAP)], axis=0)
    through = contract(cotangents, rows_out, 1, 0)
    upper = contract(joined, stacked, 1, 0)
    grown = (through * gelu_slope(upper)).astype(BF)
    back = contract(grown, stacked, 1, 1)
    back = back[:own_bytes] + lax.ppermute(back[own_bytes:].astype(BF), SIDE, SWAP).astype(F32)
    ups = contract(joined[:, columns:], grown, 0, 0)[:RANK].astype(BF)
    back_norm = back[:, :columns]
    back_rank = back[:, columns : columns + RANK]
    grad_local_scales = task_totals(byte_tasks, back_rank * lowered)
    moved = (back_rank * scales).astype(BF)
    grad_local_down = contract(moved, normed, 0, 0)
    back_total = back_norm + contract(moved, local_down, 1, 1)
    gained = back_total * norm_gain
    average = jnp.mean(gained * inputs, axis=1, keepdims=True)
    back_inputs = cotangent.astype(F32) + inverse * (
        gained - inputs * inverse * inverse * average
    )
    patch_grad = back_inputs.reshape(own_patches, PATCH, -1).sum(axis=1)
    patch_grad = lax.optimization_barrier(patch_grad).astype(BF)

    spare = jnp.zeros((TASKS, columns - RANK), F32)
    local_rows = jnp.concatenate([grad_local_scales, spare], axis=1)
    local_rows = jnp.concatenate([grad_local_down, local_rows, jnp.zeros_like(local_rows)])
    row_pack = jnp.concatenate([patch_grad, local_rows.astype(BF)], axis=0)
    row_pack = jnp.broadcast_to(row_pack[None], (row_count, *row_pack.shape))
    ups = jnp.stack([ups[:, units * k : units * (k + 1)] for k in range(line)])
    ups = jnp.stack([jnp.where(side == k, ups, jnp.zeros_like(ups)) for k in range(2)], axis=1)
    ups = jnp.pad(ups.reshape(row_count, RANK, units), [(0, 0), (0, 0), (0, columns - units)])
    row_pack = exchange(jnp.concatenate([row_pack, ups], axis=1), ROW)
    patch_grads = row_pack[:, :own_patches].reshape(rows, columns)
    local_sums = total(row_pack[:, own_patches:])
    back_mixed = contract(patch_grads, local_weight, 1, 1).astype(BF)
    back_whole = contract(patch_grads, local_whole, 1, 1).astype(BF)
    back_scaled = contract(back_whole, up_whole, 1, 1)
    grad_global_up = contract(scaled, back_mixed, 0, 0)
    grad_global_scales = task_totals(patch_tasks, back_scaled * reduced)
    back_reduced = (back_scaled * task_scales).astype(BF)
    grad_global_down = contract(back_reduced, attended, 0, 0)

    small = jnp.concatenate([grad_global_scales, jnp.zeros((TASKS, width - RANK), F32)], axis=1)
    small_local = local_sums[RANK : RANK + TASKS, :width]
    packed = jnp.concatenate(
        [
            grad_global_down,
            grad_global_up,
            local_sums[2 * RANK :, :units],
            local_sums[:RANK, :width],
            local_sums[:RANK, width:],
            small,
            small_local,
        ]
    ).astype(BF)
    shape = packed.shape
    pieces = packed.reshape(lax.axis_size(EIGHT), -1, shape[1])
    pieces = total(exchange(pieces, EIGHT)).astype(BF)
    pieces = total(to_everyone(pieces, Z)).astype(BF)
    packed = to_everyone(pieces, EIGHT).reshape(shape).astype(F32)
    return (
        jnp.transpose(packed[:16]),
        packed[16:32],
        packed[80:88, :RANK],
        jnp.transpose(jnp.concatenate([packed[48:64], packed[64:80]], axis=1)),
        packed[32:48],
        packed[88:96, :RANK],
    )


def solution(mesh):
    torus = Mesh(mesh.devices.reshape(8, 2, 2, 2, 4, 2), SEQ_ROW)
    placed = (
        P(SEQ, ROW),
        P(SEQ, ROW),
        P(SEQ, ROW),
        P(SEQ),
        P(SEQ, ROW),
        P(ROW, None),
        P(ROW, None),
        P(None, ROW),
        P(),
        P(ROW, None),
        P(SEQ),
        P(),
        P(),
        P(),
        P(ROW, SEQ),
        P(ROW, SEQ),
        P(),
        P(None, ROW),
        P(),
        P(SEQ_ROW, None),
    )
    return jax.shard_map(
        body,
        mesh=torus,
        in_specs=placed,
        out_specs=(P(ROW, None), P(None, ROW), P(), P(), P(None, ROW), P()),
        check_vma=False,
    )
```

```python
import functools
import math

import jax
import jax.numpy as jnp
from jax import lax
from jax.experimental import pallas as pl
from jax.experimental.pallas import tpu as pltpu
from jax.sharding import Mesh
from jax.sharding import PartitionSpec as P

HEAD = 128
VOCAB = 256
PATCH = 8
TASKS = 8
RANK = 16
ROW = ("row_0", "row_1")
SEQ = ("seq_0", "near", "seq_1", "seq_2")
Z, NEAR, FAR, CORE = SEQ
QUAD = (NEAR, FAR)
EIGHT = (NEAR, FAR, CORE)
LINE, SIDE = ROW
SEQ_ROW = SEQ + ROW
SWAP = [(0, 1), (1, 0)]
BF = jnp.bfloat16
F32 = jnp.float32


def exchange(pieces, axis):
    return lax.all_to_all(pieces, axis, split_axis=0, concat_axis=0, tiled=True)


def to_everyone(array, axis):
    size = lax.axis_size(axis)
    return exchange(jnp.broadcast_to(array[None], (size, *array.shape)), axis)


def contract(left, right, left_dim, right_dim):
    return lax.dot_general(
        left, right, (((left_dim,), (right_dim,)), ((), ())), preferred_element_type=F32
    )


def select_rows(table, tasks):
    picks = (tasks[:, None] == jnp.arange(table.shape[0], dtype=jnp.int32)[None, :]).astype(F32)
    return jnp.dot(picks, table, precision=lax.Precision.HIGHEST)


def task_totals(tasks, values):
    picks = (tasks[:, None] == jnp.arange(TASKS, dtype=jnp.int32)[None, :]).astype(F32)
    return lax.dot_general(picks, values, (((0,), (0,)), ((), ())), precision=lax.Precision.HIGHEST)


def gelu_slope(upper):
    cumulative = 0.5 * (1.0 + lax.erf(upper * 0.7071067811865476))
    density = jnp.exp(-0.5 * upper * upper) * 0.3989422804014327
    return cumulative + upper * density


def in_pair_order(mine, other, place, axis):
    first = jnp.where(place == 0, mine, other)
    second = jnp.where(place == 0, other, mine)
    return jnp.concatenate([first, second], axis=axis)


def total(array):
    return lax.optimization_barrier(array.astype(F32).sum(axis=0))


def fold(array):
    array = jnp.concatenate([array[:, :128], array[:, 128:]], axis=0)
    return jnp.concatenate([array[8 * k : 8 * k + 8] for k in range(4)], axis=1)


def unfold(array):
    array = jnp.concatenate([array[:, :, 128 * k : 128 * k + 128] for k in range(4)], axis=1)
    return jnp.concatenate([array[:, :RANK], array[:, RANK:]], axis=2)


def attend_kernel(spots, queries, *refs, count, start, finish):
    packets, refs = refs[:count], refs[count:]
    rows = queries.shape[0]
    half = rows // 2
    if start:
        top = jnp.full((rows, 1), -1e20, F32)
        mass = jnp.zeros((rows, HEAD), F32)
        out = jnp.zeros((rows, HEAD), F32)
    else:
        top, mass, out = refs[0][:, :1], refs[1][...], refs[2][...]
        refs = refs[3:]
    core = spots[0]

    def inside(shape, dim):
        at = lax.broadcasted_iota(jnp.int32, shape, dim)
        return jnp.where(at < half, at + core * half, at - core * half)

    query_places = (spots[1] + pl.program_id(0)) * rows + inside((rows, 1), 0)
    own = queries[...]
    for index in range(count):
        keys = packets[index][:, :HEAD]
        values = packets[index][:, HEAD:]
        key_places = spots[2 + index] * rows + inside((1, rows), 1)
        scores = contract(own, keys, 1, 1) * (1.0 / math.sqrt(HEAD))
        scores = jnp.where(key_places <= query_places, scores, -1e30)
        new_top = jnp.maximum(top, jnp.max(scores, axis=1, keepdims=True))
        weights = jnp.exp(scores - new_top)
        shrink = jnp.exp(top - new_top)
        mass = mass * shrink + (weights[:, :HEAD] + weights[:, HEAD:])
        out = out * shrink + jnp.dot(weights.astype(BF), values, preferred_element_type=F32)
        top = new_top
    if not finish:
        refs[0][...] = jnp.broadcast_to(top, (rows, HEAD))
        refs[1][...] = mass
        refs[2][...] = out
        return
    mass = jnp.sum(mass, axis=1, keepdims=True)
    safe = jnp.where(mass > 0, mass, 1.0)
    level = jnp.where(mass > 0, top + jnp.log(safe), -1e30)
    level = jnp.broadcast_to(level, (rows, HEAD))
    high = level.astype(BF).astype(F32)
    middle = (level - high).astype(BF).astype(F32)
    low = level - high - middle
    lane = lax.broadcasted_iota(jnp.int32, (rows, HEAD), 1)
    level = jnp.where(lane < 32, high, jnp.where(lane < 64, middle, low))
    refs[0][:, :HEAD] = (out / safe).astype(BF)
    refs[0][:, HEAD:] = level.astype(BF)


def attend(spots, queries, packets, state, finish):
    total_rows = queries.shape[0]
    rows = packets[0].shape[0]
    block = pl.BlockSpec((rows, HEAD), lambda k: (k, 0))
    whole = pl.BlockSpec(packets[0].shape, lambda k: (0, 0))
    start = state is None
    state = () if start else state
    if finish:
        shapes = jax.ShapeDtypeStruct((total_rows // rows, rows, 2 * HEAD), BF)
        outs = pl.BlockSpec((None, rows, 2 * HEAD), lambda k: (k, 0, 0))
    else:
        shapes = (jax.ShapeDtypeStruct((total_rows, HEAD), F32),) * 3
        outs = (block,) * 3
    return pl.pallas_call(
        functools.partial(attend_kernel, count=len(packets), start=start, finish=finish),
        grid=(total_rows // rows,),
        in_specs=[pl.BlockSpec(memory_space=pltpu.SMEM), block]
        + [whole] * len(packets)
        + [block] * len(state),
        out_specs=outs,
        out_shape=shapes,
        name="attend",
    )(spots, queries, *packets, *state)


def body(
    patch_queries,
    patch_keys,
    patch_values,
    patch_tasks,
    residual,
    output_weight,
    global_down,
    global_up,
    global_scales,
    local_weight,
    byte_ids,
    byte_table,
    position_table,
    norm_gain,
    hidden_in,
    hidden_out,
    local_down,
    local_up,
    local_scales,
    cotangent,
):
    rows, width = patch_queries.shape
    ring = lax.axis_size(Z)
    row_count = lax.axis_size(ROW)
    z = lax.axis_index(Z)
    near = lax.axis_index(NEAR)
    far = lax.axis_index(FAR)
    side = lax.axis_index(SIDE)
    line = lax.axis_size(LINE)
    core = lax.axis_index(CORE)
    row_index = lax.axis_index(ROW)
    columns = local_weight.shape[1]
    units = hidden_in.shape[0]
    share = hidden_in.shape[1]

    hidden = jnp.concatenate([hidden_in.T, hidden_out.T], axis=0)
    weights = jnp.concatenate([local_weight, fold(global_up), fold(local_up)], axis=0)
    weights = lax.all_gather(weights, ROW, axis=0, tiled=False)
    cotangents = jnp.concatenate([cotangent, lax.ppermute(cotangent, SIDE, SWAP)], axis=0)

    def head(array, which):
        return lax.dynamic_slice_in_dim(array, which * HEAD, HEAD, 1)

    trio = (patch_queries, patch_keys, patch_values)
    mine = jnp.concatenate([head(a, core) for a in trio], axis=1)
    other = jnp.concatenate([head(a, 1 - core) for a in trio], axis=1)
    both = jnp.concatenate([mine, lax.ppermute(other, CORE, SWAP)], axis=0)
    chip_rows = 2 * rows
    packet = both[:, HEAD:]
    quad = to_everyone(both[:, :HEAD], QUAD)
    sides = lax.axis_size(QUAD)
    queries = quad.reshape(sides * chip_rows, HEAD)

    up = [(i, (i + 1) % ring) for i in range(ring)]
    down = [(i, (i - 1) % ring) for i in range(ring)]

    rising = falling = packet
    held, at = [packet], [z]
    for step in range(1, ring // 2 + 1):
        rising = lax.ppermute(rising, Z, up)
        held.append(rising)
        at.append((z - step) % ring)
        if step < ring // 2:
            falling = lax.ppermute(falling, Z, down)
            held.append(falling)
            at.append((z + step) % ring)
        if step == 1:
            rising, falling, hidden, queries = lax.optimization_barrier(
                (rising, falling, hidden, queries)
            )
            hidden = to_everyone(hidden, (NEAR, FAR, LINE))
            hidden = hidden.reshape(sides, line, 2, share, units)
            hidden = jnp.transpose(hidden, (1, 2, 0, 3, 4)).reshape(-1, units)
        elif step == 2:
            rising, falling, hidden = lax.optimization_barrier((rising, falling, hidden))
    spots = jnp.stack([z * sides] + [k * sides + near * 2 + far for k in at]).astype(jnp.int32)
    spots = jnp.concatenate([core.astype(jnp.int32)[None], spots])
    state = attend(spots, queries, held[:-1], None, False)
    last, weights, hidden = lax.optimization_barrier((held[-1], weights, hidden))
    met = attend(jnp.concatenate([spots[:2], spots[-1:]]), queries, [last], state, True)
    riders = lax.all_gather(hidden, Z, axis=0, tiled=True)

    local_whole = weights[:, :width].reshape(-1, columns)
    up_whole = unfold(weights[:, width : width + 8])
    up_whole = jnp.transpose(up_whole, (1, 0, 2)).reshape(RANK, -1)
    local_ups = unfold(weights[:, width + 8 :]).reshape(line, 2, RANK, units)
    local_ups = lax.dynamic_index_in_dim(local_ups, side, 1, keepdims=False)

    met = exchange(met, QUAD).astype(F32)
    levels = met[:, :, 128:129] + met[:, :, 160:161] + met[:, :, 192:193]
    parts = jnp.exp(levels - jnp.max(levels, axis=0, keepdims=True))
    merged = (parts * met[:, :, :HEAD]).sum(axis=0) / parts.sum(axis=0)
    merged = merged.astype(BF)
    partner = lax.ppermute(merged[rows:], CORE, SWAP)
    attended = in_pair_order(merged[:rows], partner, core, 1)

    task_scales = select_rows(global_scales, patch_tasks)
    part = contract(output_weight, attended, 0, 1).astype(BF).reshape(row_count, width, rows)
    low_part = contract(global_down, attended, 0, 1).astype(BF)
    low_part = jnp.broadcast_to(low_part[None], (row_count, RANK, rows))
    arrived = exchange(jnp.concatenate([part, low_part], axis=1), ROW)
    arrived = arrived.astype(F32).sum(axis=0)

    reduced = jnp.transpose(arrived[width:])
    scaled = (reduced * task_scales).astype(BF)
    mixed = arrived[:width] + jnp.transpose(residual.astype(F32)) + contract(global_up, scaled, 0, 1)
    mixed_b = mixed.astype(BF)
    own_patches = rows // row_count
    own_bytes = own_patches * PATCH
    own_tasks = lax.dynamic_slice_in_dim(patch_tasks, row_index * own_patches, own_patches)
    own_ids = lax.dynamic_slice_in_dim(byte_ids, row_index * own_bytes, own_bytes)
    projected = contract(mixed_b, local_weight, 0, 0).astype(BF)
    projected = exchange(projected.reshape(row_count, own_patches, columns), ROW)
    projected, riders = lax.optimization_barrier((projected, riders))
    projected = total(projected).astype(BF)

    rest = lax.ppermute(riders, CORE, SWAP)
    split = (ring, line, 2, sides, 1, share, units)
    riders = in_pair_order(riders.reshape(split), rest.reshape(split), core, 4)
    riders = jnp.transpose(riders, (2, 1, 0, 3, 4, 5, 6)).reshape(2, line, columns, units)
    rows_in, rows_out = riders[0], riders[1]
    lanes = 128
    spare_rows = jnp.zeros((line, lanes - RANK, units), BF)
    stacked = jnp.concatenate([rows_in, local_ups, spare_rows], axis=1)

    picks = (own_ids[:, None] == jnp.arange(VOCAB, dtype=jnp.int32)[None, :]).astype(BF)
    embedded = jnp.dot(picks, byte_table, preferred_element_type=F32)
    embedded = embedded.reshape(own_patches, PATCH, -1) + position_table.astype(F32)[None]
    inputs = (embedded + projected.astype(F32)[:, None, :]).reshape(own_bytes, columns)
    inverse = lax.rsqrt(jnp.mean(inputs * inputs, axis=1, keepdims=True) + 1e-06)
    normed = (inputs * inverse * norm_gain).astype(BF)
    lowered = jnp.dot(normed, local_down, preferred_element_type=F32)
    byte_tasks = jnp.repeat(own_tasks, PATCH)
    scales = select_rows(local_scales, byte_tasks)
    shrunk = (lowered * scales).astype(BF)
    joined = jnp.concatenate(
        [normed, shrunk, jnp.zeros((own_bytes, lanes - RANK), BF)], axis=1
    )
    joined = jnp.concatenate([joined, lax.ppermute(joined, SIDE, SWAP)], axis=0)
    through = contract(cotangents, rows_out, 1, 1)
    upper = contract(joined, stacked, 1, 1)
    grown = (through * gelu_slope(upper)).astype(BF)
    back = lax.dot_general(
        grown, stacked, (((1, 2), (0, 2)), ((), ())), preferred_element_type=F32
    )
    back = back[:own_bytes] + lax.ppermute(back[own_bytes:].astype(BF), SIDE, SWAP).astype(F32)
    ups = contract(joined[:, columns:], grown, 0, 0)[:RANK].astype(BF)
    back_norm = back[:, :columns]
    back_rank = back[:, columns : columns + RANK]
    grad_local_scales = task_totals(byte_tasks, back_rank * lowered)
    moved = (back_rank * scales).astype(BF)
    grad_local_down = contract(moved, normed, 0, 0)
    back_total = back_norm + contract(moved, local_down, 1, 1)
    gained = back_total * norm_gain
    average = jnp.mean(gained * inputs, axis=1, keepdims=True)
    back_inputs = cotangent.astype(F32) + inverse * (
        gained - inputs * inverse * inverse * average
    )
    patch_grad = back_inputs.reshape(own_patches, PATCH, -1).sum(axis=1)
    patch_grad = lax.optimization_barrier(patch_grad).astype(BF)

    spare = jnp.zeros((TASKS, columns - RANK), F32)
    local_rows = jnp.concatenate([grad_local_scales, spare], axis=1)
    local_rows = jnp.concatenate([grad_local_down, local_rows, jnp.zeros_like(local_rows)])
    row_pack = jnp.concatenate([patch_grad, local_rows.astype(BF)], axis=0)
    row_pack = jnp.broadcast_to(row_pack[None], (row_count, *row_pack.shape))
    ups = jnp.transpose(ups, (1, 0, 2))
    ups = jnp.stack([jnp.where(side == k, ups, jnp.zeros_like(ups)) for k in range(2)], axis=1)
    ups = jnp.pad(ups.reshape(row_count, RANK, units), [(0, 0), (0, 0), (0, columns - units)])
    row_pack = exchange(jnp.concatenate([row_pack, ups], axis=1), ROW)
    patch_grads = row_pack[:, :own_patches].reshape(rows, columns)
    local_sums = total(row_pack[:, own_patches:])
    back_mixed = contract(patch_grads, local_weight, 1, 1).astype(BF)
    back_whole = contract(patch_grads, local_whole, 1, 1).astype(BF)
    back_scaled = contract(back_whole, up_whole, 1, 1)
    grad_global_up = contract(scaled, back_mixed, 0, 0)
    grad_global_scales = task_totals(patch_tasks, back_scaled * reduced)
    back_reduced = (back_scaled * task_scales).astype(BF)
    grad_global_down = contract(back_reduced, attended, 0, 0)

    small = jnp.concatenate([grad_global_scales, jnp.zeros((TASKS, width - RANK), F32)], axis=1)
    small_local = local_sums[RANK : RANK + TASKS, :width]
    packed = jnp.concatenate(
        [
            grad_global_down,
            grad_global_up,
            local_sums[2 * RANK :, :units],
            local_sums[:RANK, :width],
            local_sums[:RANK, width:],
            small,
            small_local,
        ]
    ).astype(BF)
    shape = packed.shape
    pieces = packed.reshape(lax.axis_size(EIGHT), -1, shape[1])
    pieces = total(exchange(pieces, EIGHT)).astype(BF)
    pieces = total(to_everyone(pieces, Z)).astype(BF)
    packed = to_everyone(pieces, EIGHT).reshape(shape).astype(F32)
    return (
        jnp.transpose(packed[:16]),
        packed[16:32],
        packed[80:88, :RANK],
        jnp.transpose(jnp.concatenate([packed[48:64], packed[64:80]], axis=1)),
        packed[32:48],
        packed[88:96, :RANK],
    )


def solution(mesh):
    torus = Mesh(mesh.devices.reshape(8, 2, 2, 2, 4, 2), SEQ_ROW)
    placed = (
        P(SEQ, ROW),
        P(SEQ, ROW),
        P(SEQ, ROW),
        P(SEQ),
        P(SEQ, ROW),
        P(ROW, None),
        P(ROW, None),
        P(None, ROW),
        P(),
        P(ROW, None),
        P(SEQ),
        P(),
        P(),
        P(),
        P(ROW, SEQ),
        P(ROW, SEQ),
        P(),
        P(None, ROW),
        P(),
        P(SEQ_ROW, None),
    )
    return jax.shard_map(
        body,
        mesh=torus,
        in_specs=placed,
        out_specs=(P(ROW, None), P(None, ROW), P(), P(), P(None, ROW), P()),
        check_vma=False,
    )
```

```python
import functools
import math

import jax
import jax.numpy as jnp
from jax import lax
from jax.experimental import pallas as pl
from jax.experimental.pallas import tpu as pltpu
from jax.sharding import Mesh
from jax.sharding import PartitionSpec as P

HEAD = 128
VOCAB = 256
PATCH = 8
TASKS = 8
RANK = 16
ROW = ("row_0", "row_1")
SEQ = ("seq_0", "near", "seq_1", "seq_2")
Z, NEAR, FAR, CORE = SEQ
QUAD = (NEAR, FAR)
EIGHT = (NEAR, FAR, CORE)
LINE, SIDE = ROW
SEQ_ROW = SEQ + ROW
SWAP = [(0, 1), (1, 0)]
BF = jnp.bfloat16
F32 = jnp.float32


def exchange(pieces, axis):
    return lax.all_to_all(pieces, axis, split_axis=0, concat_axis=0, tiled=True)


def to_everyone(array, axis):
    size = lax.axis_size(axis)
    return exchange(jnp.broadcast_to(array[None], (size, *array.shape)), axis)


def contract(left, right, left_dim, right_dim):
    return lax.dot_general(
        left, right, (((left_dim,), (right_dim,)), ((), ())), preferred_element_type=F32
    )


def select_rows(table, tasks):
    picks = (tasks[:, None] == jnp.arange(table.shape[0], dtype=jnp.int32)[None, :]).astype(F32)
    return jnp.dot(picks, table, precision=lax.Precision.HIGHEST)


def task_totals(tasks, values):
    picks = (tasks[:, None] == jnp.arange(TASKS, dtype=jnp.int32)[None, :]).astype(F32)
    return lax.dot_general(picks, values, (((0,), (0,)), ((), ())), precision=lax.Precision.HIGHEST)


def gelu_slope(upper):
    cumulative = 0.5 * (1.0 + lax.erf(upper * 0.7071067811865476))
    density = jnp.exp(-0.5 * upper * upper) * 0.3989422804014327
    return cumulative + upper * density


def in_pair_order(mine, other, place, axis):
    first = jnp.where(place == 0, mine, other)
    second = jnp.where(place == 0, other, mine)
    return jnp.concatenate([first, second], axis=axis)


def total(array):
    return lax.optimization_barrier(array.astype(F32).sum(axis=0))


def fold(array):
    array = jnp.concatenate([array[:, :128], array[:, 128:]], axis=0)
    return jnp.concatenate([array[8 * k : 8 * k + 8] for k in range(4)], axis=1)


def unfold(array):
    array = jnp.concatenate([array[:, :, 128 * k : 128 * k + 128] for k in range(4)], axis=1)
    return jnp.concatenate([array[:, :RANK], array[:, RANK:]], axis=2)


def attend_kernel(spots, queries, *refs, count, start, finish):
    packets, refs = refs[:count], refs[count:]
    rows = queries.shape[0]
    half = rows // 2
    if start:
        top = jnp.full((rows, 1), -1e20, F32)
        mass = jnp.zeros((rows, HEAD), F32)
        out = jnp.zeros((rows, HEAD), F32)
    else:
        top, mass, out = refs[0][:, :1], refs[1][...], refs[2][...]
        refs = refs[3:]
    core = spots[0]

    def inside(shape, dim):
        at = lax.broadcasted_iota(jnp.int32, shape, dim)
        return jnp.where(at < half, at + core * half, at - core * half)

    query_places = (spots[1] + pl.program_id(0)) * rows + inside((rows, 1), 0)
    own = queries[...]
    for index in range(count):
        keys = packets[index][:, :HEAD]
        values = packets[index][:, HEAD:]
        key_places = spots[2 + index] * rows + inside((1, rows), 1)
        scores = contract(own, keys, 1, 1) * (1.0 / math.sqrt(HEAD))
        scores = jnp.where(key_places <= query_places, scores, -1e30)
        new_top = jnp.maximum(top, jnp.max(scores, axis=1, keepdims=True))
        weights = jnp.exp(scores - new_top)
        shrink = jnp.exp(top - new_top)
        mass = mass * shrink + (weights[:, :HEAD] + weights[:, HEAD:])
        out = out * shrink + jnp.dot(weights.astype(BF), values, preferred_element_type=F32)
        top = new_top
    if not finish:
        refs[0][...] = jnp.broadcast_to(top, (rows, HEAD))
        refs[1][...] = mass
        refs[2][...] = out
        return
    mass = jnp.sum(mass, axis=1, keepdims=True)
    safe = jnp.where(mass > 0, mass, 1.0)
    level = jnp.where(mass > 0, top + jnp.log(safe), -1e30)
    level = jnp.broadcast_to(level, (rows, HEAD))
    high = level.astype(BF).astype(F32)
    middle = (level - high).astype(BF).astype(F32)
    low = level - high - middle
    lane = lax.broadcasted_iota(jnp.int32, (rows, HEAD), 1)
    level = jnp.where(lane < 32, high, jnp.where(lane < 64, middle, low))
    refs[0][:, :HEAD] = (out / safe).astype(BF)
    refs[0][:, HEAD:] = level.astype(BF)


def in_place_kernel(spots, *refs):
    out = refs[-1]
    for index, piece in enumerate(refs[:-1]):
        tall = piece.shape[0]
        out[pl.ds(pl.multiple_of(spots[index] * tall, tall), tall), :] = piece[...]


def in_place(spots, pieces, tall):
    wide = pieces[0].shape[1]
    count = len(pieces)
    specs = [
        pl.BlockSpec((tall, wide), functools.partial(lambda at, k: (at, 0), p.shape[0] // tall - 1))
        for p in pieces
    ]
    return pl.pallas_call(
        in_place_kernel,
        grid=(1,),
        in_specs=[pl.BlockSpec(memory_space=pltpu.SMEM)] + specs,
        out_specs=pl.BlockSpec((count * tall, wide), lambda k: (0, 0)),
        out_shape=jax.ShapeDtypeStruct((count * tall, wide), pieces[0].dtype),
        name="in_place",
    )(spots, *pieces)


def attend(spots, queries, packets, state, finish, rows):
    total_rows = queries.shape[0] * rows
    block = pl.BlockSpec((rows, HEAD), lambda k: (k, 0))
    asked = pl.BlockSpec((None, rows, HEAD), lambda k: (k, 0, 0))
    whole = pl.BlockSpec((rows, 2 * HEAD), lambda k: (0, 0))
    start = state is None
    state = () if start else state
    if finish:
        shapes = jax.ShapeDtypeStruct((queries.shape[0], rows, 2 * HEAD), BF)
        outs = pl.BlockSpec((None, rows, 2 * HEAD), lambda k: (k, 0, 0))
    else:
        shapes = (jax.ShapeDtypeStruct((total_rows, HEAD), F32),) * 3
        outs = (block,) * 3
    return pl.pallas_call(
        functools.partial(attend_kernel, count=len(packets), start=start, finish=finish),
        grid=(total_rows // rows,),
        in_specs=[pl.BlockSpec(memory_space=pltpu.SMEM), asked]
        + [whole] * len(packets)
        + [block] * len(state),
        out_specs=outs,
        out_shape=shapes,
        name="attend",
    )(spots, queries, *packets, *state)


def body(
    patch_queries,
    patch_keys,
    patch_values,
    patch_tasks,
    residual,
    output_weight,
    global_down,
    global_up,
    global_scales,
    local_weight,
    byte_ids,
    byte_table,
    position_table,
    norm_gain,
    hidden_in,
    hidden_out,
    local_down,
    local_up,
    local_scales,
    cotangent,
):
    rows, width = patch_queries.shape
    ring = lax.axis_size(Z)
    row_count = lax.axis_size(ROW)
    z = lax.axis_index(Z)
    near = lax.axis_index(NEAR)
    far = lax.axis_index(FAR)
    side = lax.axis_index(SIDE)
    line = lax.axis_size(LINE)
    core = lax.axis_index(CORE)
    row_index = lax.axis_index(ROW)
    columns = local_weight.shape[1]
    units = hidden_in.shape[0]
    share = hidden_in.shape[1]

    hidden = jnp.concatenate([hidden_in.T, hidden_out.T], axis=0)
    weights = jnp.concatenate([local_weight, fold(global_up), fold(local_up)], axis=0)
    weights = lax.all_gather(weights, ROW, axis=0, tiled=False)
    cotangents = jnp.concatenate([cotangent, lax.ppermute(cotangent, SIDE, SWAP)], axis=0)

    def head(array, which):
        return lax.dynamic_slice_in_dim(array, which * HEAD, HEAD, 1)

    trio = (patch_queries, patch_keys, patch_values)
    mine = jnp.concatenate([head(a, core) for a in trio], axis=1)
    other = jnp.concatenate([head(a, 1 - core) for a in trio], axis=1)
    both = jnp.concatenate([mine, lax.ppermute(other, CORE, SWAP)], axis=0)
    chip_rows = 2 * rows
    packet = both[:, HEAD:]
    halves = [hidden[:, k * HEAD : (k + 1) * HEAD] for k in range(units // HEAD)]
    queries = to_everyone(jnp.concatenate([both[:, :HEAD], *halves], axis=0), QUAD)
    sides = lax.axis_size(QUAD)
    tall = sides * 2 * share

    up = [(i, (i + 1) % ring) for i in range(ring)]
    down = [(i, (i - 1) % ring) for i in range(ring)]

    rising = lax.ppermute(packet, Z, up)
    falling = lax.ppermute(packet, Z, down)
    held, at = [packet, rising, falling], [z, z - 1, z + 1]
    rising, falling, queries = lax.optimization_barrier((rising, falling, queries))
    riders = jnp.concatenate(
        [
            queries[:, chip_rows + k * 2 * share :][:, : 2 * share].reshape(tall, HEAD)
            for k in range(units // HEAD)
        ],
        axis=1,
    )
    pieces, whose = [riders], [z]
    rising = jnp.concatenate([rising, riders], axis=0)
    falling = jnp.concatenate([falling, riders], axis=0)
    for step in range(2, ring // 2):
        rising = lax.ppermute(rising, Z, up)
        falling = lax.ppermute(falling, Z, down)
        held += [rising, falling]
        at += [z - step, z + step]
        pieces += [rising, falling]
        whose += [z - step + 1, z + step - 1]
    rising = lax.ppermute(rising, Z, up)
    falling = lax.ppermute(falling[chip_rows:], Z, down)
    held.append(rising)
    at.append(z - ring // 2)
    pieces += [rising, falling, lax.ppermute(rising[chip_rows:], Z, up)]
    whose += [z - ring // 2 + 1, z + ring // 2 - 1, z - ring // 2]
    at = [k % ring for k in at]
    whose = jnp.stack([k % ring for k in whose]).astype(jnp.int32)
    spots = jnp.stack([z * sides] + [k * sides + near * 2 + far for k in at]).astype(jnp.int32)
    spots = jnp.concatenate([core.astype(jnp.int32)[None], spots])
    state = attend(spots, queries, held[:-1], None, False, chip_rows)
    last, weights = lax.optimization_barrier((held[-1], weights))
    spots = jnp.concatenate([spots[:2], spots[-1:]])
    met = attend(spots, queries, [last], state, True, chip_rows)
    riders = lax.all_gather(in_place(whose, pieces, tall), LINE, axis=0, tiled=False)

    local_whole = weights[:, :width].reshape(-1, columns)
    up_whole = unfold(weights[:, width : width + 8])
    up_whole = jnp.transpose(up_whole, (1, 0, 2)).reshape(RANK, -1)
    local_ups = unfold(weights[:, width + 8 :]).reshape(line, 2, RANK, units)
    local_ups = lax.dynamic_index_in_dim(local_ups, side, 1, keepdims=False)

    met = exchange(met, QUAD).astype(F32)
    levels = met[:, :, 128:129] + met[:, :, 160:161] + met[:, :, 192:193]
    parts = jnp.exp(levels - jnp.max(levels, axis=0, keepdims=True))
    merged = (parts * met[:, :, :HEAD]).sum(axis=0) / parts.sum(axis=0)
    merged = merged.astype(BF)
    partner = lax.ppermute(merged[rows:], CORE, SWAP)
    attended = in_pair_order(merged[:rows], partner, core, 1)

    task_scales = select_rows(global_scales, patch_tasks)
    part = contract(output_weight, attended, 0, 1).astype(BF).reshape(row_count, width, rows)
    low_part = contract(global_down, attended, 0, 1).astype(BF)
    low_part = jnp.broadcast_to(low_part[None], (row_count, RANK, rows))
    arrived = exchange(jnp.concatenate([part, low_part], axis=1), ROW)
    arrived = arrived.astype(F32).sum(axis=0)

    reduced = jnp.transpose(arrived[width:])
    scaled = (reduced * task_scales).astype(BF)
    mixed = arrived[:width] + jnp.transpose(residual.astype(F32)) + contract(global_up, scaled, 0, 1)
    mixed_b = mixed.astype(BF)
    own_patches = rows // row_count
    own_bytes = own_patches * PATCH
    own_tasks = lax.dynamic_slice_in_dim(patch_tasks, row_index * own_patches, own_patches)
    own_ids = lax.dynamic_slice_in_dim(byte_ids, row_index * own_bytes, own_bytes)
    projected = contract(mixed_b, local_weight, 0, 0).astype(BF)
    projected = exchange(projected.reshape(row_count, own_patches, columns), ROW)
    projected, riders = lax.optimization_barrier((projected, riders))
    projected = total(projected).astype(BF)

    rest = lax.ppermute(riders, CORE, SWAP)
    split = (line, columns // (2 * share), 2, 1, share, units)
    riders = in_pair_order(riders.reshape(split), rest.reshape(split), core, 3)
    riders = jnp.moveaxis(riders, 2, 0).reshape(2, line, columns, units)
    rows_in, rows_out = riders[0], riders[1]
    lanes = 128
    spare_rows = jnp.zeros((line, lanes - RANK, units), BF)
    stacked = jnp.concatenate([rows_in, local_ups, spare_rows], axis=1)

    picks = (own_ids[:, None] == jnp.arange(VOCAB, dtype=jnp.int32)[None, :]).astype(BF)
    embedded = jnp.dot(picks, byte_table, preferred_element_type=F32)
    embedded = embedded.reshape(own_patches, PATCH, -1) + position_table.astype(F32)[None]
    inputs = (embedded + projected.astype(F32)[:, None, :]).reshape(own_bytes, columns)
    inverse = lax.rsqrt(jnp.mean(inputs * inputs, axis=1, keepdims=True) + 1e-06)
    normed = (inputs * inverse * norm_gain).astype(BF)
    lowered = jnp.dot(normed, local_down, preferred_element_type=F32)
    byte_tasks = jnp.repeat(own_tasks, PATCH)
    scales = select_rows(local_scales, byte_tasks)
    shrunk = (lowered * scales).astype(BF)
    joined = jnp.concatenate(
        [normed, shrunk, jnp.zeros((own_bytes, lanes - RANK), BF)], axis=1
    )
    joined = jnp.concatenate([joined, lax.ppermute(joined, SIDE, SWAP)], axis=0)
    through = contract(cotangents, rows_out, 1, 1)
    upper = contract(joined, stacked, 1, 1)
    grown = (through * gelu_slope(upper)).astype(BF)
    back = lax.dot_general(
        grown, stacked, (((1, 2), (0, 2)), ((), ())), preferred_element_type=F32
    )
    back = back[:own_bytes] + lax.ppermute(back[own_bytes:].astype(BF), SIDE, SWAP).astype(F32)
    ups = contract(joined[:, columns:], grown, 0, 0)[:RANK].astype(BF)
    back_norm = back[:, :columns]
    back_rank = back[:, columns : columns + RANK]
    grad_local_scales = task_totals(byte_tasks, back_rank * lowered)
    moved = (back_rank * scales).astype(BF)
    grad_local_down = contract(moved, normed, 0, 0)
    back_total = back_norm + contract(moved, local_down, 1, 1)
    gained = back_total * norm_gain
    average = jnp.mean(gained * inputs, axis=1, keepdims=True)
    back_inputs = cotangent.astype(F32) + inverse * (
        gained - inputs * inverse * inverse * average
    )
    patch_grad = back_inputs.reshape(own_patches, PATCH, -1).sum(axis=1)
    patch_grad = lax.optimization_barrier(patch_grad).astype(BF)

    spare = jnp.zeros((TASKS, columns - RANK), F32)
    local_rows = jnp.concatenate([grad_local_scales, spare], axis=1)
    local_rows = jnp.concatenate([grad_local_down, local_rows, jnp.zeros_like(local_rows)])
    row_pack = jnp.concatenate([patch_grad, local_rows.astype(BF)], axis=0)
    row_pack = jnp.broadcast_to(row_pack[None], (row_count, *row_pack.shape))
    ups = jnp.transpose(ups, (1, 0, 2))
    ups = jnp.stack([jnp.where(side == k, ups, jnp.zeros_like(ups)) for k in range(2)], axis=1)
    ups = jnp.pad(ups.reshape(row_count, RANK, units), [(0, 0), (0, 0), (0, columns - units)])
    row_pack = exchange(jnp.concatenate([row_pack, ups], axis=1), ROW)
    patch_grads = row_pack[:, :own_patches].reshape(rows, columns)
    local_sums = total(row_pack[:, own_patches:])
    back_mixed = contract(patch_grads, local_weight, 1, 1).astype(BF)
    back_whole = contract(patch_grads, local_whole, 1, 1).astype(BF)
    back_scaled = contract(back_whole, up_whole, 1, 1)
    grad_global_up = contract(scaled, back_mixed, 0, 0)
    grad_global_scales = task_totals(patch_tasks, back_scaled * reduced)
    back_reduced = (back_scaled * task_scales).astype(BF)
    grad_global_down = contract(back_reduced, attended, 0, 0)

    small = jnp.concatenate([grad_global_scales, jnp.zeros((TASKS, width - RANK), F32)], axis=1)
    small_local = local_sums[RANK : RANK + TASKS, :width]
    packed = jnp.concatenate(
        [
            grad_global_down,
            grad_global_up,
            local_sums[2 * RANK :, :units],
            local_sums[:RANK, :width],
            local_sums[:RANK, width:],
            small,
            small_local,
        ]
    ).astype(BF)
    shape = packed.shape
    pieces = packed.reshape(lax.axis_size(EIGHT), -1, shape[1])
    pieces = total(exchange(pieces, EIGHT)).astype(BF)
    pieces = total(to_everyone(pieces, Z)).astype(BF)
    packed = to_everyone(pieces, EIGHT).reshape(shape).astype(F32)
    return (
        jnp.transpose(packed[:16]),
        packed[16:32],
        packed[80:88, :RANK],
        jnp.transpose(jnp.concatenate([packed[48:64], packed[64:80]], axis=1)),
        packed[32:48],
        packed[88:96, :RANK],
    )


def solution(mesh):
    torus = Mesh(mesh.devices.reshape(8, 2, 2, 2, 4, 2), SEQ_ROW)
    placed = (
        P(SEQ, ROW),
        P(SEQ, ROW),
        P(SEQ, ROW),
        P(SEQ),
        P(SEQ, ROW),
        P(ROW, None),
        P(ROW, None),
        P(None, ROW),
        P(),
        P(ROW, None),
        P(SEQ),
        P(),
        P(),
        P(),
        P(ROW, SEQ),
        P(ROW, SEQ),
        P(),
        P(None, ROW),
        P(),
        P(SEQ_ROW, None),
    )
    return jax.shard_map(
        body,
        mesh=torus,
        in_specs=placed,
        out_specs=(P(ROW, None), P(None, ROW), P(), P(), P(None, ROW), P()),
        check_vma=False,
    )
```

```python
import functools
import math

import jax
import jax.numpy as jnp
from jax import lax
from jax.experimental import pallas as pl
from jax.experimental.pallas import tpu as pltpu
from jax.sharding import Mesh
from jax.sharding import PartitionSpec as P

HEAD = 128
VOCAB = 256
PATCH = 8
TASKS = 8
RANK = 16
ROW = ("row_0", "row_1")
SEQ = ("seq_0", "near", "seq_1", "seq_2")
Z, NEAR, FAR, CORE = SEQ
QUAD = (NEAR, FAR)
EIGHT = (NEAR, FAR, CORE)
LINE, SIDE = ROW
SEQ_ROW = SEQ + ROW
SWAP = [(0, 1), (1, 0)]
BF = jnp.bfloat16
F32 = jnp.float32


def exchange(pieces, axis):
    return lax.all_to_all(pieces, axis, split_axis=0, concat_axis=0, tiled=True)


def to_everyone(array, axis):
    size = lax.axis_size(axis)
    return exchange(jnp.broadcast_to(array[None], (size, *array.shape)), axis)


def contract(left, right, left_dim, right_dim):
    return lax.dot_general(
        left, right, (((left_dim,), (right_dim,)), ((), ())), preferred_element_type=F32
    )


def select_rows(table, tasks):
    picks = (tasks[:, None] == jnp.arange(table.shape[0], dtype=jnp.int32)[None, :]).astype(F32)
    return jnp.dot(picks, table, precision=lax.Precision.HIGHEST)


def task_totals(tasks, values):
    picks = (tasks[:, None] == jnp.arange(TASKS, dtype=jnp.int32)[None, :]).astype(F32)
    return lax.dot_general(picks, values, (((0,), (0,)), ((), ())), precision=lax.Precision.HIGHEST)


def gelu_slope(upper):
    cumulative = 0.5 * (1.0 + lax.erf(upper * 0.7071067811865476))
    density = jnp.exp(-0.5 * upper * upper) * 0.3989422804014327
    return cumulative + upper * density


def in_pair_order(mine, other, place, axis):
    first = jnp.where(place == 0, mine, other)
    second = jnp.where(place == 0, other, mine)
    return jnp.concatenate([first, second], axis=axis)


def total(array):
    return lax.optimization_barrier(array.astype(F32).sum(axis=0))


def fold(array):
    array = jnp.concatenate([array[:, :128], array[:, 128:]], axis=0)
    return jnp.concatenate([array[8 * k : 8 * k + 8] for k in range(4)], axis=1)


def unfold(array):
    array = jnp.concatenate([array[:, :, 128 * k : 128 * k + 128] for k in range(4)], axis=1)
    return jnp.concatenate([array[:, :RANK], array[:, RANK:]], axis=2)


def attend_kernel(spots, queries, *refs, count, start, finish):
    packets, refs = refs[:count], refs[count:]
    blocks, rows = queries.shape[:2]
    half = rows // 2
    core = spots[0]
    state_in = () if start else refs[:3]
    refs = refs[len(state_in) :]

    def inside(shape, dim):
        at = lax.broadcasted_iota(jnp.int32, shape, dim)
        return jnp.where(at < half, at + core * half, at - core * half)

    for block in range(blocks):
        here = pl.ds(block * rows, rows)
        if start:
            top = jnp.full((rows, 1), -1e20, F32)
            mass = jnp.zeros((rows, HEAD), F32)
            out = jnp.zeros((rows, HEAD), F32)
        else:
            top = state_in[0][here, :1]
            mass, out = state_in[1][here, :], state_in[2][here, :]
        place = spots[1] + pl.program_id(0) * blocks + block
        query_places = place * rows + inside((rows, 1), 0)
        own = queries[block]
        for index in range(count):
            keys = packets[index][:, :HEAD]
            values = packets[index][:, HEAD:]
            key_places = spots[2 + index] * rows + inside((1, rows), 1)
            scores = contract(own, keys, 1, 1) * (1.0 / math.sqrt(HEAD))
            scores = jnp.where(key_places <= query_places, scores, -1e30)
            new_top = jnp.maximum(top, jnp.max(scores, axis=1, keepdims=True))
            weights = jnp.exp(scores - new_top)
            shrink = jnp.exp(top - new_top)
            mass = mass * shrink + (weights[:, :HEAD] + weights[:, HEAD:])
            out = out * shrink + jnp.dot(weights.astype(BF), values, preferred_element_type=F32)
            top = new_top
        if not finish:
            refs[0][here, :] = jnp.broadcast_to(top, (rows, HEAD))
            refs[1][here, :] = mass
            refs[2][here, :] = out
            continue
        mass = jnp.sum(mass, axis=1, keepdims=True)
        safe = jnp.where(mass > 0, mass, 1.0)
        level = jnp.where(mass > 0, top + jnp.log(safe), -1e30)
        level = jnp.broadcast_to(level, (rows, HEAD))
        high = level.astype(BF).astype(F32)
        middle = (level - high).astype(BF).astype(F32)
        low = level - high - middle
        lane = lax.broadcasted_iota(jnp.int32, (rows, HEAD), 1)
        level = jnp.where(lane < 32, high, jnp.where(lane < 64, middle, low))
        refs[0][block, :, :HEAD] = (out / safe).astype(BF)
        refs[0][block, :, HEAD:] = level.astype(BF)


def in_place_kernel(spots, *refs):
    out = refs[-1]
    for index, piece in enumerate(refs[:-1]):
        tall = piece.shape[0]
        out[pl.ds(pl.multiple_of(spots[index] * tall, tall), tall), :] = piece[...]


def in_place(spots, pieces, tall):
    wide = pieces[0].shape[1]
    count = len(pieces)
    specs = [
        pl.BlockSpec((tall, wide), functools.partial(lambda at, k: (at, 0), p.shape[0] // tall - 1))
        for p in pieces
    ]
    return pl.pallas_call(
        in_place_kernel,
        grid=(1,),
        in_specs=[pl.BlockSpec(memory_space=pltpu.SMEM)] + specs,
        out_specs=pl.BlockSpec((count * tall, wide), lambda k: (0, 0)),
        out_shape=jax.ShapeDtypeStruct((count * tall, wide), pieces[0].dtype),
        name="in_place",
    )(spots, *pieces)


def attend(spots, queries, packets, state, finish, rows):
    sides = queries.shape[0]
    blocks = sides if finish else 2
    block = pl.BlockSpec((blocks * rows, HEAD), lambda k: (k, 0))
    asked = pl.BlockSpec((blocks, rows, HEAD), lambda k: (k, 0, 0))
    whole = pl.BlockSpec((rows, 2 * HEAD), lambda k: (0, 0))
    start = state is None
    state = () if start else state
    if finish:
        shapes = jax.ShapeDtypeStruct((sides, rows, 2 * HEAD), BF)
        outs = pl.BlockSpec((blocks, rows, 2 * HEAD), lambda k: (k, 0, 0))
    else:
        shapes = (jax.ShapeDtypeStruct((sides * rows, HEAD), F32),) * 3
        outs = (block,) * 3
    return pl.pallas_call(
        functools.partial(attend_kernel, count=len(packets), start=start, finish=finish),
        grid=(sides // blocks,),
        in_specs=[pl.BlockSpec(memory_space=pltpu.SMEM), asked]
        + [whole] * len(packets)
        + [block] * len(state),
        out_specs=outs,
        out_shape=shapes,
        name="attend",
    )(spots, queries, *packets, *state)


def body(
    patch_queries,
    patch_keys,
    patch_values,
    patch_tasks,
    residual,
    output_weight,
    global_down,
    global_up,
    global_scales,
    local_weight,
    byte_ids,
    byte_table,
    position_table,
    norm_gain,
    hidden_in,
    hidden_out,
    local_down,
    local_up,
    local_scales,
    cotangent,
):
    rows, width = patch_queries.shape
    ring = lax.axis_size(Z)
    row_count = lax.axis_size(ROW)
    z = lax.axis_index(Z)
    near = lax.axis_index(NEAR)
    far = lax.axis_index(FAR)
    side = lax.axis_index(SIDE)
    line = lax.axis_size(LINE)
    core = lax.axis_index(CORE)
    row_index = lax.axis_index(ROW)
    columns = local_weight.shape[1]
    units = hidden_in.shape[0]
    share = hidden_in.shape[1]

    def head(array, which):
        return lax.dynamic_slice_in_dim(array, which * HEAD, HEAD, 1)

    trio = (patch_queries, patch_keys, patch_values)
    mine = jnp.concatenate([head(a, core) for a in trio], axis=1)
    other = jnp.concatenate([head(a, 1 - core) for a in trio], axis=1)
    hidden = jnp.concatenate([hidden_in.T, hidden_out.T], axis=0)
    other, *early = lax.optimization_barrier((other, local_weight, global_up, local_up))
    weights = jnp.concatenate([early[0], fold(early[1]), fold(early[2])], axis=0)
    weights = lax.all_gather(weights, ROW, axis=0, tiled=False)
    cotangents = jnp.concatenate([cotangent, lax.ppermute(cotangent, SIDE, SWAP)], axis=0)

    both = jnp.concatenate([mine, lax.ppermute(other, CORE, SWAP)], axis=0)
    chip_rows = 2 * rows
    packet = both[:, HEAD:]
    halves = [hidden[:, k * HEAD : (k + 1) * HEAD] for k in range(units // HEAD)]
    queries = to_everyone(jnp.concatenate([both[:, :HEAD], *halves], axis=0), QUAD)
    sides = lax.axis_size(QUAD)
    tall = sides * 2 * share

    up = [(i, (i + 1) % ring) for i in range(ring)]
    down = [(i, (i - 1) % ring) for i in range(ring)]

    rising = lax.ppermute(packet, Z, up)
    falling = lax.ppermute(packet, Z, down)
    held, at = [packet, rising, falling], [z, z - 1, z + 1]
    rising, falling, queries = lax.optimization_barrier((rising, falling, queries))
    riders = jnp.concatenate(
        [
            queries[:, chip_rows + k * 2 * share :][:, : 2 * share].reshape(tall, HEAD)
            for k in range(units // HEAD)
        ],
        axis=1,
    )
    pieces, whose = [riders], [z]
    rising = jnp.concatenate([rising, riders], axis=0)
    falling = jnp.concatenate([falling, riders], axis=0)
    for step in range(2, ring // 2):
        rising = lax.ppermute(rising, Z, up)
        falling = lax.ppermute(falling, Z, down)
        held += [rising, falling]
        at += [z - step, z + step]
        pieces += [rising, falling]
        whose += [z - step + 1, z + step - 1]
    rising = lax.ppermute(rising, Z, up)
    falling = lax.ppermute(falling[chip_rows:], Z, down)
    held.append(rising)
    at.append(z - ring // 2)
    pieces.append(rising)
    whose += [z - ring // 2 + 1, z + ring // 2 - 1, z - ring // 2]
    at = [k % ring for k in at]
    whose = jnp.stack([k % ring for k in whose]).astype(jnp.int32)
    spots = jnp.stack([z * sides] + [k * sides + near * 2 + far for k in at]).astype(jnp.int32)
    spots = jnp.concatenate([core.astype(jnp.int32)[None], spots])
    state = attend(spots, queries, held[:-1], None, False, chip_rows)
    state, last, weights, falling = lax.optimization_barrier((state, rising, weights, falling))
    final = lax.ppermute(last[chip_rows:], Z, up)
    spots = jnp.concatenate([spots[:2], spots[-1:]])
    met = attend(spots, queries, [last], state, True, chip_rows)
    met, final = lax.optimization_barrier((met, final))
    pieces += [falling, final]
    riders = lax.all_gather(in_place(whose, pieces, tall), LINE, axis=0, tiled=False)

    local_whole = weights[:, :width].reshape(-1, columns)
    up_whole = unfold(weights[:, width : width + 8])
    up_whole = jnp.transpose(up_whole, (1, 0, 2)).reshape(RANK, -1)
    local_ups = unfold(weights[:, width + 8 :]).reshape(line, 2, RANK, units)
    local_ups = lax.dynamic_index_in_dim(local_ups, side, 1, keepdims=False)

    met = exchange(met, QUAD).astype(F32)
    levels = met[:, :, 128:129] + met[:, :, 160:161] + met[:, :, 192:193]
    parts = jnp.exp(levels - jnp.max(levels, axis=0, keepdims=True))
    merged = (parts * met[:, :, :HEAD]).sum(axis=0) / parts.sum(axis=0)
    merged = merged.astype(BF)
    partner = lax.ppermute(merged[rows:], CORE, SWAP)
    attended = in_pair_order(merged[:rows], partner, core, 1)

    task_scales = select_rows(global_scales, patch_tasks)
    part = contract(output_weight, attended, 0, 1).astype(BF).reshape(row_count, width, rows)
    low_part = contract(global_down, attended, 0, 1).astype(BF)
    low_part = jnp.broadcast_to(low_part[None], (row_count, RANK, rows))
    arrived = exchange(jnp.concatenate([part, low_part], axis=1), ROW)
    arrived = arrived.astype(F32).sum(axis=0)

    reduced = jnp.transpose(arrived[width:])
    scaled = (reduced * task_scales).astype(BF)
    mixed = arrived[:width] + jnp.transpose(residual.astype(F32)) + contract(global_up, scaled, 0, 1)
    mixed_b = mixed.astype(BF)
    own_patches = rows // row_count
    own_bytes = own_patches * PATCH
    own_tasks = lax.dynamic_slice_in_dim(patch_tasks, row_index * own_patches, own_patches)
    own_ids = lax.dynamic_slice_in_dim(byte_ids, row_index * own_bytes, own_bytes)
    projected = contract(mixed_b, local_weight, 0, 0).astype(BF)
    projected = exchange(projected.reshape(row_count, own_patches, columns), ROW)
    projected, riders = lax.optimization_barrier((projected, riders))
    projected = total(projected).astype(BF)

    rest = lax.ppermute(riders, CORE, SWAP)
    split = (line, columns // (2 * share), 2, 1, share, units)
    riders = in_pair_order(riders.reshape(split), rest.reshape(split), core, 3)
    riders = jnp.moveaxis(riders, 2, 0).reshape(2, line, columns, units)
    rows_in, rows_out = riders[0], riders[1]
    lanes = 128
    spare_rows = jnp.zeros((line, lanes - RANK, units), BF)
    stacked = jnp.concatenate([rows_in, local_ups, spare_rows], axis=1)

    picks = (own_ids[:, None] == jnp.arange(VOCAB, dtype=jnp.int32)[None, :]).astype(BF)
    embedded = jnp.dot(picks, byte_table, preferred_element_type=F32)
    embedded = embedded.reshape(own_patches, PATCH, -1) + position_table.astype(F32)[None]
    inputs = (embedded + projected.astype(F32)[:, None, :]).reshape(own_bytes, columns)
    inverse = lax.rsqrt(jnp.mean(inputs * inputs, axis=1, keepdims=True) + 1e-06)
    normed = (inputs * inverse * norm_gain).astype(BF)
    lowered = jnp.dot(normed, local_down, preferred_element_type=F32)
    byte_tasks = jnp.repeat(own_tasks, PATCH)
    scales = select_rows(local_scales, byte_tasks)
    shrunk = (lowered * scales).astype(BF)
    joined = jnp.concatenate(
        [normed, shrunk, jnp.zeros((own_bytes, lanes - RANK), BF)], axis=1
    )
    joined = jnp.concatenate([joined, lax.ppermute(joined, SIDE, SWAP)], axis=0)
    through = contract(cotangents, rows_out, 1, 1)
    upper = contract(joined, stacked, 1, 1)
    grown = (through * gelu_slope(upper)).astype(BF)
    back = lax.dot_general(
        grown, stacked, (((1, 2), (0, 2)), ((), ())), preferred_element_type=F32
    )
    back = back[:own_bytes] + lax.ppermute(back[own_bytes:].astype(BF), SIDE, SWAP).astype(F32)
    ups = contract(joined[:, columns:], grown, 0, 0)[:RANK].astype(BF)
    back_norm = back[:, :columns]
    back_rank = back[:, columns : columns + RANK]
    grad_local_scales = task_totals(byte_tasks, back_rank * lowered)
    moved = (back_rank * scales).astype(BF)
    grad_local_down = contract(moved, normed, 0, 0)
    back_total = back_norm + contract(moved, local_down, 1, 1)
    gained = back_total * norm_gain
    average = jnp.mean(gained * inputs, axis=1, keepdims=True)
    back_inputs = cotangent.astype(F32) + inverse * (
        gained - inputs * inverse * inverse * average
    )
    patch_grad = back_inputs.reshape(own_patches, PATCH, -1).sum(axis=1)
    patch_grad = lax.optimization_barrier(patch_grad).astype(BF)

    spare = jnp.zeros((TASKS, columns - RANK), F32)
    local_rows = jnp.concatenate([grad_local_scales, spare], axis=1)
    local_rows = jnp.concatenate([grad_local_down, local_rows, jnp.zeros_like(local_rows)])
    row_pack = jnp.concatenate([patch_grad, local_rows.astype(BF)], axis=0)
    row_pack = jnp.broadcast_to(row_pack[None], (row_count, *row_pack.shape))
    ups = jnp.transpose(ups, (1, 0, 2))
    ups = jnp.stack([jnp.where(side == k, ups, jnp.zeros_like(ups)) for k in range(2)], axis=1)
    ups = jnp.pad(ups.reshape(row_count, RANK, units), [(0, 0), (0, 0), (0, columns - units)])
    row_pack = exchange(jnp.concatenate([row_pack, ups], axis=1), ROW)
    patch_grads = row_pack[:, :own_patches].reshape(rows, columns)
    local_sums = total(row_pack[:, own_patches:])
    back_mixed = contract(patch_grads, local_weight, 1, 1).astype(BF)
    back_whole = contract(patch_grads, local_whole, 1, 1).astype(BF)
    back_scaled = contract(back_whole, up_whole, 1, 1)
    grad_global_up = contract(scaled, back_mixed, 0, 0)
    grad_global_scales = task_totals(patch_tasks, back_scaled * reduced)
    back_reduced = (back_scaled * task_scales).astype(BF)
    grad_global_down = contract(back_reduced, attended, 0, 0)

    small = jnp.concatenate([grad_global_scales, jnp.zeros((TASKS, width - RANK), F32)], axis=1)
    small_local = local_sums[RANK : RANK + TASKS, :width]
    packed = jnp.concatenate(
        [
            grad_global_down,
            grad_global_up,
            local_sums[2 * RANK :, :units],
            local_sums[:RANK, :width],
            local_sums[:RANK, width:],
            small,
            small_local,
        ]
    ).astype(BF)
    shape = packed.shape
    pieces = packed.reshape(lax.axis_size(EIGHT), -1, shape[1])
    pieces = total(exchange(pieces, EIGHT)).astype(BF)
    pieces = total(to_everyone(pieces, Z)).astype(BF)
    packed = to_everyone(pieces, EIGHT).reshape(shape).astype(F32)
    return (
        jnp.transpose(packed[:16]),
        packed[16:32],
        packed[80:88, :RANK],
        jnp.transpose(jnp.concatenate([packed[48:64], packed[64:80]], axis=1)),
        packed[32:48],
        packed[88:96, :RANK],
    )


def solution(mesh):
    torus = Mesh(mesh.devices.reshape(8, 2, 2, 2, 4, 2), SEQ_ROW)
    placed = (
        P(SEQ, ROW),
        P(SEQ, ROW),
        P(SEQ, ROW),
        P(SEQ),
        P(SEQ, ROW),
        P(ROW, None),
        P(ROW, None),
        P(None, ROW),
        P(),
        P(ROW, None),
        P(SEQ),
        P(),
        P(),
        P(),
        P(ROW, SEQ),
        P(ROW, SEQ),
        P(),
        P(None, ROW),
        P(),
        P(SEQ_ROW, None),
    )
    return jax.shard_map(
        body,
        mesh=torus,
        in_specs=placed,
        out_specs=(P(ROW, None), P(None, ROW), P(), P(), P(None, ROW), P()),
        check_vma=False,
    )
```

```python
import functools
import math

import jax
import jax.numpy as jnp
from jax import lax
from jax.experimental import pallas as pl
from jax.experimental.pallas import tpu as pltpu
from jax.sharding import Mesh
from jax.sharding import PartitionSpec as P

HEAD = 128
VOCAB = 256
PATCH = 8
TASKS = 8
RANK = 16
ROW = ("row_0", "row_1")
SEQ = ("seq_0", "near", "seq_1", "seq_2")
Z, NEAR, FAR, CORE = SEQ
QUAD = (NEAR, FAR)
EIGHT = (NEAR, FAR, CORE)
LINE, SIDE = ROW
SEQ_ROW = SEQ + ROW
SWAP = [(0, 1), (1, 0)]
BF = jnp.bfloat16
F32 = jnp.float32


def exchange(pieces, axis):
    return lax.all_to_all(pieces, axis, split_axis=0, concat_axis=0, tiled=True)


def to_everyone(array, axis):
    size = lax.axis_size(axis)
    return exchange(jnp.broadcast_to(array[None], (size, *array.shape)), axis)


def contract(left, right, left_dim, right_dim):
    return lax.dot_general(
        left, right, (((left_dim,), (right_dim,)), ((), ())), preferred_element_type=F32
    )


def select_rows(table, tasks):
    picks = (tasks[:, None] == jnp.arange(table.shape[0], dtype=jnp.int32)[None, :]).astype(F32)
    return jnp.dot(picks, table, precision=lax.Precision.HIGHEST)


def task_totals(tasks, values):
    picks = (tasks[:, None] == jnp.arange(TASKS, dtype=jnp.int32)[None, :]).astype(F32)
    return lax.dot_general(picks, values, (((0,), (0,)), ((), ())), precision=lax.Precision.HIGHEST)


def gelu_slope(upper):
    cumulative = 0.5 * (1.0 + lax.erf(upper * 0.7071067811865476))
    density = jnp.exp(-0.5 * upper * upper) * 0.3989422804014327
    return cumulative + upper * density


def in_pair_order(mine, other, place, axis):
    first = jnp.where(place == 0, mine, other)
    second = jnp.where(place == 0, other, mine)
    return jnp.concatenate([first, second], axis=axis)


def total(array):
    return lax.optimization_barrier(array.astype(F32).sum(axis=0))


def fold(array):
    array = jnp.concatenate([array[:, :128], array[:, 128:]], axis=0)
    return jnp.concatenate([array[8 * k : 8 * k + 8] for k in range(4)], axis=1)


def unfold(array):
    array = jnp.concatenate([array[:, :, 128 * k : 128 * k + 128] for k in range(4)], axis=1)
    return jnp.concatenate([array[:, :RANK], array[:, RANK:]], axis=2)


def attend_kernel(spots, queries, *refs, count, start, hosted):
    finish = hosted > 0
    packets, refs = refs[:count], refs[count:]
    blocks, rows = queries.shape[:2]
    half = rows // 2
    core = spots[0]
    state_in = () if start else refs[:3]
    refs = refs[len(state_in) :]
    guests, refs = refs[:hosted], refs[hosted:]

    def inside(shape, dim):
        at = lax.broadcasted_iota(jnp.int32, shape, dim)
        return jnp.where(at < half, at + core * half, at - core * half)

    for block in range(blocks):
        here = pl.ds(block * rows, rows)
        if start:
            top = jnp.full((rows, 1), -1e20, F32)
            mass = jnp.zeros((rows, HEAD), F32)
            out = jnp.zeros((rows, HEAD), F32)
        else:
            top = state_in[0][here, :1]
            mass, out = state_in[1][here, :], state_in[2][here, :]
        place = spots[1] + pl.program_id(0) * blocks + block
        query_places = place * rows + inside((rows, 1), 0)
        own = queries[block]
        for index in range(count):
            keys = packets[index][:, :HEAD]
            values = packets[index][:, HEAD:]
            key_places = spots[2 + index] * rows + inside((1, rows), 1)
            scores = contract(own, keys, 1, 1) * (1.0 / math.sqrt(HEAD))
            scores = jnp.where(key_places <= query_places, scores, -1e30)
            new_top = jnp.maximum(top, jnp.max(scores, axis=1, keepdims=True))
            weights = jnp.exp(scores - new_top)
            shrink = jnp.exp(top - new_top)
            mass = mass * shrink + (weights[:, :HEAD] + weights[:, HEAD:])
            out = out * shrink + jnp.dot(weights.astype(BF), values, preferred_element_type=F32)
            top = new_top
        if not finish:
            refs[0][here, :] = jnp.broadcast_to(top, (rows, HEAD))
            refs[1][here, :] = mass
            refs[2][here, :] = out
            continue
        mass = jnp.sum(mass, axis=1, keepdims=True)
        safe = jnp.where(mass > 0, mass, 1.0)
        level = jnp.where(mass > 0, top + jnp.log(safe), -1e30)
        level = jnp.broadcast_to(level, (rows, HEAD))
        high = level.astype(BF).astype(F32)
        middle = (level - high).astype(BF).astype(F32)
        low = level - high - middle
        lane = lax.broadcasted_iota(jnp.int32, (rows, HEAD), 1)
        level = jnp.where(lane < 32, high, jnp.where(lane < 64, middle, low))
        refs[0][block, :rows, :HEAD] = (out / safe).astype(BF)
        refs[0][block, :rows, HEAD:] = level.astype(BF)
        for index, guest in enumerate(guests):
            extra = guest.shape[0]
            spot = pl.multiple_of(rows + spots[2 + count + index] * extra, extra)
            refs[0][block, pl.ds(spot, extra), :] = guest[...]


def attend(spots, queries, packets, state, guests, rows):
    sides = queries.shape[0]
    finish = len(guests) > 0
    extra = guests[0].shape[0] - rows if finish else 0
    tall = rows + extra * len(guests)
    blocks = sides if finish else 2
    block = pl.BlockSpec((blocks * rows, HEAD), lambda k: (k, 0))
    asked = pl.BlockSpec((blocks, rows, HEAD), lambda k: (k, 0, 0))
    whole = pl.BlockSpec((rows, 2 * HEAD), lambda k: (0, 0))
    start = state is None
    state = () if start else state
    if finish:
        shapes = jax.ShapeDtypeStruct((sides, tall, 2 * HEAD), BF)
        outs = pl.BlockSpec((blocks, tall, 2 * HEAD), lambda k: (k, 0, 0))
    else:
        shapes = (jax.ShapeDtypeStruct((sides * rows, HEAD), F32),) * 3
        outs = (block,) * 3
    return pl.pallas_call(
        functools.partial(attend_kernel, count=len(packets), start=start, hosted=len(guests)),
        grid=(sides // blocks,),
        in_specs=[pl.BlockSpec(memory_space=pltpu.SMEM), asked]
        + [whole] * len(packets)
        + [block] * len(state)
        + [pl.BlockSpec((extra, 2 * HEAD), lambda k: (rows // extra, 0))] * len(guests),
        out_specs=outs,
        out_shape=shapes,
        name="attend",
    )(spots, queries, *packets, *state, *guests)


def body(
    patch_queries,
    patch_keys,
    patch_values,
    patch_tasks,
    residual,
    output_weight,
    global_down,
    global_up,
    global_scales,
    local_weight,
    byte_ids,
    byte_table,
    position_table,
    norm_gain,
    hidden_in,
    hidden_out,
    local_down,
    local_up,
    local_scales,
    cotangent,
):
    rows, width = patch_queries.shape
    ring = lax.axis_size(Z)
    row_count = lax.axis_size(ROW)
    z = lax.axis_index(Z)
    near = lax.axis_index(NEAR)
    far = lax.axis_index(FAR)
    side = lax.axis_index(SIDE)
    line = lax.axis_size(LINE)
    core = lax.axis_index(CORE)
    row_index = lax.axis_index(ROW)
    columns = local_weight.shape[1]
    units = hidden_in.shape[0]
    share = hidden_in.shape[1]

    def head(array, which):
        return lax.dynamic_slice_in_dim(array, which * HEAD, HEAD, 1)

    trio = (patch_queries, patch_keys, patch_values)
    mine = jnp.concatenate([head(a, core) for a in trio], axis=1)
    other = jnp.concatenate([head(a, 1 - core) for a in trio], axis=1)
    hidden = jnp.concatenate([hidden_in.T, hidden_out.T], axis=0)
    other, *early = lax.optimization_barrier((other, local_weight, global_up, local_up))
    weights = jnp.concatenate([early[0], fold(early[1]), fold(early[2])], axis=0)
    weights = lax.all_gather(weights, ROW, axis=0, tiled=False)
    cotangents = jnp.concatenate([cotangent, lax.ppermute(cotangent, SIDE, SWAP)], axis=0)

    both = jnp.concatenate([mine, lax.ppermute(other, CORE, SWAP)], axis=0)
    chip_rows = 2 * rows
    packet = both[:, HEAD:]
    packet = jnp.concatenate([packet, hidden], axis=0)
    queries = to_everyone(both[:, :HEAD], QUAD)
    sides = lax.axis_size(QUAD)

    up = [(i, (i + 1) % ring) for i in range(ring)]
    down = [(i, (i - 1) % ring) for i in range(ring)]

    rising = falling = packet
    held, at = [packet], [z]
    for step in range(1, ring // 2 + 1):
        rising = lax.ppermute(rising, Z, up)
        held.append(rising)
        at.append(z - step)
        if step < ring // 2:
            falling = lax.ppermute(falling, Z, down)
            held.append(falling)
            at.append(z + step)
        if step == 1:
            rising, falling, queries = lax.optimization_barrier((rising, falling, queries))
    at = [k % ring for k in at]
    spots = jnp.stack([z * sides] + [k * sides + near * 2 + far for k in at]).astype(jnp.int32)
    spots = jnp.concatenate([core.astype(jnp.int32)[None], spots])
    state = attend(spots, queries, held[:-1], None, [], chip_rows)
    state, last, weights = lax.optimization_barrier((state, held[-1], weights))
    spots = jnp.concatenate([spots[:2], spots[-1:], jnp.stack(at).astype(jnp.int32)])
    met = attend(spots, queries, [last], state, held[:-1] + [last], chip_rows)

    local_whole = weights[:, :width].reshape(-1, columns)
    up_whole = unfold(weights[:, width : width + 8])
    up_whole = jnp.transpose(up_whole, (1, 0, 2)).reshape(RANK, -1)
    local_ups = unfold(weights[:, width + 8 :]).reshape(line, 2, RANK, units)
    local_ups = lax.dynamic_index_in_dim(local_ups, side, 1, keepdims=False)

    met = exchange(met, QUAD)
    riders = met[:, chip_rows:].reshape(-1, units)
    riders = lax.all_gather(riders, LINE, axis=0, tiled=False)
    met = met[:, :chip_rows].astype(F32)
    levels = met[:, :, 128:129] + met[:, :, 160:161] + met[:, :, 192:193]
    parts = jnp.exp(levels - jnp.max(levels, axis=0, keepdims=True))
    merged = (parts * met[:, :, :HEAD]).sum(axis=0) / parts.sum(axis=0)
    merged = merged.astype(BF)
    partner = lax.ppermute(merged[rows:], CORE, SWAP)
    attended = in_pair_order(merged[:rows], partner, core, 1)

    task_scales = select_rows(global_scales, patch_tasks)
    part = contract(output_weight, attended, 0, 1).astype(BF).reshape(row_count, width, rows)
    low_part = contract(global_down, attended, 0, 1).astype(BF)
    low_part = jnp.broadcast_to(low_part[None], (row_count, RANK, rows))
    arrived = exchange(jnp.concatenate([part, low_part], axis=1), ROW)
    arrived = arrived.astype(F32).sum(axis=0)

    reduced = jnp.transpose(arrived[width:])
    scaled = (reduced * task_scales).astype(BF)
    mixed = arrived[:width] + jnp.transpose(residual.astype(F32)) + contract(global_up, scaled, 0, 1)
    mixed_b = mixed.astype(BF)
    own_patches = rows // row_count
    own_bytes = own_patches * PATCH
    own_tasks = lax.dynamic_slice_in_dim(patch_tasks, row_index * own_patches, own_patches)
    own_ids = lax.dynamic_slice_in_dim(byte_ids, row_index * own_bytes, own_bytes)
    projected = contract(mixed_b, local_weight, 0, 0).astype(BF)
    projected = exchange(projected.reshape(row_count, own_patches, columns), ROW)
    projected, riders = lax.optimization_barrier((projected, riders))
    projected = total(projected).astype(BF)

    rest = lax.ppermute(riders, CORE, SWAP)
    split = (line, sides, ring, 2, 1, share, units)
    riders = in_pair_order(riders.reshape(split), rest.reshape(split), core, 4)
    riders = jnp.transpose(riders, (3, 0, 2, 1, 4, 5, 6)).reshape(2, line, columns, units)
    rows_in, rows_out = riders[0], riders[1]
    lanes = 128
    spare_rows = jnp.zeros((line, lanes - RANK, units), BF)
    stacked = jnp.concatenate([rows_in, local_ups, spare_rows], axis=1)

    picks = (own_ids[:, None] == jnp.arange(VOCAB, dtype=jnp.int32)[None, :]).astype(BF)
    embedded = jnp.dot(picks, byte_table, preferred_element_type=F32)
    embedded = embedded.reshape(own_patches, PATCH, -1) + position_table.astype(F32)[None]
    inputs = (embedded + projected.astype(F32)[:, None, :]).reshape(own_bytes, columns)
    inverse = lax.rsqrt(jnp.mean(inputs * inputs, axis=1, keepdims=True) + 1e-06)
    normed = (inputs * inverse * norm_gain).astype(BF)
    lowered = jnp.dot(normed, local_down, preferred_element_type=F32)
    byte_tasks = jnp.repeat(own_tasks, PATCH)
    scales = select_rows(local_scales, byte_tasks)
    shrunk = (lowered * scales).astype(BF)
    joined = jnp.concatenate(
        [normed, shrunk, jnp.zeros((own_bytes, lanes - RANK), BF)], axis=1
    )
    joined = jnp.concatenate([joined, lax.ppermute(joined, SIDE, SWAP)], axis=0)
    through = contract(cotangents, rows_out, 1, 1)
    upper = contract(joined, stacked, 1, 1)
    grown = (through * gelu_slope(upper)).astype(BF)
    back = lax.dot_general(
        grown, stacked, (((1, 2), (0, 2)), ((), ())), preferred_element_type=F32
    )
    back = back[:own_bytes] + lax.ppermute(back[own_bytes:].astype(BF), SIDE, SWAP).astype(F32)
    ups = contract(joined[:, columns:], grown, 0, 0)[:RANK].astype(BF)
    back_norm = back[:, :columns]
    back_rank = back[:, columns : columns + RANK]
    grad_local_scales = task_totals(byte_tasks, back_rank * lowered)
    moved = (back_rank * scales).astype(BF)
    grad_local_down = contract(moved, normed, 0, 0)
    back_total = back_norm + contract(moved, local_down, 1, 1)
    gained = back_total * norm_gain
    average = jnp.mean(gained * inputs, axis=1, keepdims=True)
    back_inputs = cotangent.astype(F32) + inverse * (
        gained - inputs * inverse * inverse * average
    )
    patch_grad = back_inputs.reshape(own_patches, PATCH, -1).sum(axis=1)
    patch_grad = lax.optimization_barrier(patch_grad).astype(BF)

    spare = jnp.zeros((TASKS, columns - RANK), F32)
    local_rows = jnp.concatenate([grad_local_scales, spare], axis=1)
    local_rows = jnp.concatenate([grad_local_down, local_rows, jnp.zeros_like(local_rows)])
    row_pack = jnp.concatenate([patch_grad, local_rows.astype(BF)], axis=0)
    row_pack = jnp.broadcast_to(row_pack[None], (row_count, *row_pack.shape))
    ups = jnp.transpose(ups, (1, 0, 2))
    ups = jnp.stack([jnp.where(side == k, ups, jnp.zeros_like(ups)) for k in range(2)], axis=1)
    ups = jnp.pad(ups.reshape(row_count, RANK, units), [(0, 0), (0, 0), (0, columns - units)])
    row_pack = exchange(jnp.concatenate([row_pack, ups], axis=1), ROW)
    patch_grads = row_pack[:, :own_patches].reshape(rows, columns)
    local_sums = total(row_pack[:, own_patches:])
    back_mixed = contract(patch_grads, local_weight, 1, 1).astype(BF)
    back_whole = contract(patch_grads, local_whole, 1, 1).astype(BF)
    back_scaled = contract(back_whole, up_whole, 1, 1)
    grad_global_up = contract(scaled, back_mixed, 0, 0)
    grad_global_scales = task_totals(patch_tasks, back_scaled * reduced)
    back_reduced = (back_scaled * task_scales).astype(BF)
    grad_global_down = contract(back_reduced, attended, 0, 0)

    small = jnp.concatenate([grad_global_scales, jnp.zeros((TASKS, width - RANK), F32)], axis=1)
    small_local = local_sums[RANK : RANK + TASKS, :width]
    packed = jnp.concatenate(
        [
            grad_global_down,
            grad_global_up,
            local_sums[2 * RANK :, :units],
            local_sums[:RANK, :width],
            local_sums[:RANK, width:],
            small,
            small_local,
        ]
    ).astype(BF)
    shape = packed.shape
    pieces = packed.reshape(lax.axis_size(EIGHT), -1, shape[1])
    pieces = total(exchange(pieces, EIGHT)).astype(BF)
    pieces = total(to_everyone(pieces, Z)).astype(BF)
    packed = to_everyone(pieces, EIGHT).reshape(shape).astype(F32)
    return (
        jnp.transpose(packed[:16]),
        packed[16:32],
        packed[80:88, :RANK],
        jnp.transpose(jnp.concatenate([packed[48:64], packed[64:80]], axis=1)),
        packed[32:48],
        packed[88:96, :RANK],
    )


def solution(mesh):
    torus = Mesh(mesh.devices.reshape(8, 2, 2, 2, 4, 2), SEQ_ROW)
    placed = (
        P(SEQ, ROW),
        P(SEQ, ROW),
        P(SEQ, ROW),
        P(SEQ),
        P(SEQ, ROW),
        P(ROW, None),
        P(ROW, None),
        P(None, ROW),
        P(),
        P(ROW, None),
        P(SEQ),
        P(),
        P(),
        P(),
        P(ROW, SEQ),
        P(ROW, SEQ),
        P(),
        P(None, ROW),
        P(),
        P(SEQ_ROW, None),
    )
    return jax.shard_map(
        body,
        mesh=torus,
        in_specs=placed,
        out_specs=(P(ROW, None), P(None, ROW), P(), P(), P(None, ROW), P()),
        check_vma=False,
    )
```

```python
import functools
import math

import jax
import jax.numpy as jnp
from jax import lax
from jax.experimental import pallas as pl
from jax.experimental.pallas import tpu as pltpu
from jax.sharding import Mesh
from jax.sharding import PartitionSpec as P

HEAD = 128
VOCAB = 256
PATCH = 8
TASKS = 8
RANK = 16
ROW = ("row_0", "row_1")
SEQ = ("seq_0", "near", "seq_1", "seq_2")
Z, NEAR, FAR, CORE = SEQ
QUAD = (NEAR, FAR)
EIGHT = (NEAR, FAR, CORE)
LINE, SIDE = ROW
SEQ_ROW = SEQ + ROW
SWAP = [(0, 1), (1, 0)]
BF = jnp.bfloat16
F32 = jnp.float32


def exchange(pieces, axis):
    return lax.all_to_all(pieces, axis, split_axis=0, concat_axis=0, tiled=True)


def to_everyone(array, axis):
    size = lax.axis_size(axis)
    return exchange(jnp.broadcast_to(array[None], (size, *array.shape)), axis)


def contract(left, right, left_dim, right_dim):
    return lax.dot_general(
        left, right, (((left_dim,), (right_dim,)), ((), ())), preferred_element_type=F32
    )


def select_rows(table, tasks):
    picks = (tasks[:, None] == jnp.arange(table.shape[0], dtype=jnp.int32)[None, :]).astype(F32)
    return jnp.dot(picks, table, precision=lax.Precision.HIGHEST)


def task_totals(tasks, values):
    picks = (tasks[:, None] == jnp.arange(TASKS, dtype=jnp.int32)[None, :]).astype(F32)
    return lax.dot_general(picks, values, (((0,), (0,)), ((), ())), precision=lax.Precision.HIGHEST)


def gelu_slope(upper):
    cumulative = 0.5 * (1.0 + lax.erf(upper * 0.7071067811865476))
    density = jnp.exp(-0.5 * upper * upper) * 0.3989422804014327
    return cumulative + upper * density


def in_pair_order(mine, other, place, axis):
    first = jnp.where(place == 0, mine, other)
    second = jnp.where(place == 0, other, mine)
    return jnp.concatenate([first, second], axis=axis)


def total(array):
    return lax.optimization_barrier(array.astype(F32).sum(axis=0))


def fold(array):
    array = jnp.concatenate([array[:, :128], array[:, 128:]], axis=0)
    return jnp.concatenate([array[8 * k : 8 * k + 8] for k in range(4)], axis=1)


def unfold(array):
    array = jnp.concatenate([array[:, :, 128 * k : 128 * k + 128] for k in range(4)], axis=1)
    return jnp.concatenate([array[:, :RANK], array[:, RANK:]], axis=2)


def attend_kernel(spots, queries, *refs, count, start, hosted):
    finish = hosted > 0
    packets, refs = refs[:count], refs[count:]
    blocks, rows = queries.shape[:2]
    half = rows // 2
    core = spots[0]
    state_in = () if start else refs[:3]
    refs = refs[len(state_in) :]
    guests, refs = refs[:hosted], refs[hosted:]

    def inside(shape, dim):
        at = lax.broadcasted_iota(jnp.int32, shape, dim)
        return jnp.where(at < half, at + core * half, at - core * half)

    for block in range(blocks):
        here = pl.ds(block * rows, rows)
        if start:
            top = jnp.full((rows, 1), -1e20, F32)
            mass = jnp.zeros((rows, HEAD), F32)
            out = jnp.zeros((rows, HEAD), F32)
        else:
            top = state_in[0][here, :1]
            mass, out = state_in[1][here, :], state_in[2][here, :]
        place = spots[1] + pl.program_id(0) * blocks + block
        query_places = place * rows + inside((rows, 1), 0)
        own = queries[block]
        for index in range(count):
            keys = packets[index][:, :HEAD]
            values = packets[index][:, HEAD:]
            key_places = spots[2 + index] * rows + inside((1, rows), 1)
            scores = contract(own, keys, 1, 1) * (1.0 / math.sqrt(HEAD))
            scores = jnp.where(key_places <= query_places, scores, -1e30)
            new_top = jnp.maximum(top, jnp.max(scores, axis=1, keepdims=True))
            weights = jnp.exp(scores - new_top)
            shrink = jnp.exp(top - new_top)
            mass = mass * shrink + (weights[:, :HEAD] + weights[:, HEAD:])
            out = out * shrink + jnp.dot(weights.astype(BF), values, preferred_element_type=F32)
            top = new_top
        if not finish:
            refs[0][here, :] = jnp.broadcast_to(top, (rows, HEAD))
            refs[1][here, :] = mass
            refs[2][here, :] = out
            continue
        mass = jnp.sum(mass, axis=1, keepdims=True)
        safe = jnp.where(mass > 0, mass, 1.0)
        level = jnp.where(mass > 0, top + jnp.log(safe), -1e30)
        level = jnp.transpose(jnp.broadcast_to(level, (rows, HEAD)))[:16]
        high = level.astype(BF).astype(F32)
        middle = (level - high).astype(BF).astype(F32)
        low = level - high - middle
        line = lax.broadcasted_iota(jnp.int32, level.shape, 0)
        level = jnp.where(line == 0, high, jnp.where(line == 1, middle, low))
        out = (out / safe).astype(BF)
        refs[0][block, :half, :HEAD] = out[:half]
        refs[0][block, :half, HEAD:] = out[half:]
        refs[0][block, half : half + 16, :] = level.astype(BF)
        for index, guest in enumerate(guests):
            extra = guest.shape[0]
            spot = pl.multiple_of(half + 16 + spots[2 + count + index] * extra, extra)
            refs[0][block, pl.ds(spot, extra), :] = guest[...]


def attend(spots, queries, packets, state, guests, rows):
    sides = queries.shape[0]
    finish = len(guests) > 0
    extra = guests[0].shape[0] - rows if finish else 0
    tall = rows // 2 + 16 + extra * len(guests)
    blocks = sides if finish else 2
    block = pl.BlockSpec((blocks * rows, HEAD), lambda k: (k, 0))
    asked = pl.BlockSpec((blocks, rows, HEAD), lambda k: (k, 0, 0))
    whole = pl.BlockSpec((rows, 2 * HEAD), lambda k: (0, 0))
    start = state is None
    state = () if start else state
    if finish:
        shapes = jax.ShapeDtypeStruct((sides, tall, 2 * HEAD), BF)
        outs = pl.BlockSpec((blocks, tall, 2 * HEAD), lambda k: (k, 0, 0))
    else:
        shapes = (jax.ShapeDtypeStruct((sides * rows, HEAD), F32),) * 3
        outs = (block,) * 3
    return pl.pallas_call(
        functools.partial(attend_kernel, count=len(packets), start=start, hosted=len(guests)),
        grid=(sides // blocks,),
        in_specs=[pl.BlockSpec(memory_space=pltpu.SMEM), asked]
        + [whole] * len(packets)
        + [block] * len(state)
        + [pl.BlockSpec((extra, 2 * HEAD), lambda k: (rows // extra, 0))] * len(guests),
        out_specs=outs,
        out_shape=shapes,
        name="attend",
    )(spots, queries, *packets, *state, *guests)


def body(
    patch_queries,
    patch_keys,
    patch_values,
    patch_tasks,
    residual,
    output_weight,
    global_down,
    global_up,
    global_scales,
    local_weight,
    byte_ids,
    byte_table,
    position_table,
    norm_gain,
    hidden_in,
    hidden_out,
    local_down,
    local_up,
    local_scales,
    cotangent,
):
    rows, width = patch_queries.shape
    ring = lax.axis_size(Z)
    row_count = lax.axis_size(ROW)
    z = lax.axis_index(Z)
    near = lax.axis_index(NEAR)
    far = lax.axis_index(FAR)
    side = lax.axis_index(SIDE)
    line = lax.axis_size(LINE)
    core = lax.axis_index(CORE)
    row_index = lax.axis_index(ROW)
    columns = local_weight.shape[1]
    units = hidden_in.shape[0]
    share = hidden_in.shape[1]

    def head(array, which):
        return lax.dynamic_slice_in_dim(array, which * HEAD, HEAD, 1)

    trio = (patch_queries, patch_keys, patch_values)
    mine = jnp.concatenate([head(a, core) for a in trio], axis=1)
    other = jnp.concatenate([head(a, 1 - core) for a in trio], axis=1)
    hidden = jnp.concatenate([hidden_in.T, hidden_out.T], axis=0)
    other, *early = lax.optimization_barrier((other, local_weight, global_up, local_up))
    weights = jnp.concatenate([early[0], fold(early[1]), fold(early[2])], axis=0)
    weights = lax.all_gather(weights, ROW, axis=0, tiled=False)
    cotangents = jnp.concatenate([cotangent, lax.ppermute(cotangent, SIDE, SWAP)], axis=0)

    both = jnp.concatenate([mine, lax.ppermute(other, CORE, SWAP)], axis=0)
    chip_rows = 2 * rows
    packet = both[:, HEAD:]
    packet = jnp.concatenate([packet, hidden], axis=0)
    queries = to_everyone(both[:, :HEAD], QUAD)
    sides = lax.axis_size(QUAD)

    up = [(i, (i + 1) % ring) for i in range(ring)]
    down = [(i, (i - 1) % ring) for i in range(ring)]

    rising = falling = packet
    held, at = [packet], [z]
    for step in range(1, ring // 2 + 1):
        rising = lax.ppermute(rising, Z, up)
        held.append(rising)
        at.append(z - step)
        if step < ring // 2:
            falling = lax.ppermute(falling, Z, down)
            held.append(falling)
            at.append(z + step)
        if step == 1:
            rising, falling, queries = lax.optimization_barrier((rising, falling, queries))
    at = [k % ring for k in at]
    spots = jnp.stack([z * sides] + [k * sides + near * 2 + far for k in at]).astype(jnp.int32)
    spots = jnp.concatenate([core.astype(jnp.int32)[None], spots])
    state = attend(spots, queries, held[:-1], None, [], chip_rows)
    state, last = lax.optimization_barrier((state, held[-1]))
    spots = jnp.concatenate([spots[:2], spots[-1:], jnp.stack(at).astype(jnp.int32)])
    met = attend(spots, queries, [last], state, held[:-1] + [last], chip_rows)

    met = exchange(met, QUAD)
    riders = met[:, rows + 16 :].reshape(-1, units)
    riders = lax.all_gather(riders, LINE, axis=0, tiled=False)
    levels = met[:, rows : rows + 3].astype(F32).sum(axis=1)[:, :, None]
    met = jnp.concatenate([met[:, :rows, :HEAD], met[:, :rows, HEAD:]], axis=1).astype(F32)
    parts = jnp.exp(levels - jnp.max(levels, axis=0, keepdims=True))
    merged = (parts * met).sum(axis=0) / parts.sum(axis=0)
    merged = merged.astype(BF)
    merged, weights = lax.optimization_barrier((merged, weights))
    partner = lax.ppermute(merged[rows:], CORE, SWAP)
    attended = in_pair_order(merged[:rows], partner, core, 1)

    local_whole = weights[:, :width].reshape(-1, columns)
    up_whole = unfold(weights[:, width : width + 8])
    up_whole = jnp.transpose(up_whole, (1, 0, 2)).reshape(RANK, -1)
    local_ups = unfold(weights[:, width + 8 :]).reshape(line, 2, RANK, units)
    local_ups = lax.dynamic_index_in_dim(local_ups, side, 1, keepdims=False)

    task_scales = select_rows(global_scales, patch_tasks)
    part = contract(output_weight, attended, 0, 1).astype(BF).reshape(row_count, width, rows)
    low_part = contract(global_down, attended, 0, 1).astype(BF)
    low_part = jnp.broadcast_to(low_part[None], (row_count, RANK, rows))
    arrived = exchange(jnp.concatenate([part, low_part], axis=1), ROW)
    arrived = arrived.astype(F32).sum(axis=0)

    reduced = jnp.transpose(arrived[width:])
    scaled = (reduced * task_scales).astype(BF)
    mixed = arrived[:width] + jnp.transpose(residual.astype(F32)) + contract(global_up, scaled, 0, 1)
    mixed_b = mixed.astype(BF)
    own_patches = rows // row_count
    own_bytes = own_patches * PATCH
    own_tasks = lax.dynamic_slice_in_dim(patch_tasks, row_index * own_patches, own_patches)
    own_ids = lax.dynamic_slice_in_dim(byte_ids, row_index * own_bytes, own_bytes)
    projected = contract(mixed_b, local_weight, 0, 0).astype(BF)
    projected = exchange(projected.reshape(row_count, own_patches, columns), ROW)
    projected, riders = lax.optimization_barrier((projected, riders))
    projected = total(projected).astype(BF)

    rest = lax.ppermute(riders, CORE, SWAP)
    split = (line, sides, ring, 2, 1, share, units)
    riders = in_pair_order(riders.reshape(split), rest.reshape(split), core, 4)
    riders = jnp.transpose(riders, (3, 0, 2, 1, 4, 5, 6)).reshape(2, line, columns, units)
    rows_in, rows_out = riders[0], riders[1]
    lanes = 128
    spare_rows = jnp.zeros((line, lanes - RANK, units), BF)
    stacked = jnp.concatenate([rows_in, local_ups, spare_rows], axis=1)

    picks = (own_ids[:, None] == jnp.arange(VOCAB, dtype=jnp.int32)[None, :]).astype(BF)
    embedded = jnp.dot(picks, byte_table, preferred_element_type=F32)
    embedded = embedded.reshape(own_patches, PATCH, -1) + position_table.astype(F32)[None]
    inputs = (embedded + projected.astype(F32)[:, None, :]).reshape(own_bytes, columns)
    inverse = lax.rsqrt(jnp.mean(inputs * inputs, axis=1, keepdims=True) + 1e-06)
    normed = (inputs * inverse * norm_gain).astype(BF)
    lowered = jnp.dot(normed, local_down, preferred_element_type=F32)
    byte_tasks = jnp.repeat(own_tasks, PATCH)
    scales = select_rows(local_scales, byte_tasks)
    shrunk = (lowered * scales).astype(BF)
    joined = jnp.concatenate(
        [normed, shrunk, jnp.zeros((own_bytes, lanes - RANK), BF)], axis=1
    )
    joined = jnp.concatenate([joined, lax.ppermute(joined, SIDE, SWAP)], axis=0)
    through = contract(cotangents, rows_out, 1, 1)
    upper = contract(joined, stacked, 1, 1)
    grown = (through * gelu_slope(upper)).astype(BF)
    back = lax.dot_general(
        grown, stacked, (((1, 2), (0, 2)), ((), ())), preferred_element_type=F32
    )
    back = back[:own_bytes] + lax.ppermute(back[own_bytes:].astype(BF), SIDE, SWAP).astype(F32)
    ups = contract(joined[:, columns:], grown, 0, 0)[:RANK].astype(BF)
    back_norm = back[:, :columns]
    back_rank = back[:, columns : columns + RANK]
    grad_local_scales = task_totals(byte_tasks, back_rank * lowered)
    moved = (back_rank * scales).astype(BF)
    grad_local_down = contract(moved, normed, 0, 0)
    back_total = back_norm + contract(moved, local_down, 1, 1)
    gained = back_total * norm_gain
    average = jnp.mean(gained * inputs, axis=1, keepdims=True)
    back_inputs = cotangent.astype(F32) + inverse * (
        gained - inputs * inverse * inverse * average
    )
    patch_grad = back_inputs.reshape(own_patches, PATCH, -1).sum(axis=1)
    patch_grad = lax.optimization_barrier(patch_grad).astype(BF)

    spare = jnp.zeros((TASKS, columns - RANK), F32)
    local_rows = jnp.concatenate([grad_local_scales, spare], axis=1)
    local_rows = jnp.concatenate([grad_local_down, local_rows, jnp.zeros_like(local_rows)])
    row_pack = jnp.concatenate([patch_grad, local_rows.astype(BF)], axis=0)
    row_pack = jnp.broadcast_to(row_pack[None], (row_count, *row_pack.shape))
    ups = jnp.transpose(ups, (1, 0, 2))
    ups = jnp.stack([jnp.where(side == k, ups, jnp.zeros_like(ups)) for k in range(2)], axis=1)
    ups = jnp.pad(ups.reshape(row_count, RANK, units), [(0, 0), (0, 0), (0, columns - units)])
    row_pack = exchange(jnp.concatenate([row_pack, ups], axis=1), ROW)
    patch_grads = row_pack[:, :own_patches].reshape(rows, columns)
    local_sums = total(row_pack[:, own_patches:])
    back_mixed = contract(patch_grads, local_weight, 1, 1).astype(BF)
    back_whole = contract(patch_grads, local_whole, 1, 1).astype(BF)
    back_scaled = contract(back_whole, up_whole, 1, 1)
    grad_global_up = contract(scaled, back_mixed, 0, 0)
    grad_global_scales = task_totals(patch_tasks, back_scaled * reduced)
    back_reduced = (back_scaled * task_scales).astype(BF)
    grad_global_down = contract(back_reduced, attended, 0, 0)

    small = jnp.concatenate([grad_global_scales, jnp.zeros((TASKS, width - RANK), F32)], axis=1)
    small_local = local_sums[RANK : RANK + TASKS, :width]
    packed = jnp.concatenate(
        [
            grad_global_down,
            grad_global_up,
            local_sums[2 * RANK :, :units],
            local_sums[:RANK, :width],
            local_sums[:RANK, width:],
            small,
            small_local,
        ]
    ).astype(BF)
    shape = packed.shape
    pieces = packed.reshape(lax.axis_size(EIGHT), -1, shape[1])
    pieces = total(exchange(pieces, EIGHT)).astype(BF)
    pieces = total(to_everyone(pieces, Z)).astype(BF)
    packed = to_everyone(pieces, EIGHT).reshape(shape).astype(F32)
    return (
        jnp.transpose(packed[:16]),
        packed[16:32],
        packed[80:88, :RANK],
        jnp.transpose(jnp.concatenate([packed[48:64], packed[64:80]], axis=1)),
        packed[32:48],
        packed[88:96, :RANK],
    )


def solution(mesh):
    torus = Mesh(mesh.devices.reshape(8, 2, 2, 2, 4, 2), SEQ_ROW)
    placed = (
        P(SEQ, ROW),
        P(SEQ, ROW),
        P(SEQ, ROW),
        P(SEQ),
        P(SEQ, ROW),
        P(ROW, None),
        P(ROW, None),
        P(None, ROW),
        P(),
        P(ROW, None),
        P(SEQ),
        P(),
        P(),
        P(),
        P(ROW, SEQ),
        P(ROW, SEQ),
        P(),
        P(None, ROW),
        P(),
        P(SEQ_ROW, None),
    )
    return jax.shard_map(
        body,
        mesh=torus,
        in_specs=placed,
        out_specs=(P(ROW, None), P(None, ROW), P(), P(), P(None, ROW), P()),
        check_vma=False,
    )
```

```python
import functools
import math

import jax
import jax.numpy as jnp
from jax import lax
from jax.experimental import pallas as pl
from jax.experimental.pallas import tpu as pltpu
from jax.sharding import Mesh
from jax.sharding import PartitionSpec as P

HEAD = 128
VOCAB = 256
PATCH = 8
TASKS = 8
RANK = 16
ROW = ("row_0", "row_1")
SEQ = ("seq_0", "near", "seq_1", "seq_2")
Z, NEAR, FAR, CORE = SEQ
QUAD = (NEAR, FAR)
CHIPS = (FAR, CORE)
LINE, SIDE = ROW
SEQ_ROW = SEQ + ROW
SWAP = [(0, 1), (1, 0)]
BF = jnp.bfloat16
F32 = jnp.float32


def exchange(pieces, axis):
    return lax.all_to_all(pieces, axis, split_axis=0, concat_axis=0, tiled=True)


def to_everyone(array, axis):
    size = lax.axis_size(axis)
    return exchange(jnp.broadcast_to(array[None], (size, *array.shape)), axis)


def contract(left, right, left_dim, right_dim):
    return lax.dot_general(
        left, right, (((left_dim,), (right_dim,)), ((), ())), preferred_element_type=F32
    )


def select_rows(table, tasks):
    picks = (tasks[:, None] == jnp.arange(table.shape[0], dtype=jnp.int32)[None, :]).astype(F32)
    return jnp.dot(picks, table, precision=lax.Precision.HIGHEST)


def task_totals(tasks, values):
    picks = (tasks[:, None] == jnp.arange(TASKS, dtype=jnp.int32)[None, :]).astype(F32)
    return lax.dot_general(picks, values, (((0,), (0,)), ((), ())), precision=lax.Precision.HIGHEST)


def gelu_slope(upper):
    cumulative = 0.5 * (1.0 + lax.erf(upper * 0.7071067811865476))
    density = jnp.exp(-0.5 * upper * upper) * 0.3989422804014327
    return cumulative + upper * density


def in_pair_order(mine, other, place, axis):
    first = jnp.where(place == 0, mine, other)
    second = jnp.where(place == 0, other, mine)
    return jnp.concatenate([first, second], axis=axis)


def total(array):
    return lax.optimization_barrier(array.astype(F32).sum(axis=0))


def fold(array):
    array = jnp.concatenate([array[:, :128], array[:, 128:]], axis=0)
    return jnp.concatenate([array[8 * k : 8 * k + 8] for k in range(4)], axis=1)


def unfold(array):
    array = jnp.concatenate([array[:, :, 128 * k : 128 * k + 128] for k in range(4)], axis=1)
    return jnp.concatenate([array[:, :RANK], array[:, RANK:]], axis=2)


def attend_kernel(spots, queries, *refs, count, start, hosted):
    finish = hosted > 0
    packets, refs = refs[:count], refs[count:]
    blocks, rows = queries.shape[:2]
    half = rows // 2
    core = spots[0]
    state_in = () if start else refs[:3]
    refs = refs[len(state_in) :]
    guests, refs = refs[:hosted], refs[hosted:]

    def inside(shape, dim):
        at = lax.broadcasted_iota(jnp.int32, shape, dim)
        return jnp.where(at < half, at + core * half, at - core * half)

    for block in range(blocks):
        here = pl.ds(block * rows, rows)
        if start:
            top = jnp.full((rows, 1), -1e20, F32)
            mass = jnp.zeros((rows, HEAD), F32)
            out = jnp.zeros((rows, HEAD), F32)
        else:
            top = state_in[0][here, :1]
            mass, out = state_in[1][here, :], state_in[2][here, :]
        place = spots[1] + pl.program_id(0) * blocks + block
        query_places = place * rows + inside((rows, 1), 0)
        own = queries[block]
        for index in range(count):
            keys = packets[index][:, :HEAD]
            values = packets[index][:, HEAD:]
            key_places = spots[2 + index] * rows + inside((1, rows), 1)
            scores = contract(own, keys, 1, 1) * (1.0 / math.sqrt(HEAD))
            scores = jnp.where(key_places <= query_places, scores, -1e30)
            new_top = jnp.maximum(top, jnp.max(scores, axis=1, keepdims=True))
            weights = jnp.exp(scores - new_top)
            shrink = jnp.exp(top - new_top)
            mass = mass * shrink + (weights[:, :HEAD] + weights[:, HEAD:])
            out = out * shrink + jnp.dot(weights.astype(BF), values, preferred_element_type=F32)
            top = new_top
        if not finish:
            refs[0][here, :] = jnp.broadcast_to(top, (rows, HEAD))
            refs[1][here, :] = mass
            refs[2][here, :] = out
            continue
        mass = jnp.sum(mass, axis=1, keepdims=True)
        safe = jnp.where(mass > 0, mass, 1.0)
        level = jnp.where(mass > 0, top + jnp.log(safe), -1e30)
        level = jnp.transpose(jnp.broadcast_to(level, (rows, HEAD)))[:16]
        high = level.astype(BF).astype(F32)
        middle = (level - high).astype(BF).astype(F32)
        low = level - high - middle
        line = lax.broadcasted_iota(jnp.int32, level.shape, 0)
        level = jnp.where(line == 0, high, jnp.where(line == 1, middle, low))
        out = (out / safe).astype(BF)
        refs[0][block, :half, :HEAD] = out[:half]
        refs[0][block, :half, HEAD:] = out[half:]
        refs[0][block, half : half + 16, :] = level.astype(BF)
        for index, guest in enumerate(guests):
            extra = guest.shape[0]
            spot = pl.multiple_of(half + 16 + spots[2 + count + index] * extra, extra)
            refs[0][block, pl.ds(spot, extra), :] = guest[...]


def attend(spots, queries, packets, state, guests, rows):
    sides = queries.shape[0]
    finish = len(guests) > 0
    extra = guests[0].shape[0] - rows if finish else 0
    tall = rows // 2 + 16 + extra * len(guests)
    blocks = sides if finish else 2
    block = pl.BlockSpec((blocks * rows, HEAD), lambda k: (k, 0))
    asked = pl.BlockSpec((blocks, rows, HEAD), lambda k: (k, 0, 0))
    whole = pl.BlockSpec((rows, 2 * HEAD), lambda k: (0, 0))
    start = state is None
    state = () if start else state
    if finish:
        shapes = jax.ShapeDtypeStruct((sides, tall, 2 * HEAD), BF)
        outs = pl.BlockSpec((blocks, tall, 2 * HEAD), lambda k: (k, 0, 0))
    else:
        shapes = (jax.ShapeDtypeStruct((sides * rows, HEAD), F32),) * 3
        outs = (block,) * 3
    return pl.pallas_call(
        functools.partial(attend_kernel, count=len(packets), start=start, hosted=len(guests)),
        grid=(sides // blocks,),
        in_specs=[pl.BlockSpec(memory_space=pltpu.SMEM), asked]
        + [whole] * len(packets)
        + [block] * len(state)
        + [pl.BlockSpec((extra, 2 * HEAD), lambda k: (rows // extra, 0))] * len(guests),
        out_specs=outs,
        out_shape=shapes,
        name="attend",
    )(spots, queries, *packets, *state, *guests)


def body(
    patch_queries,
    patch_keys,
    patch_values,
    patch_tasks,
    residual,
    output_weight,
    global_down,
    global_up,
    global_scales,
    local_weight,
    byte_ids,
    byte_table,
    position_table,
    norm_gain,
    hidden_in,
    hidden_out,
    local_down,
    local_up,
    local_scales,
    cotangent,
):
    rows, width = patch_queries.shape
    ring = lax.axis_size(Z)
    row_count = lax.axis_size(ROW)
    z = lax.axis_index(Z)
    near = lax.axis_index(NEAR)
    far = lax.axis_index(FAR)
    side = lax.axis_index(SIDE)
    line = lax.axis_size(LINE)
    core = lax.axis_index(CORE)
    row_index = lax.axis_index(ROW)
    columns = local_weight.shape[1]
    units = hidden_in.shape[0]
    share = hidden_in.shape[1]

    def head(array, which):
        return lax.dynamic_slice_in_dim(array, which * HEAD, HEAD, 1)

    trio = (patch_queries, patch_keys, patch_values)
    mine = jnp.concatenate([head(a, core) for a in trio], axis=1)
    other = jnp.concatenate([head(a, 1 - core) for a in trio], axis=1)
    hidden = jnp.concatenate([hidden_in.T, hidden_out.T], axis=0)
    other, *early = lax.optimization_barrier((other, local_weight, global_up, local_up))
    weights = jnp.concatenate([early[0], fold(early[1]), fold(early[2])], axis=0)
    weights = lax.all_gather(weights, ROW, axis=0, tiled=False)
    cotangents = jnp.concatenate([cotangent, lax.ppermute(cotangent, SIDE, SWAP)], axis=0)

    both = jnp.concatenate([mine, lax.ppermute(other, CORE, SWAP)], axis=0)
    chip_rows = 2 * rows
    packet = both[:, HEAD:]
    packet = jnp.concatenate([packet, hidden], axis=0)
    queries = to_everyone(both[:, :HEAD], QUAD)
    sides = lax.axis_size(QUAD)

    up = [(i, (i + 1) % ring) for i in range(ring)]
    down = [(i, (i - 1) % ring) for i in range(ring)]

    rising = falling = packet
    held, at = [packet], [z]
    for step in range(1, ring // 2 + 1):
        rising = lax.ppermute(rising, Z, up)
        held.append(rising)
        at.append(z - step)
        if step < ring // 2:
            falling = lax.ppermute(falling, Z, down)
            held.append(falling)
            at.append(z + step)
        if step == 1:
            rising, falling, queries = lax.optimization_barrier((rising, falling, queries))
    at = [k % ring for k in at]
    spots = jnp.stack([z * sides] + [k * sides + near * 2 + far for k in at]).astype(jnp.int32)
    spots = jnp.concatenate([core.astype(jnp.int32)[None], spots])
    state = attend(spots, queries, held[:-1], None, [], chip_rows)
    state, last = lax.optimization_barrier((state, held[-1]))
    spots = jnp.concatenate([spots[:2], spots[-1:], jnp.stack(at).astype(jnp.int32)])
    met = attend(spots, queries, [last], state, held[:-1] + [last], chip_rows)

    met = exchange(met, QUAD)
    riders = met[:, rows + 16 :].reshape(-1, units)
    riders = lax.all_gather(riders, LINE, axis=0, tiled=False)
    levels = met[:, rows : rows + 3].astype(F32).sum(axis=1)[:, :, None]
    met = jnp.concatenate([met[:, :rows, :HEAD], met[:, :rows, HEAD:]], axis=1).astype(F32)
    parts = jnp.exp(levels - jnp.max(levels, axis=0, keepdims=True))
    merged = (parts * met).sum(axis=0) / parts.sum(axis=0)
    merged = merged.astype(BF)
    merged, weights = lax.optimization_barrier((merged, weights))
    partner = lax.ppermute(merged[rows:], CORE, SWAP)
    attended = in_pair_order(merged[:rows], partner, core, 1)

    local_whole = weights[:, :width].reshape(-1, columns)
    up_whole = unfold(weights[:, width : width + 8])
    up_whole = jnp.transpose(up_whole, (1, 0, 2)).reshape(RANK, -1)
    local_ups = unfold(weights[:, width + 8 :]).reshape(line, 2, RANK, units)
    local_ups = lax.dynamic_index_in_dim(local_ups, side, 1, keepdims=False)

    task_scales = select_rows(global_scales, patch_tasks)
    part = contract(output_weight, attended, 0, 1).astype(BF).reshape(row_count, width, rows)
    low_part = contract(global_down, attended, 0, 1).astype(BF)
    low_part = jnp.broadcast_to(low_part[None], (row_count, RANK, rows))
    arrived = exchange(jnp.concatenate([part, low_part], axis=1), ROW)
    arrived = arrived.astype(F32).sum(axis=0)

    reduced = jnp.transpose(arrived[width:])
    scaled = (reduced * task_scales).astype(BF)
    mixed = arrived[:width] + jnp.transpose(residual.astype(F32)) + contract(global_up, scaled, 0, 1)
    mixed_b = mixed.astype(BF)
    own_patches = rows // row_count
    own_bytes = own_patches * PATCH
    own_tasks = lax.dynamic_slice_in_dim(patch_tasks, row_index * own_patches, own_patches)
    own_ids = lax.dynamic_slice_in_dim(byte_ids, row_index * own_bytes, own_bytes)
    projected = contract(mixed_b, local_weight, 0, 0).astype(BF)
    projected = exchange(projected.reshape(row_count, own_patches, columns), ROW)
    projected, riders = lax.optimization_barrier((projected, riders))
    projected = total(projected).astype(BF)

    rest = lax.ppermute(riders, CORE, SWAP)
    split = (line, sides, ring, 2, 1, share, units)
    riders = in_pair_order(riders.reshape(split), rest.reshape(split), core, 4)
    riders = jnp.transpose(riders, (3, 0, 2, 1, 4, 5, 6)).reshape(2, line, columns, units)
    rows_in, rows_out = riders[0], riders[1]
    lanes = 128
    spare_rows = jnp.zeros((line, lanes - RANK, units), BF)
    stacked = jnp.concatenate([rows_in, local_ups, spare_rows], axis=1)

    picks = (own_ids[:, None] == jnp.arange(VOCAB, dtype=jnp.int32)[None, :]).astype(BF)
    embedded = jnp.dot(picks, byte_table, preferred_element_type=F32)
    embedded = embedded.reshape(own_patches, PATCH, -1) + position_table.astype(F32)[None]
    inputs = (embedded + projected.astype(F32)[:, None, :]).reshape(own_bytes, columns)
    inverse = lax.rsqrt(jnp.mean(inputs * inputs, axis=1, keepdims=True) + 1e-06)
    normed = (inputs * inverse * norm_gain).astype(BF)
    lowered = jnp.dot(normed, local_down, preferred_element_type=F32)
    byte_tasks = jnp.repeat(own_tasks, PATCH)
    scales = select_rows(local_scales, byte_tasks)
    shrunk = (lowered * scales).astype(BF)
    joined = jnp.concatenate(
        [normed, shrunk, jnp.zeros((own_bytes, lanes - RANK), BF)], axis=1
    )
    joined = jnp.concatenate([joined, lax.ppermute(joined, SIDE, SWAP)], axis=0)
    through = contract(cotangents, rows_out, 1, 1)
    upper = contract(joined, stacked, 1, 1)
    grown = (through * gelu_slope(upper)).astype(BF)
    back = lax.dot_general(
        grown, stacked, (((1, 2), (0, 2)), ((), ())), preferred_element_type=F32
    )
    back = back[:own_bytes] + lax.ppermute(back[own_bytes:].astype(BF), SIDE, SWAP).astype(F32)
    ups = contract(joined[:, columns:], grown, 0, 0)[:RANK].astype(BF)
    back_norm = back[:, :columns]
    back_rank = back[:, columns : columns + RANK]
    grad_local_scales = task_totals(byte_tasks, back_rank * lowered)
    moved = (back_rank * scales).astype(BF)
    grad_local_down = contract(moved, normed, 0, 0)
    back_total = back_norm + contract(moved, local_down, 1, 1)
    gained = back_total * norm_gain
    average = jnp.mean(gained * inputs, axis=1, keepdims=True)
    back_inputs = cotangent.astype(F32) + inverse * (
        gained - inputs * inverse * inverse * average
    )
    patch_grad = back_inputs.reshape(own_patches, PATCH, -1).sum(axis=1)
    patch_grad = lax.optimization_barrier(patch_grad).astype(BF)

    spare = jnp.zeros((TASKS, columns - RANK), F32)
    local_rows = jnp.concatenate([grad_local_scales, spare], axis=1)
    local_rows = jnp.concatenate([grad_local_down, local_rows, jnp.zeros_like(local_rows)])
    row_pack = jnp.concatenate([patch_grad, local_rows.astype(BF)], axis=0)
    row_pack = jnp.broadcast_to(row_pack[None], (row_count, *row_pack.shape))
    ups = jnp.transpose(ups, (1, 0, 2))
    ups = jnp.stack([jnp.where(side == k, ups, jnp.zeros_like(ups)) for k in range(2)], axis=1)
    ups = jnp.pad(ups.reshape(row_count, RANK, units), [(0, 0), (0, 0), (0, columns - units)])
    row_pack = exchange(jnp.concatenate([row_pack, ups], axis=1), ROW)
    patch_grads = row_pack[:, :own_patches].reshape(rows, columns)
    local_sums = total(row_pack[:, own_patches:])
    back_mixed = contract(patch_grads, local_weight, 1, 1).astype(BF)
    back_whole = contract(patch_grads, local_whole, 1, 1).astype(BF)
    back_scaled = contract(back_whole, up_whole, 1, 1)
    grad_global_up = contract(scaled, back_mixed, 0, 0)
    grad_global_scales = task_totals(patch_tasks, back_scaled * reduced)
    back_reduced = (back_scaled * task_scales).astype(BF)
    grad_global_down = contract(back_reduced, attended, 0, 0)

    small = jnp.concatenate([grad_global_scales, jnp.zeros((TASKS, width - RANK), F32)], axis=1)
    small_local = local_sums[RANK : RANK + TASKS, :width]
    packed = jnp.concatenate(
        [
            grad_global_down,
            grad_global_up,
            local_sums[2 * RANK :, :units],
            local_sums[:RANK, :width],
            local_sums[:RANK, width:],
            small,
            small_local,
        ]
    ).astype(BF)
    shape = packed.shape
    pieces = packed.reshape(lax.axis_size(CHIPS), -1, shape[1])
    pieces = total(exchange(pieces, CHIPS)).astype(BF)
    pieces = total(to_everyone(pieces, (Z, NEAR))).astype(BF)
    packed = to_everyone(pieces, CHIPS).reshape(shape).astype(F32)
    return (
        jnp.transpose(packed[:16]),
        packed[16:32],
        packed[80:88, :RANK],
        jnp.transpose(jnp.concatenate([packed[48:64], packed[64:80]], axis=1)),
        packed[32:48],
        packed[88:96, :RANK],
    )


def solution(mesh):
    torus = Mesh(mesh.devices.reshape(8, 2, 2, 2, 4, 2), SEQ_ROW)
    placed = (
        P(SEQ, ROW),
        P(SEQ, ROW),
        P(SEQ, ROW),
        P(SEQ),
        P(SEQ, ROW),
        P(ROW, None),
        P(ROW, None),
        P(None, ROW),
        P(),
        P(ROW, None),
        P(SEQ),
        P(),
        P(),
        P(),
        P(ROW, SEQ),
        P(ROW, SEQ),
        P(),
        P(None, ROW),
        P(),
        P(SEQ_ROW, None),
    )
    return jax.shard_map(
        body,
        mesh=torus,
        in_specs=placed,
        out_specs=(P(ROW, None), P(None, ROW), P(), P(), P(None, ROW), P()),
        check_vma=False,
    )
```
